32 devices in a mesh: pipe: 2 (over core), tensor: 4 (over y, x), dp: 4 (over z).
Axes of the slice: x: 2, y: 2, z: 4, core: 2. Of those that a mesh axis runs over, the one named last changes fastest.
Arguments:
- tokens: bfloat16 [8192, 2048], P('dp'), may hold values from -6 to 6
- cotangent: bfloat16 [8192, 2048], P('dp'), may hold values from -6 to 6
- lengths: int32 [8], P('dp'), may hold values from 513 to 1024, as said below
- inward: float32 [2, 2048, 3, 2048], P('pipe', 'dp', None, 'tensor'), may hold values from -0.125 to 0.125
- outward: float32 [2, 2048, 2048], P('pipe', 'tensor', 'dp'), may hold values from -1 to 1
- expand: float32 [2, 2048, 8192], P('pipe', 'dp', 'tensor'), may hold values from -0.125 to 0.125
- contract: float32 [2, 8192, 2048], P('pipe', 'tensor', 'dp'), may hold values from -0.0625 to 0.0625
- vectors: float32 [2, 5, 2048], P('pipe', None, 'dp'), as said below
- offsets: float32 [2, 8192], P('pipe', ('tensor', 'dp')), may hold values from -3 to 3
- inward_first: float32 [2, 2048, 3, 2048], P('pipe', 'dp', None, 'tensor'), may hold values from -48 to 48
- inward_second: float32 [2, 2048, 3, 2048], P('pipe', 'dp', None, 'tensor'), may hold values from 327.68 to 1310.72
- outward_first: float32 [2, 2048, 2048], P('pipe', 'tensor', 'dp'), may hold values from -6 to 6
- outward_second: float32 [2, 2048, 2048], P('pipe', 'tensor', 'dp'), may hold values from 7.3728 to 29.4912
- expand_first: float32 [2, 2048, 8192], P('pipe', 'dp', 'tensor'), may hold values from -16 to 16
- expand_second: float32 [2, 2048, 8192], P('pipe', 'dp', 'tensor'), may hold values from 29.4912 to 117.9648
- contract_first: float32 [2, 8192, 2048], P('pipe', 'tensor', 'dp'), may hold values from -32 to 32
- contract_second: float32 [2, 8192, 2048], P('pipe', 'tensor', 'dp'), may hold values from 117.9648 to 471.8592
- vectors_first: float32 [2, 5, 2048], P('pipe', None, 'dp'), may hold values from -96 to 96
- vectors_second: float32 [2, 5, 2048], P('pipe', None, 'dp'), may hold values from 1310.72 to 5242.88
- offsets_first: float32 [2, 8192], P('pipe', ('tensor', 'dp')), may hold values from -16 to 16
- offsets_second: float32 [2, 8192], P('pipe', ('tensor', 'dp')), may hold values from 29.4912 to 117.9648
Outputs:
- activations: bfloat16 [2, 8, 1024, 2048], P('pipe', 'dp', 'tensor')
- input_grads: float32 [2, 8, 1024, 2048], P('pipe', 'dp', 'tensor')
- inward_new: float32 [2, 2048, 3, 2048], P('pipe', 'dp', None, 'tensor')
- inward_moment: float32 [2, 2048, 3, 2048], P('pipe', 'dp', None, 'tensor')
- inward_square: float32 [2, 2048, 3, 2048], P('pipe', 'dp', None, 'tensor')
- outward_new: float32 [2, 2048, 2048], P('pipe', 'tensor', 'dp')
- outward_moment: float32 [2, 2048, 2048], P('pipe', 'tensor', 'dp')
- outward_square: float32 [2, 2048, 2048], P('pipe', 'tensor', 'dp')
- expand_new: float32 [2, 2048, 8192], P('pipe', 'dp', 'tensor')
- expand_moment: float32 [2, 2048, 8192], P('pipe', 'dp', 'tensor')
- expand_square: float32 [2, 2048, 8192], P('pipe', 'dp', 'tensor')
- contract_new: float32 [2, 8192, 2048], P('pipe', 'tensor', 'dp')
- contract_moment: float32 [2, 8192, 2048], P('pipe', 'tensor', 'dp')
- contract_square: float32 [2, 8192, 2048], P('pipe', 'tensor', 'dp')
- vectors_new: float32 [2, 5, 2048], P('pipe', None, 'dp')
- vectors_moment: float32 [2, 5, 2048], P('pipe', None, 'dp')
- vectors_square: float32 [2, 5, 2048], P('pipe', None, 'dp')
- offsets_new: float32 [2, 8192], P('pipe', ('tensor', 'dp'))
- offsets_moment: float32 [2, 8192], P('pipe', ('tensor', 'dp'))
- offsets_square: float32 [2, 8192], P('pipe', ('tensor', 'dp'))
The draws below stay inside these ranges and needn't reach their ends.
Inputs may be any that keep to these rules, and one draw needn't show every extreme that they name: `lengths`: valid slots of each sequence; some sequence is full (1024 valid slots). `vectors`: rows 0 and 2 of each section (the norms' gains) are positive.
All inputs are finite; a program needn't handle non-finite values.
Results may differ from the reference program's by a relative error of at most 0.025.
Values may be sent and summed in bfloat16 or wider, within the bound.
No kernel may reach another device: no remote copies, remote signals or barrier semaphores. Data moves between devices by JAX's collectives and lax.ppermute only.
A program may use at most 832 MiB of HBM per device.

```python
import math
import jax
import jax.numpy as jnp
from jax import lax

D = 2048
HEADS = 8
HEAD_DIM = 256
FF = 8192
ROT = 64
SEQ = 1024
STEP = 10
SECTIONS = 2
SEQS = 8
TOKENS = 8192


def draw_lengths(key, part):
    key = jax.random.fold_in(key, 11)
    first, second = jax.random.split(key)
    values = jax.random.randint(first, (SEQS,), SEQ // 2 + 1, SEQ + 1)
    chosen = jax.random.randint(second, (), 0, SEQS)
    return jnp.where(jnp.arange(SEQS) == chosen, SEQ, values).astype(jnp.int32)


def draw_vectors(key, part):
    key = jax.random.fold_in(key, 5)
    gain_key, shift_key = jax.random.split(key)
    gains = jax.random.uniform(gain_key, (SECTIONS, 5, D), minval=0.5, maxval=1.5)
    shifts = 0.5 * jax.random.normal(shift_key, (SECTIONS, 5, D))
    row = jnp.arange(5)[None, :, None]
    return jnp.where((row == 0) | (row == 2), gains, shifts).astype(jnp.float32)


def level_of(key, extent, cuts, least, largest):
    level, own = 1.0, jax.random.fold_in(key, 6)
    for position, shards_of in cuts:
        draws = jnp.exp(jax.random.uniform(jax.random.fold_in(own, position), (shards_of,), jnp.float32, least / len(cuts), largest / len(cuts)))
        level = level * jnp.repeat(draws, extent[position] // shards_of).reshape([-1 if axis == position else 1 for axis in range(len(extent))])
    return level


def noise(own_key, shape, scale, limit, pieces=(), held_as=jnp.bfloat16):
    drawn = jax.random.normal(own_key, shape, jnp.float32) * scale
    if len(pieces) > 0:
        drawn = level_of(own_key, shape, pieces, -0.22, 0.18) * drawn
    return jnp.clip(drawn, min=-limit, max=limit).astype(held_as)


def setup_inputs(seed: int = 0) -> dict:
    seeds = jax.random.split(jax.random.key(seed), 22)
    return {
        "tokens": noise(seeds[0], (TOKENS, D), 1.0, 6.0, ((0, 4),)),
        "cotangent": noise(seeds[1], (TOKENS, D), 1.0, 6.0, ((0, 4),)),
        "lengths": draw_lengths(jax.random.fold_in(seeds[21], 71), 0),
        "inward": noise(seeds[3], (SECTIONS, D, 3, D), D ** -0.5, 0.125, ((0, 2), (1, 4), (3, 4)), jnp.float32),
        "outward": noise(seeds[4], (SECTIONS, D, D), (D * 16 // SEQ) ** -0.5, 1.0, ((0, 2), (1, 4), (2, 4)), jnp.float32),
        "expand": noise(seeds[5], (SECTIONS, D, FF), D ** -0.5, 0.125, ((0, 2), (1, 4), (2, 4)), jnp.float32),
        "contract": noise(seeds[6], (SECTIONS, FF, D), FF ** -0.5, 0.0625, ((0, 2), (1, 4), (2, 4)), jnp.float32),
        "vectors": draw_vectors(jax.random.fold_in(seeds[21], 71), 0),
        "offsets": noise(seeds[8], (SECTIONS, FF), 0.5, 3.0, ((0, 2), (1, 16)), jnp.float32),
        "inward_first": noise(seeds[9], (SECTIONS, D, 3, D), (0.095 * TOKENS ** 0.5), 48.0, ((0, 2), (1, 4), (3, 4)), jnp.float32),
        "inward_second": jnp.clip(jnp.exp(math.log(1310.72) - 1.3862944 * jax.random.uniform(seeds[10], (SECTIONS, D, 3, D), jnp.float32) ** level_of(seeds[10], (SECTIONS, D, 3, D), ((0, 2), (1, 4), (3, 4)), -0.2, 0.2)), 327.68, 1310.72),
        "outward_first": noise(seeds[11], (SECTIONS, D, D), (0.014 * TOKENS ** 0.5), 6.0, ((0, 2), (1, 4), (2, 4)), jnp.float32),
        "outward_second": jnp.clip(jnp.exp(math.log(29.4912) - 1.3862944 * jax.random.uniform(seeds[12], (SECTIONS, D, D), jnp.float32) ** level_of(seeds[12], (SECTIONS, D, D), ((0, 2), (1, 4), (2, 4)), -0.2, 0.2)), 7.3728, 29.4912),
        "expand_first": noise(seeds[13], (SECTIONS, D, FF), (0.029 * TOKENS ** 0.5), 16.0, ((0, 2), (1, 4), (2, 4)), jnp.float32),
        "expand_second": jnp.clip(jnp.exp(math.log(117.9648) - 1.3862944 * jax.random.uniform(seeds[14], (SECTIONS, D, FF), jnp.float32) ** level_of(seeds[14], (SECTIONS, D, FF), ((0, 2), (1, 4), (2, 4)), -0.2, 0.2)), 29.4912, 117.9648),
        "contract_first": noise(seeds[15], (SECTIONS, FF, D), (0.057 * TOKENS ** 0.5), 32.0, ((0, 2), (1, 4), (2, 4)), jnp.float32),
        "contract_second": jnp.clip(jnp.exp(math.log(471.8592) - 1.3862944 * jax.random.uniform(seeds[16], (SECTIONS, FF, D), jnp.float32) ** level_of(seeds[16], (SECTIONS, FF, D), ((0, 2), (1, 4), (2, 4)), -0.2, 0.2)), 117.9648, 471.8592),
        "vectors_first": noise(seeds[17], (SECTIONS, 5, D), (0.19 * TOKENS ** 0.5), 96.0, ((0, 2), (2, 4)), jnp.float32),
        "vectors_second": jnp.clip(jnp.exp(math.log(5242.88) - 1.3862944 * jax.random.uniform(seeds[18], (SECTIONS, 5, D), jnp.float32) ** level_of(seeds[18], (SECTIONS, 5, D), ((0, 2), (2, 4)), -0.2, 0.2)), 1310.72, 5242.88),
        "offsets_first": noise(seeds[19], (SECTIONS, FF), (0.029 * TOKENS ** 0.5), 16.0, ((0, 2), (1, 16)), jnp.float32),
        "offsets_second": jnp.clip(jnp.exp(math.log(117.9648) - 1.3862944 * jax.random.uniform(seeds[20], (SECTIONS, FF), jnp.float32) ** level_of(seeds[20], (SECTIONS, FF), ((0, 2), (1, 16)), -0.2, 0.2)), 29.4912, 117.9648),
    }


@jax.custom_vjp
def low(v):
    return lax.optimization_barrier(v.astype(jnp.bfloat16)).astype(jnp.float32)

@jax.custom_vjp
def low_back(v):
    return v

def low_keep(v):
    return (low(v), None)

def low_pass(kept, grad):
    return (grad,)

def back_keep(v):
    return (v, None)

def back_low(kept, grad):
    return (low(grad),)
low.defvjp(low_keep, low_pass)
low_back.defvjp(back_keep, back_low)
HIGH = lax.Precision.HIGHEST
RATES = (0.03, 0.2, 0.03, 0.015, 0.3, 0.3)
DECAYS = (0.01, 0.01, 0.01, 0.01, 0.0, 0.0)

def angle_tables(slots):
    half = ROT // 2
    positions = jnp.arange(slots).astype(jnp.float32)
    frequency = 10000.0 ** (-(2.0 * jnp.arange(half).astype(jnp.float32)) / ROT)
    angles = positions[:, None] * frequency[None, :]
    return (jnp.cos(angles)[:, None, :], jnp.sin(angles)[:, None, :])

def rotate(block, cosine, sine):
    half = cosine.shape[-1]
    first = block[..., :half]
    second = block[..., half:2 * half]
    return jnp.concatenate([first * cosine - second * sine, second * cosine + first * sine, block[..., 2 * half:]], axis=-1)

def norm_parts(rows, gain, shift):
    center = rows - lax.optimization_barrier(jnp.mean(rows, axis=1, keepdims=True))
    scale = lax.rsqrt(lax.optimization_barrier(jnp.mean(center * center, axis=1, keepdims=True)) + 1e-05)
    normed = center * scale
    return (normed * gain + shift, normed, scale)

def layer(params, rows, length):
    inward, outward, expand, contract, vectors, offsets = params
    slots = rows.shape[0]
    first_in = low(norm_parts(rows, vectors[0], vectors[1])[0])
    second_in = low(norm_parts(rows, vectors[2], vectors[3])[0])
    mixed = low_back(jnp.dot(first_in, inward.reshape(D, 3 * D), precision=HIGH)).reshape(slots, 3, HEADS, HEAD_DIM)
    cosine, sine = angle_tables(slots)
    query = low(rotate(mixed[:, 0], cosine, sine))
    keys = low(rotate(mixed[:, 1], cosine, sine))
    values = low(mixed[:, 2])
    scores = low_back(jnp.einsum('qhd,khd->hqk', query, keys, precision=HIGH) * HEAD_DIM ** (-0.5))
    places = jnp.arange(slots)
    allowed = (places[None, :] <= places[:, None]) & (places[None, :] < length)
    probs = jax.nn.softmax(jnp.where(allowed[None], scores, -jnp.inf), axis=-1)
    heads_out = low(low_back(jnp.einsum('hqk,khd->qhd', low(probs), values, precision=HIGH).reshape(slots, D)))
    hidden = low_back(jnp.dot(second_in, expand, precision=HIGH) + offsets)
    activated = low(jax.nn.gelu(hidden, approximate=False))
    branch = jnp.dot(heads_out, outward, precision=HIGH) + jnp.dot(activated, contract, precision=HIGH)
    return rows + branch + vectors[4]

def run_section(params, rows_all, lengths):
    step_fn = jax.checkpoint(layer)
    return lax.map(lambda pair: step_fn(params, pair[0], pair[1]), (rows_all, lengths))

def forward(masters, tokens_f, offset, lengths):
    work = tuple((low(m) for m in masters))
    first_section = tuple((w[0] for w in work))
    second_section = tuple((w[1] for w in work))
    middle = run_section(first_section, tokens_f, lengths)
    sent = low_back(low(middle)) + offset
    final = run_section(second_section, sent, lengths)
    return (middle, final)

def adam_update(master, grad, first, second, rate, decay):
    new_first = 0.9 * first + 0.1 * grad
    new_second = 0.95 * second + 0.05 * grad * grad
    corrected = new_first / (1.0 - 0.9 ** STEP)
    spread = jnp.sqrt(new_second / (1.0 - 0.95 ** STEP))
    return (master - rate * (corrected / (spread + 1e-08) + decay * master), new_first, new_second)

def reference(tokens, cotangent, lengths, inward, outward, expand, contract, vectors, offsets, inward_first, inward_second, outward_first, outward_second, expand_first, expand_second, contract_first, contract_second, vectors_first, vectors_second, offsets_first, offsets_second):
    masters = (inward, outward, expand, contract, vectors, offsets)
    firsts = (inward_first, outward_first, expand_first, contract_first, vectors_first, offsets_first)
    seconds = (inward_second, outward_second, expand_second, contract_second, vectors_second, offsets_second)
    sequences = lengths.shape[0]
    tokens_f = tokens.astype(jnp.float32).reshape(sequences, -1, D)
    slots = tokens_f.shape[1]
    valid = (jnp.arange(slots)[None, :] < lengths[:, None]).astype(jnp.float32)
    grad_final = cotangent.astype(jnp.float32).reshape(sequences, slots, D) * valid[:, :, None]
    offset_zero = jnp.zeros_like(tokens_f)
    outputs, pullback = jax.vjp(lambda m, t, o: forward(m, t, o, lengths), masters, tokens_f, offset_zero)
    middle, final = outputs
    master_grads, token_grad, middle_grad = pullback((jnp.zeros_like(middle), grad_final))
    activations = jnp.stack([middle, final]).astype(jnp.bfloat16)
    input_grads = jnp.stack([token_grad, middle_grad])
    updated = [adam_update(masters[i], master_grads[i], firsts[i], seconds[i], RATES[i], DECAYS[i]) for i in range(6)]
    return (activations, input_grads, updated[0][0], updated[0][1], updated[0][2], updated[1][0], updated[1][1], updated[1][2], updated[2][0], updated[2][1], updated[2][2], updated[3][0], updated[3][1], updated[3][2], updated[4][0], updated[4][1], updated[4][2], updated[5][0], updated[5][1], updated[5][2])
```

```python
import functools

import jax
import jax.numpy as jnp
from jax import lax
from jax.experimental import pallas as pl
from jax.experimental.pallas import tpu as pltpu
from jax.sharding import PartitionSpec as P

HEAD_DIM = 256
ROT = 64
STEP = 10


RATES = (0.03, 0.2, 0.03, 0.015, 0.3, 0.3)
DECAYS = (0.01, 0.01, 0.01, 0.01, 0.0, 0.0)


def angle_tables(slots):
    half = ROT // 2
    positions = jnp.arange(slots).astype(jnp.float32)
    frequency = 10000.0 ** (-(2.0 * jnp.arange(half).astype(jnp.float32)) / ROT)
    angles = positions[:, None] * frequency[None, :]
    return (jnp.cos(angles)[:, None, :], jnp.sin(angles)[:, None, :])


def rotate(block, cosine, sine):
    half = cosine.shape[-1]
    first = block[..., :half]
    second = block[..., half : 2 * half]
    return jnp.concatenate(
        [first * cosine - second * sine, second * cosine + first * sine, block[..., 2 * half :]],
        axis=-1,
    )


def rotate_back(grad, cosine, sine):
    half = cosine.shape[-1]
    first = grad[..., :half]
    second = grad[..., half : 2 * half]
    return jnp.concatenate(
        [first * cosine + second * sine, second * cosine - first * sine, grad[..., 2 * half :]],
        axis=-1,
    )


def norm_parts(rows, gain, shift):
    center = rows - jnp.mean(rows, axis=1, keepdims=True)
    scale = lax.rsqrt(jnp.mean(center * center, axis=1, keepdims=True) + 1e-05)
    normed = center * scale
    return (normed * gain + shift, normed, scale)


def norm_back(back, rows, gain):
    unused, normed, scale = norm_parts(rows, gain, 0.0)
    hat = back * gain
    row_grad = scale * (
        hat
        - jnp.mean(hat, axis=1, keepdims=True)
        - normed * jnp.mean(hat * normed, axis=1, keepdims=True)
    )
    return (row_grad, jnp.sum(back * normed, axis=0), jnp.sum(back, axis=0))


def gelu_slope(hidden):
    return (
        0.5 * (1.0 + lax.erf(hidden * 0.7071067811865476))
        + hidden * jnp.exp(-0.5 * hidden * hidden) * 0.3989422804014327
    )


def allowed_mask(slots, length):
    places = jnp.arange(slots)
    return (places[None, :] <= places[:, None]) & (places[None, :] < length)


def after(array, *earlier):
    return lax.optimization_barrier((array, *earlier))[0]


def added(array, axis):
    peers = lax.axis_size(axis)
    bits = peers.bit_length() - 1
    if peers != 1 << bits:
        return lax.psum(array, axis)
    for bit in range(bits):
        array = array + lax.ppermute(array, axis, [(i, i ^ (1 << bit)) for i in range(peers)])
    return array


def swap(array):
    return lax.ppermute(array, "pipe", [(0, 1), (1, 0)])


def halves(array, core):
    size = array.shape[-1] // 2
    axis = array.ndim - 1
    mine = lax.dynamic_slice_in_dim(array, core * size, size, axis)
    theirs = lax.dynamic_slice_in_dim(array, (1 - core) * size, size, axis)
    return (mine, theirs)


def ordered(mine, theirs, core):
    return jnp.where(
        core == 0,
        jnp.concatenate([mine, theirs], axis=-1),
        jnp.concatenate([theirs, mine], axis=-1),
    )


def flipped(array, peers, bit):
    return lax.ppermute(array, "tensor", [(i, i ^ (1 << bit)) for i in range(peers)])


def halving(peers, rows):
    bits = peers.bit_length() - 1
    return bits if peers == 1 << bits and bits > 0 and rows % (16 * peers) == 0 else 0


def step_bits(bits, stream):
    return [step if stream == 0 else bits - 1 - step for step in range(bits)]


def relative_order(bits, stream):
    order = [0]
    for bit in reversed(step_bits(bits, stream)):
        order = order + [other ^ (1 << bit) for other in order]
    return order


def scatter_places(me, peers, bits):
    half = peers // 2
    places = []
    for stream in (0, 1):
        bit = step_bits(bits, stream)[0]
        own = (me >> bit) & 1
        for value in (1 - own, own):
            for place in range(half):
                low = place & ((1 << bit) - 1)
                high = (place >> bit) << (bit + 1)
                places.append(high | (value << bit) | low)
    return places


def sum_scatter(pieces, peers, bits):
    me = lax.axis_index("tensor")
    half = peers // 2
    width = pieces[0].shape[1]
    sends = [pieces[k * (half + 1) : k * (half + 1) + half] for k in (0, 1)]
    keeps = [pieces[k * (half + 1) + half] for k in (0, 1)]
    left = [[b for b in reversed(range(bits)) if b != step_bits(bits, k)[0]] for k in (0, 1)]
    for step in range(bits):
        arrived = lax.optimization_barrier(
            [[flipped(item, peers, step_bits(bits, k)[step]) for item in sends[k]] for k in (0, 1)]
        )
        for k in (0, 1):
            got = arrived[k]
            total = jnp.stack(
                [
                    keep.astype(jnp.float32) + item.astype(jnp.float32)
                    for keep, item in zip(jnp.split(keeps[k], len(got), axis=0), got)
                ]
            )
            if step == bits - 1:
                keeps[k] = total[0]
                continue
            total = total.astype(jnp.bfloat16).reshape((2,) * len(left[k]) + (-1, width))
            bit = step_bits(bits, k)[step + 1]
            axis = left[k].index(bit)
            own = (me >> bit) & 1
            keep = lax.dynamic_index_in_dim(total, own, axis, keepdims=False)
            send = lax.dynamic_index_in_dim(total, 1 - own, axis, keepdims=False)
            keeps[k] = keep.reshape(-1, width)
            sends[k] = jnp.split(send.reshape(-1, width), len(got) // 2, axis=0)
            left[k].pop(axis)
    return keeps


def rows_pieces(blocks, peers, bits):
    current = [[item] for item in blocks]
    for step in reversed(range(bits)):
        arrived = lax.optimization_barrier(
            [[flipped(item, peers, step_bits(bits, k)[step]) for item in current[k]] for k in (0, 1)]
        )
        current = [current[k] + arrived[k] for k in (0, 1)]
    return current[0] + current[1]


def attend(mixed, length, tables):
    slots = mixed.shape[0]
    cosine, sine = tables
    query = rotate(mixed[:, 0], cosine, sine).astype(jnp.bfloat16)
    keys = rotate(mixed[:, 1], cosine, sine).astype(jnp.bfloat16)
    values = mixed[:, 2].astype(jnp.bfloat16)
    scores = jnp.einsum(
        "qhd,khd->hqk", query, keys, preferred_element_type=jnp.float32
    ) * HEAD_DIM ** (-0.5)
    scores = jnp.where(allowed_mask(slots, length)[None], scores, -jnp.inf)
    peak = jnp.max(scores, axis=-1, keepdims=True)
    expo = jnp.exp(scores - peak)
    total = jnp.sum(expo, axis=-1, keepdims=True)
    probs_low = (expo / total).astype(jnp.bfloat16)
    logsum = peak + jnp.log(total)
    heads_out = jnp.einsum("hqk,khd->qhd", probs_low, values, preferred_element_type=jnp.float32)
    return (heads_out.reshape(slots, -1).astype(jnp.bfloat16), (query, keys, values, logsum))


def attend_back(out_grad, saved, length, tables):
    query, keys, values, logsum = saved
    slots, heads = query.shape[:2]
    cosine, sine = tables
    out_grad = out_grad.reshape(slots, heads, HEAD_DIM)
    scores = jnp.einsum(
        "qhd,khd->hqk", query, keys, preferred_element_type=jnp.float32
    ) * HEAD_DIM ** (-0.5)
    probs = jnp.where(allowed_mask(slots, length)[None], jnp.exp(scores - logsum), 0.0)
    probs_low = probs.astype(jnp.bfloat16)
    prob_grad = jnp.einsum("qhd,khd->hqk", out_grad, values, preferred_element_type=jnp.float32)
    value_grad = jnp.einsum("hqk,qhd->khd", probs_low, out_grad, preferred_element_type=jnp.float32)
    score_grad = (probs * (prob_grad - jnp.sum(probs * prob_grad, axis=-1, keepdims=True))).astype(
        jnp.bfloat16
    )
    query_grad = jnp.einsum(
        "hqk,khd->qhd", score_grad, keys, preferred_element_type=jnp.float32
    ) * HEAD_DIM ** (-0.5)
    key_grad = jnp.einsum(
        "hqk,qhd->khd", score_grad, query, preferred_element_type=jnp.float32
    ) * HEAD_DIM ** (-0.5)
    query_grad = rotate_back(query_grad, cosine, sine)
    key_grad = rotate_back(key_grad, cosine, sine)
    return jnp.stack([query_grad, key_grad, value_grad], axis=1).astype(jnp.bfloat16)


def dot(left, right):
    return jnp.dot(left, right, preferred_element_type=jnp.float32)


def dot_nt(left, right):
    return lax.dot_general(
        left, right, (((1,), (1,)), ((), ())), preferred_element_type=jnp.float32
    )


def dot_tn(left, right):
    return lax.dot_general(
        left, right, (((0,), (0,)), ((), ())), preferred_element_type=jnp.float32
    )


CHEAP = pl.CostEstimate(flops=1, transcendentals=0, bytes_accessed=1)
SCALE = HEAD_DIM ** (-0.5)


def call(body, grid, in_specs, out_specs, out_shape, info, args, scratch=(), cost=CHEAP):
    return pl.pallas_call(
        body,
        grid_spec=pltpu.PrefetchScalarGridSpec(
            num_scalar_prefetch=1,
            grid=grid,
            in_specs=in_specs,
            out_specs=out_specs,
            scratch_shapes=list(scratch),
        ),
        out_shape=out_shape,
        cost_estimate=cost,
        compiler_params=pltpu.CompilerParams(vmem_limit_bytes=56 << 20),
    )(info, *args)


def low_shape(*shape):
    return jax.ShapeDtypeStruct(shape, jnp.bfloat16)


def full_shape(*shape):
    return jax.ShapeDtypeStruct(shape, jnp.float32)


def fixed(shape):
    return pl.BlockSpec(
        shape, lambda *index: (0,) * len(shape), pipeline_mode=pl.Buffered(buffer_count=1)
    )


def held(width, columns, at):
    return pl.BlockSpec(
        (width, columns), lambda i, info: (0, at), pipeline_mode=pl.Buffered(buffer_count=1)
    )


def row_stats(rows):
    mean = jnp.mean(rows, axis=1, keepdims=True)
    center = rows - mean
    scale = lax.rsqrt(jnp.mean(center * center, axis=1, keepdims=True) + 1e-05)
    return (mean, scale)


def two_norms(rows, vec_ref, outs):
    rows = rows.astype(jnp.float32)
    mean, scale = row_stats(rows)
    normed = (rows - mean) * scale
    first = normed * vec_ref[0:1] + vec_ref[1:2]
    second = normed * vec_ref[2:3] + vec_ref[3:4]
    outs[0][...] = first.astype(jnp.bfloat16)
    outs[1][...] = second.astype(jnp.bfloat16)
    outs[2][...] = mean
    outs[3][...] = scale
    if len(outs) > 4:
        outs[4][...] = first.T.astype(jnp.bfloat16)
        outs[5][...] = second.T.astype(jnp.bfloat16)


def norms_body(info, z_ref, vec_ref, *outs):
    two_norms(z_ref[...], vec_ref, outs)


def norm_specs(tall, slots, width, row, turn):
    specs = [pl.BlockSpec((tall, width), lambda i, info: (row(i, info), 0))] * 2
    specs += [pl.BlockSpec((tall, 1), lambda i, info: (row(i, info), 0))] * 2
    shapes = [low_shape(slots, width)] * 2 + [full_shape(slots, 1)] * 2
    if turn:
        specs += [pl.BlockSpec((width, tall), lambda i, info: (0, row(i, info)))] * 2
        shapes += [low_shape(width, slots)] * 2
    return (specs, shapes)


def with_turned(out, turn):
    out = list(out)
    return out if turn else out + [out[0].T, out[1].T]


def norms_call(rows, vectors, info):
    slots, width = rows.shape
    tall = min(slots, 256)
    turn = tall % 128 == 0
    specs, shapes = norm_specs(tall, slots, width, lambda i, info: i, turn)
    out = call(
        norms_body,
        (slots // tall,),
        [pl.BlockSpec((tall, width), lambda i, info: (i, 0)), fixed(vectors.shape)],
        specs,
        shapes,
        info,
        (rows, vectors),
    )
    return with_turned(out, turn)


def target_body(info, x_ref, out_ref, *turned_ref):
    tall = x_ref.shape[0]
    place = pl.program_id(0) * tall + lax.broadcasted_iota(jnp.int32, x_ref.shape, 0)
    value = jnp.where(place < info[0], x_ref[...].astype(jnp.float32), 0.0)
    out_ref[...] = value.astype(jnp.bfloat16)
    if turned_ref:
        turned_ref[0][...] = value.T.astype(jnp.bfloat16)


def target_call(cotangent, slots, info):
    width = cotangent.shape[1]
    tall = min(slots, 256)
    steps = slots // tall
    turn = tall % 128 == 0
    out = call(
        target_body,
        (steps,),
        [pl.BlockSpec((tall, width), lambda i, info: (info[1] * steps + i, 0))],
        [pl.BlockSpec((tall, width), lambda i, info: (i, 0))]
        + [pl.BlockSpec((width, tall), lambda i, info: (0, i))] * turn,
        [low_shape(slots, width)] + [low_shape(width, slots)] * turn,
        info,
        (cotangent,),
    )
    return (out[0], out[1]) if turn else (out[0], out[0].T)


def assemble_body(count, normed, info, *refs):
    step = pl.program_id(0)
    rest = refs[count:]
    for which in range(count):

        @pl.when(step == which)
        def _():
            block = refs[which][...]
            if normed:
                rest[1][...] = block
                two_norms(block, rest[0], rest[2:])
            else:
                rest[0][...] = block
                if len(rest) > 1:
                    rest[1][...] = block.astype(jnp.float32).T.astype(jnp.bfloat16)


def assemble(pieces, peers, bits, vectors=None):
    count = len(pieces)
    tall, width = pieces[0].shape
    slots = count * tall
    turn = tall % 128 == 0
    me = lax.axis_index("tensor")
    order = [2 * (me ^ r) + k for k in (0, 1) for r in relative_order(bits, k)]
    info = jnp.stack([jnp.asarray(item, jnp.int32) for item in order])

    def row(s, info):
        return info[s]

    in_specs, args = [fixed(item.shape) for item in pieces], list(pieces)
    specs = [pl.BlockSpec((tall, width), lambda s, info: (info[s], 0))]
    shapes = [low_shape(slots, width)]
    if vectors is not None:
        in_specs.append(fixed(vectors.shape))
        args.append(vectors)
        more, more_shapes = norm_specs(tall, slots, width, row, turn)
        specs, shapes = specs + more, shapes + more_shapes
    elif turn:
        specs.append(pl.BlockSpec((width, tall), lambda s, info: (0, info[s])))
        shapes.append(low_shape(width, slots))
    out = call(
        functools.partial(assemble_body, count, vectors is not None),
        (count,),
        in_specs,
        specs,
        shapes,
        info,
        args,
    )
    if vectors is not None:
        return (out[0], with_turned(out[1:], turn))
    return (out[0], out[1] if turn else out[0].T)


def turned(block, tables, sign):
    cosine, low, high = tables
    front = block[:, :128]
    front = front * cosine + sign * (
        pltpu.roll(front, 128 - ROT // 2, 1) * low + pltpu.roll(front, ROT // 2, 1) * high
    )
    return jnp.concatenate([front, block[:, 128:]], axis=1)


def turn_tables(slots):
    cosine, sine = (item[:, 0] for item in angle_tables(slots))
    rest = 128 - ROT
    zero = jnp.zeros_like(sine)
    pad = jnp.zeros((slots, rest), jnp.float32)
    return (
        jnp.concatenate([cosine, cosine, pad + 1.0], axis=1),
        jnp.concatenate([-sine, zero, pad], axis=1),
        jnp.concatenate([zero, sine, pad], axis=1),
    )


def allowed_block(start, rows, span, length):
    query = start + lax.broadcasted_iota(jnp.int32, (rows, span), 0)
    key = lax.broadcasted_iota(jnp.int32, (rows, span), 1)
    return (key <= query) & (key < length)


def heads_body(
    steps, info, x_ref, w_ref, cos_ref, low_ref, high_ref, out_ref, qkv_ref, lse_ref, k_ref, v_ref
):
    step = pl.program_id(0)
    rows = x_ref.shape[0]
    tables = (cos_ref[...], low_ref[...], high_ref[...])
    mixed = dot(x_ref[...], w_ref[...])
    query = turned(mixed[:, :HEAD_DIM], tables, 1.0).astype(jnp.bfloat16)
    keys = turned(mixed[:, HEAD_DIM : 2 * HEAD_DIM], tables, 1.0).astype(jnp.bfloat16)
    values = mixed[:, 2 * HEAD_DIM :].astype(jnp.bfloat16)
    qkv_ref[:, :HEAD_DIM] = query
    qkv_ref[:, HEAD_DIM : 2 * HEAD_DIM] = keys
    qkv_ref[:, 2 * HEAD_DIM :] = values
    place = pl.multiple_of(step * rows, rows)
    k_ref[pl.ds(place, rows), :] = keys
    v_ref[pl.ds(place, rows), :] = values
    for now in range(steps):

        @pl.when(step == now)
        def _():
            span = (now + 1) * rows
            scores = dot_nt(query, k_ref[:span]) * SCALE
            scores = jnp.where(allowed_block(now * rows, rows, span, info[0]), scores, -jnp.inf)
            peak = jnp.max(scores, axis=1, keepdims=True)
            expo = jnp.exp(scores - peak)
            total = jnp.sum(expo, axis=1, keepdims=True)
            probs = (expo / total).astype(jnp.bfloat16)
            out_ref[...] = dot(probs, v_ref[:span]).astype(jnp.bfloat16)
            lse_ref[...] = peak + jnp.log(total)


def heads_call(first_in, inward, tables, info):
    slots, width = first_in.shape
    rows = min(slots, 256)
    steps = slots // rows
    columns = 3 * HEAD_DIM

    def tall(size):
        return pl.BlockSpec((rows, size), lambda i, info: (i, 0))

    out, qkv, lse = call(
        functools.partial(heads_body, steps),
        (steps,),
        [
            tall(width),
            pl.BlockSpec(
                (width, columns), lambda i, info: (0, 0), pipeline_mode=pl.Buffered(buffer_count=1)
            ),
        ]
        + [tall(128)] * 3,
        [tall(HEAD_DIM), tall(columns), tall(1)],
        [low_shape(slots, HEAD_DIM), low_shape(slots, columns), full_shape(slots, 1)],
        info,
        (first_in, inward, *tables),
        [pltpu.VMEM((slots, HEAD_DIM), jnp.bfloat16)] * 2,
    )
    return (out, (qkv, lse))


def heads_back_body(
    steps, info, qkv_ref, lse_ref, grad_ref, cos_ref, low_ref, high_ref, out_ref, dk_ref, dv_ref
):
    step = pl.program_id(0)
    slots = qkv_ref.shape[0]
    rows = slots // steps

    def tables(start, size):
        return tuple(ref[start : start + size] for ref in (cos_ref, low_ref, high_ref))

    @pl.when(step == 0)
    def _():
        dk_ref[...] = jnp.zeros_like(dk_ref)
        dv_ref[...] = jnp.zeros_like(dv_ref)

    for now in range(steps):

        @pl.when(step == now)
        def _():
            span, start = (now + 1) * rows, now * rows
            query = qkv_ref[start:span, :HEAD_DIM]
            keys = qkv_ref[:span, HEAD_DIM : 2 * HEAD_DIM]
            values = qkv_ref[:span, 2 * HEAD_DIM :]
            grad = grad_ref[...]
            scores = dot_nt(query, keys) * SCALE
            allowed = allowed_block(start, rows, span, info[0])
            probs = jnp.where(allowed, jnp.exp(scores - lse_ref[...]), 0.0)
            prob_grad = dot_nt(grad, values)
            spread = jnp.sum(probs * prob_grad, axis=1, keepdims=True)
            score_grad = (probs * (prob_grad - spread)).astype(jnp.bfloat16)
            query_grad = dot(score_grad, keys) * SCALE
            out_ref[start:span, :HEAD_DIM] = turned(
                query_grad, tables(start, rows), -1.0
            ).astype(jnp.bfloat16)
            dv_ref[:span] += dot_tn(probs.astype(jnp.bfloat16), grad)
            dk_ref[:span] += dot_tn(score_grad, query)

    @pl.when(step == steps - 1)
    def _():
        out_ref[:, HEAD_DIM : 2 * HEAD_DIM] = turned(
            dk_ref[...] * SCALE, tables(0, slots), -1.0
        ).astype(jnp.bfloat16)
        out_ref[:, 2 * HEAD_DIM :] = dv_ref[...].astype(jnp.bfloat16)


def heads_back_call(saved, out_grad, tables, info):
    qkv, lse = saved
    slots, columns = qkv.shape
    rows = min(slots, 256)
    steps = slots // rows
    return call(
        functools.partial(heads_back_body, steps),
        (steps,),
        [
            fixed(qkv.shape),
            pl.BlockSpec((rows, 1), lambda i, info: (i, 0)),
            pl.BlockSpec((rows, HEAD_DIM), lambda i, info: (i, 0)),
        ]
        + [fixed((slots, 128))] * 3,
        pl.BlockSpec((slots, columns), lambda i, info: (0, 0)),
        low_shape(slots, columns),
        info,
        (qkv, lse, out_grad, *tables),
        [pltpu.VMEM((slots, HEAD_DIM), jnp.float32)] * 2,
    )


def units_body(info, x_ref, w_ref, offset_ref, act_ref, slope_ref):
    columns = w_ref.shape[1]
    size = min(columns, 512)
    for start in range(0, columns, size):
        here = slice(start, start + size)
        hidden = dot(x_ref[...], w_ref[:, here]) + offset_ref[:, here]
        cdf = 0.5 * (1.0 + lax.erf(hidden * 0.7071067811865476))
        act_ref[:, here] = (hidden * cdf).astype(jnp.bfloat16)
        bell = jnp.exp(-0.5 * hidden * hidden) * 0.3989422804014327
        slope_ref[:, here] = (cdf + hidden * bell).astype(jnp.bfloat16)


def units_call(second_in, expand, start, offsets, unit, info):
    slots, width = second_in.shape
    columns = offsets.shape[0]
    tall = min(slots, 256)
    spec = pl.BlockSpec((tall, columns), lambda i, info: (i, 0))
    return call(
        units_body,
        (slots // tall,),
        [
            pl.BlockSpec((tall, width), lambda i, info: (i, 0)),
            held(width, columns, start * unit // columns),
            fixed((1, columns)),
        ],
        [spec, spec],
        [low_shape(slots, columns)] * 2,
        info,
        (second_in, expand, offsets[None]),
    )


def halving_blocks(half, tall):
    return ([tall] * half + [half * tall]) * 2


def place_rows(info, value_ref, outs, half, tall):
    for which in range(4):
        stream, kept = which // 2, which % 2
        for place in range(half):
            start = (2 * info[which * half + place] + stream) * tall
            rows = value_ref[pl.ds(pl.multiple_of(start, tall), tall)]
            if kept:
                outs[stream * (half + 1) + half][place * tall : (place + 1) * tall] = rows
            else:
                outs[stream * (half + 1) + place][...] = rows


def partial_body(half, tall, info, *refs):
    value = None
    for left, right in zip(refs[:4], refs[4:8]):
        term = dot_nt(left[...], right[...])
        value = term if value is None else value + term
    outs, value_ref = refs[8:-1], refs[-1]
    value_ref[...] = value.astype(jnp.bfloat16)
    if half:
        place_rows(info, value_ref, outs, half, tall)
    else:
        outs[0][...] = value_ref[...]


def partial_call(heads, acts, outward, contract, outward_at, contract_at, places):
    slots, unit = heads[0].shape
    wide = acts[0].shape[1]
    width = outward[0].shape[0]
    block = min(width, 512)
    half = len(places) // 4
    tall = slots // (4 * half) if half else 0
    heights = halving_blocks(half, tall) if half else [slots]
    info = jnp.stack([jnp.asarray(item, jnp.int32) for item in (places or [0])])
    return call(
        functools.partial(partial_body, half, tall),
        (width // block,),
        [fixed(item.shape) for item in (*heads, *acts)]
        + [pl.BlockSpec((block, unit), lambda j, info: (j, outward_at))] * 2
        + [pl.BlockSpec((block, wide), lambda j, info: (j, contract_at * unit // wide))] * 2,
        [pl.BlockSpec((height, block), lambda j, info: (0, j)) for height in heights],
        [low_shape(height, width) for height in heights],
        info,
        (*heads, *acts, *outward, *contract),
        [pltpu.VMEM((slots, block), jnp.bfloat16)],
    )


PIECES = 4


def grads_body(count, split, info, *refs):
    lefts, rights, rest = refs[:count], refs[count : 2 * count], refs[2 * count :]
    got, outs = ((), rest) if split else (rest[:PIECES], rest[PIECES:])
    size = (outs[0].shape[1]) if split else got[0].shape[1]
    start = 0
    for left, right in zip(lefts, rights):
        value = dot(left[...], right[...])
        for piece in range(PIECES):
            low = max(start, piece * size)
            high = min(start + right.shape[1], (piece + 1) * size)
            if low >= high:
                continue
            term = value[:, low - start : high - start]
            inner = slice(low - piece * size, high - piece * size)
            if split:
                outs[piece][:, inner] = term.astype(jnp.bfloat16)
            else:
                term = term + got[piece][:, inner].astype(jnp.float32)
                outs[0][:, low:high] = term.astype(jnp.bfloat16)
        start = start + right.shape[1]


def grads_call(lefts, rights, info, got=None, cost=CHEAP):
    width, slots = lefts[0].shape
    columns = sum(item.shape[1] for item in rights)
    block = min(width, 256)
    split = got is None
    spec = pl.BlockSpec((block, columns), lambda j, info: (j, 0))
    piece_specs = [pl.BlockSpec((block, columns // PIECES), lambda j, info: (j, 0))] * PIECES
    out = call(
        functools.partial(grads_body, len(lefts), split),
        (width // block,),
        [pl.BlockSpec((block, slots), lambda j, info: (j, 0))] * len(lefts)
        + [fixed(item.shape) for item in rights]
        + ([] if split else piece_specs),
        piece_specs if split else spec,
        [low_shape(width, columns // PIECES)] * PIECES if split else low_shape(width, columns),
        info,
        (*lefts, *rights, *(got or ())),
        cost=cost,
    )
    return out


def lifted_body(info, g_ref, outward_ref, contract_ref, slope_ref, out_ref, hidden_ref, sum_ref):
    columns = contract_ref.shape[1]
    size = min(columns, 512)

    @pl.when(pl.program_id(0) == 0)
    def _():
        sum_ref[...] = jnp.zeros_like(sum_ref)

    for start in range(0, columns, size):
        here = slice(start, start + size)
        value = dot(g_ref[...], contract_ref[:, here]) * slope_ref[:, here].astype(jnp.float32)
        value = value.astype(jnp.bfloat16)
        hidden_ref[:, here] = value
        sum_ref[:, here] += jnp.sum(value.astype(jnp.float32), axis=0, keepdims=True)
    out_ref[...] = dot(g_ref[...], outward_ref[...]).astype(jnp.bfloat16)


def lifted_call(grad, outward, contract, outward_at, contract_at, slope, unit, info):
    slots, width = grad.shape
    columns = slope.shape[1]
    tall = min(slots, 256)

    def rows(size):
        return pl.BlockSpec((tall, size), lambda i, info: (i, 0))

    return call(
        lifted_body,
        (slots // tall,),
        [
            rows(width),
            held(width, unit, outward_at),
            held(width, columns, contract_at * unit // columns),
            rows(columns),
        ],
        [rows(unit), rows(columns), pl.BlockSpec((1, columns), lambda i, info: (0, 0))],
        [low_shape(slots, unit), low_shape(slots, columns), full_shape(1, columns)],
        info,
        (grad, outward, contract, slope),
    )


def back_body(half, tall, info, *refs):
    z_ref, mean_ref, scale_ref, vec_ref = refs[:4]
    mixed, hidden, inward, expand = refs[4:6], refs[6:8], refs[8:10], refs[10:12]
    outs, sums_ref, hat_ref, total_ref, along_ref = refs[12:-4], *refs[-4:]
    part, block = pl.program_id(0), pl.program_id(1)
    size = inward[0].shape[0]
    width = z_ref.shape[1]
    columns = pl.ds(pl.multiple_of(block * size, size), size)
    mean, scale = mean_ref[...], scale_ref[...]
    first = dot_nt(mixed[0][...], inward[0][...]) + dot_nt(mixed[1][...], inward[1][...])
    second = dot_nt(hidden[0][...], expand[0][...]) + dot_nt(hidden[1][...], expand[1][...])
    normed = (z_ref[:, columns].astype(jnp.float32) - mean) * scale
    sums = [
        jnp.sum(value, axis=0, keepdims=True)
        for value in (first * normed, first, second * normed, second)
    ]

    @pl.when(part == 0)
    def _():
        for row in range(4):
            sums_ref[row : row + 1, columns] = sums[row]

    @pl.when(part > 0)
    def _():
        for row in range(4):
            sums_ref[row : row + 1, columns] += sums[row]

    hat = first * vec_ref[0:1] + second * vec_ref[2:3]
    hat_ref[:, columns] = hat
    total = jnp.sum(hat, axis=1, keepdims=True)
    along = jnp.sum(hat * normed, axis=1, keepdims=True)

    @pl.when(block == 0)
    def _():
        total_ref[...] = total
        along_ref[...] = along

    @pl.when(block > 0)
    def _():
        total_ref[...] += total
        along_ref[...] += along

    @pl.when(block == pl.num_programs(1) - 1)
    def _():
        rows = hat_ref.shape[0]
        step = tall if half else min(rows, 256)
        for start in range(0, rows, step):
            here = slice(start, start + step)
            normed_here = (z_ref[here].astype(jnp.float32) - mean_ref[here]) * scale_ref[here]
            result = scale_ref[here] * (
                hat_ref[here]
                - total_ref[here] / width
                - normed_here * (along_ref[here] / width)
            )
            result = result.astype(jnp.bfloat16)
            if not half:
                outs[0][pl.ds(part * rows + start, step)] = result
                continue
            stream = start // tall % 2
            peer = part * (rows // (2 * tall)) + start // (2 * tall)
            at = 2 * (2 * peer + stream)
            own_outs = outs[stream * (half + 1) : (stream + 1) * (half + 1)]

            @pl.when(info[at] == 0)
            def _():
                own_outs[half][pl.ds(pl.multiple_of(info[at + 1] * tall, tall), tall)] = result

            for place in range(half):

                @pl.when((info[at] == 1) & (info[at + 1] == place))
                def _():
                    own_outs[place][...] = result


def back_call(rows, stats, vectors, mixed_grads, hidden_grads, inward, expand, expand_at, me, peers, bits):
    slots, width = rows.shape
    parts = 2 if bits else 1
    rows_each = slots // parts
    block = min(width, 512)
    half = peers // 2 if bits else 0
    tall = slots // (2 * peers) if bits else 0
    heads_columns, wide = mixed_grads[0].shape[1], hidden_grads[0].shape[1]
    table = []
    for peer in range(peers if bits else 0):
        for stream in (0, 1):
            bit = step_bits(bits, stream)[0]
            own = (me >> bit) & 1
            place = (peer & ((1 << bit) - 1)) | ((peer >> (bit + 1)) << bit)
            table.append(jnp.asarray(((peer >> bit) & 1) != own, jnp.int32))
            table.append(jnp.asarray(place, jnp.int32))
    info = jnp.stack(table or [jnp.asarray(0, jnp.int32)])
    heights = halving_blocks(half, tall) if half else [slots]

    def spec(columns):
        return pl.BlockSpec((rows_each, columns), lambda i, j, info: (i, 0))

    def weights(columns, at):
        return pl.BlockSpec((block, columns), lambda i, j, info: (j, at))

    def whole(*shape):
        return pl.BlockSpec(shape, lambda i, j, info: (0, 0))

    out = call(
        functools.partial(back_body, half, tall),
        (parts, width // block),
        [spec(width), spec(1), spec(1)]
        + [pl.BlockSpec((vectors.shape[0], block), lambda i, j, info: (0, j))]
        + [spec(item.shape[1]) for item in (*mixed_grads, *hidden_grads)]
        + [weights(heads_columns, 0)] * 2
        + [weights(wide, expand_at * heads_columns // (3 * wide))] * 2,
        [whole(height, width) for height in heights] + [whole(4, width)],
        [low_shape(height, width) for height in heights] + [full_shape(4, width)],
        info,
        (rows, *stats, vectors, *mixed_grads, *hidden_grads, *inward, *expand),
        [pltpu.VMEM((rows_each, width), jnp.float32)]
        + [pltpu.VMEM((rows_each, 1), jnp.float32)] * 2,
    )
    return out[:-1], out[-1]


def share_of(total):
    return lax.psum_scatter(total, "dp", scatter_dimension=0, tiled=True)


def adam_kernel(rate, decay, arrange, info, *refs):
    grads, (master, first, second), outs = refs[:4], refs[4:7], refs[7:]

    def run(half, region, turn):
        grad = jnp.where(info[0] == 0, grads[half][...], grads[2 + half][...]).astype(jnp.float32)
        grad = grad.T if turn else grad
        new = adam_update(master[region], grad, first[region], second[region], rate, decay)
        for out, value in zip(outs, new):
            out[region] = value

    arrange(run)


def adam_columns(index, grads, arrays, depth, starts, core):
    parts, _, columns = arrays[0].shape
    half = columns // 2
    tall = depth // 4

    def arrange(run):
        for which in (0, 1):
            run(which, (0, slice(None), pl.ds(which * half, half)), False)

    def grad_spec(start):
        return pl.BlockSpec((tall, half), lambda i, j, info: (j, start + i))

    block_spec = pl.BlockSpec((1, tall, columns), lambda i, j, info: (i, j, 0))
    return call(
        functools.partial(adam_kernel, RATES[index], DECAYS[index], arrange),
        (parts, depth // tall),
        [grad_spec(starts[which // 2]) for which in range(4)] + [block_spec] * 3,
        [block_spec] * 3,
        [jax.ShapeDtypeStruct(arrays[0].shape, jnp.float32)] * 3,
        core,
        (*grads, *arrays),
    )


def adam_rows(index, grads, arrays, starts, block, core):
    units, depth = arrays[0].shape
    each = units // 2 // block

    def arrange(run):
        for half in (0, 1):

            @pl.when(pl.program_id(0) == half)
            def _():
                run(half, Ellipsis, True)

    def grad_spec(half, start):
        def place(h, j, info):
            return (0, start + jnp.where(h == half, j, (each - 1) * (1 - half)))

        return pl.BlockSpec((depth, block), place)

    block_spec = pl.BlockSpec((block, depth), lambda h, j, info: (h * each + j, 0))
    return call(
        functools.partial(adam_kernel, RATES[index], DECAYS[index], arrange),
        (2, each),
        [grad_spec(which % 2, starts[which // 2]) for which in range(4)] + [block_spec] * 3,
        [block_spec] * 3,
        [jax.ShapeDtypeStruct(arrays[0].shape, jnp.float32)] * 3,
        core,
        (*grads, *arrays),
    )


def adam_update(master, grad, first, second, rate, decay):
    new_first = 0.9 * first + 0.1 * grad
    new_second = 0.95 * second + 0.05 * grad * grad
    corrected = new_first / (1.0 - 0.9**STEP)
    spread = jnp.sqrt(new_second / (1.0 - 0.95**STEP))
    return (master - rate * (corrected / (spread + 1e-08) + decay * master), new_first, new_second)


def local(
    tokens,
    cotangent,
    lengths,
    inward,
    outward,
    expand,
    contract,
    vectors,
    offsets,
    inward_first,
    inward_second,
    outward_first,
    outward_second,
    expand_first,
    expand_second,
    contract_first,
    contract_second,
    vectors_first,
    vectors_second,
    offsets_first,
    offsets_second,
):
    core = lax.axis_index("pipe")
    peers = lax.axis_size("tensor")
    groups = lax.axis_size("dp")
    place = lax.axis_index("tensor")
    depth = inward.shape[1]
    heads_local = inward.shape[3] // HEAD_DIM
    lone = heads_local == 2
    head_share = inward.shape[3] // 2
    unit_share = expand.shape[2] // 2
    batches = lengths.shape[0]
    width = tokens.shape[1]
    slots = tokens.shape[0] // batches
    row_share = slots // peers

    bits = halving(peers, slots)

    def packed(shard):
        mine, theirs = (item.astype(jnp.bfloat16).reshape(depth, -1) for item in halves(shard, core))
        got = swap(theirs)
        return (jnp.where(core == 0, mine, got), jnp.where(core == 0, got, mine))

    packs = [packed(item) for item in (inward[0], expand[0], outward[0].T, contract[0].T)]
    count = unit_share // head_share

    small = jnp.concatenate([vectors.reshape(-1), offsets.reshape(-1)]).astype(jnp.bfloat16)
    small = lax.all_gather(small, ("pipe", "dp"), axis=0, tiled=False).reshape(2, groups, -1)
    small = small.astype(jnp.float32)
    vector_values = [
        small[layer, :, : 5 * depth].reshape(groups, 5, depth).transpose(1, 0, 2).reshape(5, width)
        for layer in (0, 1)
    ]
    offset_pairs = [halves(small[layer, :, 5 * depth :].reshape(-1), core) for layer in (0, 1)]

    tables = angle_tables(slots)
    turns = turn_tables(slots)
    length = lax.dynamic_index_in_dim(lengths, core, 0, keepdims=False)
    info = length[None]
    own = lax.dynamic_slice_in_dim(tokens, core * slots, slots, 0)
    target, target_turned = target_call(cotangent, slots, jnp.stack([length, core]))
    places = scatter_places(place, peers, bits) if bits else []

    def whole_of(shard):
        return lax.all_gather(shard, "dp", axis=0, tiled=True)

    def pair_of(whole, *earlier):
        whole = after(whole, *earlier)
        return (whole, swap(whole))

    def block_of(array):
        block = lax.dynamic_slice_in_dim(array, place * row_share, row_share, 0)
        return block.astype(jnp.float32)

    def summed(pieces):
        if bits:
            return jnp.concatenate(sum_scatter(pieces, peers, bits), axis=0)
        return lax.psum_scatter(pieces[0], "tensor", scatter_dimension=0, tiled=True).astype(
            jnp.float32
        )

    def spread(block):
        tall = row_share // 2
        return rows_pieces((block[:tall], block[tall:]), peers, bits)

    def heads_of(first_in, inward_pair):
        if lone:
            done = [heads_call(first_in, item, turns, info) for item in inward_pair]
            return ([item[0] for item in done], [item[1] for item in done])
        mixed = [dot(first_in, w[:, : 3 * head_share]).reshape(slots, 3, -1) for w in inward_pair]
        mixed = ordered(mixed[0], mixed[1], core).reshape(slots, 3, -1, HEAD_DIM)
        out, saved = attend(mixed, length, tables)
        return (list(halves(out, core)), saved)

    def heads_back(out_grads, saved):
        if lone:
            return [heads_back_call(kept, grad, turns, info) for grad, kept in zip(out_grads, saved)]
        grad = ordered(out_grads[0], out_grads[1], core)
        mixed_grad = attend_back(grad, saved, length, tables).reshape(slots, 3, -1)
        return [item.reshape(slots, -1) for item in halves(mixed_grad, core)]

    def units_of(second_in, expand_pair, start, layer):
        done = [
            units_call(
                second_in, expand_pair[which], start, offset_pairs[layer][which], head_share, info
            )
            for which in (0, 1)
        ]
        return ([item[0] for item in done], [item[1] for item in done])

    def layer_output(layer, outward_pair, contract_pair, heads, acts):
        pieces = partial_call(
            heads, acts, outward_pair, contract_pair, outward_at[layer], contract_at[layer], places
        )
        block = summed(pieces) + block_of(inputs[layer]) + vector_values[layer][4]
        return block.astype(jnp.bfloat16)

    outward_at, contract_at, expand_at = (2 * count, 3), (0, 0), (count, 4)
    shards = [packs[0][0], jnp.concatenate([packs[3][0], packs[1][0], packs[2][0]], axis=1)]
    shards.append(jnp.concatenate([after(packs[0][1], shards[1]), packs[2][1], packs[1][1]], axis=1))
    shards.append(after(packs[3][1], shards[2]))
    shards[1] = after(shards[1], shards[0])
    wholes = [whole_of(item) for item in shards]
    inputs = [own]
    normed = norms_call(own, vector_values[0], info)
    first_in, second_in = normed[:2]
    inward_pairs = [pair_of(wholes[0], first_in, second_in, target_turned)]
    heads, saved = heads_of(first_in, inward_pairs[0])
    rest_pair = pair_of(wholes[1], *heads)
    acts, slopes = units_of(second_in, rest_pair, expand_at[0], 0)
    kept = [(normed, heads, saved, acts, slopes)]
    outward_pairs, contract_pairs, expand_pairs = [rest_pair], [rest_pair], [rest_pair]
    results = [layer_output(0, rest_pair, rest_pair, heads, acts)]
    if bits:
        rows, normed = assemble(
            spread(results[0]), peers, bits, vector_values[1]
        )
        inputs.append(rows)
    else:
        inputs.append(lax.all_gather(results[0], "tensor", axis=0, tiled=True))
        normed = norms_call(inputs[1], vector_values[1], info)
    first_in, second_in = normed[:2]
    rest_pair = pair_of(wholes[2], first_in, second_in)
    for store in (inward_pairs, outward_pairs, expand_pairs):
        store.append(rest_pair)
    acts, slopes = units_of(second_in, rest_pair, expand_at[1], 1)

    grad_low, grad_turned = target, target_turned
    shares, row_grads, vector_grads, offset_grads = [None] * 2, [None] * 2, [None] * 2, [None] * 2
    for layer in (1, 0):
        if layer == 0:
            normed, heads, saved, acts, slopes = kept[0]
        theirs = grads_call([grad_turned], [acts[1]], info)
        if layer == 1:
            heads, saved = heads_of(after(first_in, *theirs), rest_pair)
            theirs = [after(after(item, acts[0], *heads), wholes[3]) for item in theirs]
        got = [swap(item) for item in theirs]
        contract_total = grads_call([grad_turned], [acts[0]], info, got)
        contract_share = share_of(contract_total)
        if layer == 1:
            contract_pairs.append(pair_of(wholes[3], *theirs))
        grad_here = after(grad_low, contract_total)
        lifted = [
            lifted_call(
                grad_here,
                outward_pairs[layer][which],
                contract_pairs[layer][which],
                outward_at[layer],
                contract_at[layer],
                slopes[which],
                head_share,
                info,
            )
            for which in (0, 1)
        ]
        hidden_grads = [item[1] for item in lifted]
        offset_grads[layer] = [item[2][0] for item in lifted]
        first_turned, second_turned = normed[4:]

        def total_of(lefts, theirs, mine, cost=CHEAP):
            got = [swap(item) for item in grads_call(lefts, theirs, info, cost=cost)]
            return grads_call(lefts, mine, info, got, cost)

        out_grads = [item[0] for item in lifted]
        if layer == 1:
            expand_total = total_of([second_turned], [hidden_grads[1]], [hidden_grads[0]])
            expand_share = share_of(expand_total)
            out_grads = [after(item, expand_total) for item in out_grads]
        mixed_grads = heads_back(out_grads, saved)
        lefts = [first_turned, grad_turned]
        rights = [[mixed_grads[which], heads[which]] for which in (1, 0)]
        if layer == 0:
            hidden_here = [after(item, *shares[1], *mixed_grads) for item in hidden_grads]
            other_total = total_of(
                [second_turned] + lefts,
                [hidden_here[1]] + rights[0],
                [hidden_here[0]] + rights[1],
            )
            ahead = [other_total]
        else:
            ahead = [contract_share, *mixed_grads]
        pieces, norm_part = back_call(
            after(inputs[layer], *ahead),
            normed[2:4],
            vector_values[layer],
            mixed_grads,
            hidden_grads,
            inward_pairs[layer],
            expand_pairs[layer],
            expand_at[layer],
            place,
            peers,
            bits,
        )
        if layer == 1:
            lefts[0] = after(lefts[0], *pieces)
            flops = 8 * slots * width * head_share
            cost = pl.CostEstimate(
                flops=4 * flops, transcendentals=0, bytes_accessed=4 * flops // slots
            )
            shares[1] = (share_of(total_of(lefts, *rights, cost)), expand_share, contract_share)
        else:
            pieces = [after(item, contract_share) for item in pieces]
            shares[0] = (share_of(other_total), contract_share)
        upstream = block_of(grad_low)
        vector_grads[layer] = jnp.concatenate(
            [norm_part, jnp.sum(upstream, axis=0)[None]], axis=0
        )
        row_grads[layer] = upstream + summed(pieces)
        if layer == 1:
            block = row_grads[layer].astype(jnp.bfloat16)
            if bits:
                grad_low, grad_turned = assemble(
                    [after(item, expand_share) for item in spread(block)], peers, bits
                )
            else:
                grad_low = lax.all_gather(block, "tensor", axis=0, tiled=True)
                grad_turned = grad_low.T
            last = (heads, acts)
        else:
            pairs = [
                [after(item, other_total) for item in pair]
                for pair in (outward_pairs[1], contract_pairs[1])
            ]
            results.append(layer_output(1, *pairs, *last))

    activations = jnp.where(core == 0, results[0], results[1])
    got = swap(jnp.where(core == 0, results[1], results[0]))
    activations = jnp.where(
        core == 0, jnp.stack([activations, got]), jnp.stack([got, activations])
    )[None]
    gradients = jnp.where(core == 0, row_grads[0], row_grads[1])
    got = swap(jnp.where(core == 0, row_grads[1], row_grads[0]))
    gradients = jnp.where(core == 0, jnp.stack([gradients, got]), jnp.stack([got, gradients]))[None]

    def to_owner(first, second, *earlier):
        first = after(first, *earlier)
        from_first = lax.ppermute(first, "pipe", [(1, 0)])
        from_second = lax.ppermute(second, "pipe", [(0, 1)])
        return (first, from_first, from_second, second)

    vector_sum = added(jnp.stack(vector_grads), "tensor")
    offset_sum = jnp.stack([ordered(item[0], item[1], core) for item in offset_grads])
    small_sum = jnp.concatenate([vector_sum.reshape(2, -1), offset_sum], axis=1)
    small_sum = added(added(small_sum, "pipe"), "dp")
    small_sum = lax.dynamic_index_in_dim(small_sum, core, 0, keepdims=False)
    where = lax.axis_index("dp")
    vector_grad = lax.dynamic_slice_in_dim(
        small_sum[: 5 * width].reshape(5, width), where * depth, depth, 1
    )
    offset_size = offsets.shape[1]
    offset_grad = lax.dynamic_slice_in_dim(
        small_sum, 5 * width + where * offset_size, offset_size, 0
    )

    def viewed(*arrays):
        return [item[0] for item in arrays]

    def parts_first(*arrays):
        return [item[0].transpose(1, 0, 2) for item in arrays]

    which = core[None]
    contract_out = adam_rows(
        3,
        to_owner(shares[0][1], shares[1][2]),
        viewed(contract, contract_first, contract_second),
        (0, 0),
        head_share,
        which,
    )
    last_share = after(shares[0][0], contract_out[0])
    expand_out = adam_columns(
        2,
        to_owner(last_share, shares[1][1]),
        [expand, expand_first, expand_second],
        depth,
        (0, 0),
        which,
    )
    heads_grads = to_owner(last_share, shares[1][0])
    outward_out = adam_rows(
        1,
        heads_grads,
        viewed(outward, outward_first, outward_second),
        (count + 3, 3),
        head_share,
        which,
    )
    inward_out = adam_columns(
        0,
        heads_grads,
        parts_first(inward, inward_first, inward_second),
        depth,
        (count, 0),
        which,
    )
    outputs = [activations, gradients]
    outputs.extend([item.transpose(1, 0, 2)[None] for item in inward_out])
    outputs.extend([item[None] for item in outward_out])
    outputs.extend(expand_out)
    outputs.extend([item[None] for item in contract_out])
    outputs.extend(
        adam_update(vectors, vector_grad[None], vectors_first, vectors_second, RATES[4], DECAYS[4])
    )
    outputs.extend(
        adam_update(offsets, offset_grad[None], offsets_first, offsets_second, RATES[5], DECAYS[5])
    )
    return tuple(outputs)


def solution(mesh):
    return jax.shard_map(
        local,
        mesh=mesh,
        in_specs=(
            P("dp", None),
            P("dp", None),
            P("dp"),
            P("pipe", "dp", None, "tensor"),
            P("pipe", "tensor", "dp"),
            P("pipe", "dp", "tensor"),
            P("pipe", "tensor", "dp"),
            P("pipe", None, "dp"),
            P("pipe", ("tensor", "dp")),
            P("pipe", "dp", None, "tensor"),
            P("pipe", "dp", None, "tensor"),
            P("pipe", "tensor", "dp"),
            P("pipe", "tensor", "dp"),
            P("pipe", "dp", "tensor"),
            P("pipe", "dp", "tensor"),
            P("pipe", "tensor", "dp"),
            P("pipe", "tensor", "dp"),
            P("pipe", None, "dp"),
            P("pipe", None, "dp"),
            P("pipe", ("tensor", "dp")),
            P("pipe", ("tensor", "dp")),
        ),
        out_specs=(
            P("pipe", "dp", "tensor", None),
            P("pipe", "dp", "tensor", None),
            P("pipe", "dp", None, "tensor"),
            P("pipe", "dp", None, "tensor"),
            P("pipe", "dp", None, "tensor"),
            P("pipe", "tensor", "dp"),
            P("pipe", "tensor", "dp"),
            P("pipe", "tensor", "dp"),
            P("pipe", "dp", "tensor"),
            P("pipe", "dp", "tensor"),
            P("pipe", "dp", "tensor"),
            P("pipe", "tensor", "dp"),
            P("pipe", "tensor", "dp"),
            P("pipe", "tensor", "dp"),
            P("pipe", None, "dp"),
            P("pipe", None, "dp"),
            P("pipe", None, "dp"),
            P("pipe", ("tensor", "dp")),
            P("pipe", ("tensor", "dp")),
            P("pipe", ("tensor", "dp")),
        ),
        check_vma=False,
    )
```

```python
import functools

import jax
import jax.numpy as jnp
from jax import lax
from jax.experimental import pallas as pl
from jax.experimental.pallas import tpu as pltpu
from jax.sharding import PartitionSpec as P

HEAD_DIM = 256
ROT = 64
STEP = 10


RATES = (0.03, 0.2, 0.03, 0.015, 0.3, 0.3)
DECAYS = (0.01, 0.01, 0.01, 0.01, 0.0, 0.0)


def angle_tables(slots):
    half = ROT // 2
    positions = jnp.arange(slots).astype(jnp.float32)
    frequency = 10000.0 ** (-(2.0 * jnp.arange(half).astype(jnp.float32)) / ROT)
    angles = positions[:, None] * frequency[None, :]
    return (jnp.cos(angles)[:, None, :], jnp.sin(angles)[:, None, :])


def rotate(block, cosine, sine):
    half = cosine.shape[-1]
    first = block[..., :half]
    second = block[..., half : 2 * half]
    return jnp.concatenate(
        [first * cosine - second * sine, second * cosine + first * sine, block[..., 2 * half :]],
        axis=-1,
    )


def rotate_back(grad, cosine, sine):
    half = cosine.shape[-1]
    first = grad[..., :half]
    second = grad[..., half : 2 * half]
    return jnp.concatenate(
        [first * cosine + second * sine, second * cosine - first * sine, grad[..., 2 * half :]],
        axis=-1,
    )


def norm_parts(rows, gain, shift):
    center = rows - jnp.mean(rows, axis=1, keepdims=True)
    scale = lax.rsqrt(jnp.mean(center * center, axis=1, keepdims=True) + 1e-05)
    normed = center * scale
    return (normed * gain + shift, normed, scale)


def norm_back(back, rows, gain):
    unused, normed, scale = norm_parts(rows, gain, 0.0)
    hat = back * gain
    row_grad = scale * (
        hat
        - jnp.mean(hat, axis=1, keepdims=True)
        - normed * jnp.mean(hat * normed, axis=1, keepdims=True)
    )
    return (row_grad, jnp.sum(back * normed, axis=0), jnp.sum(back, axis=0))


def gelu_slope(hidden):
    return (
        0.5 * (1.0 + lax.erf(hidden * 0.7071067811865476))
        + hidden * jnp.exp(-0.5 * hidden * hidden) * 0.3989422804014327
    )


def allowed_mask(slots, length):
    places = jnp.arange(slots)
    return (places[None, :] <= places[:, None]) & (places[None, :] < length)


def after(array, *earlier):
    return lax.optimization_barrier((array, *earlier))[0]


def added(array, axis):
    peers = lax.axis_size(axis)
    bits = peers.bit_length() - 1
    if peers != 1 << bits:
        return lax.psum(array, axis)
    for bit in range(bits):
        array = array + lax.ppermute(array, axis, [(i, i ^ (1 << bit)) for i in range(peers)])
    return array


def swap(array):
    return lax.ppermute(array, "pipe", [(0, 1), (1, 0)])


def halves(array, core):
    size = array.shape[-1] // 2
    axis = array.ndim - 1
    mine = lax.dynamic_slice_in_dim(array, core * size, size, axis)
    theirs = lax.dynamic_slice_in_dim(array, (1 - core) * size, size, axis)
    return (mine, theirs)


def ordered(mine, theirs, core):
    return jnp.where(
        core == 0,
        jnp.concatenate([mine, theirs], axis=-1),
        jnp.concatenate([theirs, mine], axis=-1),
    )


def flipped(array, peers, bit):
    return lax.ppermute(array, "tensor", [(i, i ^ (1 << bit)) for i in range(peers)])


def halving(peers, rows):
    bits = peers.bit_length() - 1
    return bits if peers == 1 << bits and bits > 0 and rows % (16 * peers) == 0 else 0


def step_bits(bits, stream):
    return [step if stream == 0 else bits - 1 - step for step in range(bits)]


def relative_order(bits, stream):
    order = [0]
    for bit in reversed(step_bits(bits, stream)):
        order = order + [other ^ (1 << bit) for other in order]
    return order


def scatter_places(me, peers, bits):
    half = peers // 2
    places = []
    for stream in (0, 1):
        bit = step_bits(bits, stream)[0]
        own = (me >> bit) & 1
        for value in (1 - own, own):
            for place in range(half):
                low = place & ((1 << bit) - 1)
                high = (place >> bit) << (bit + 1)
                places.append(high | (value << bit) | low)
    return places


def sum_scatter(pieces, peers, bits):
    me = lax.axis_index("tensor")
    half = peers // 2
    width = pieces[0].shape[1]
    sends = [pieces[k * (half + 1) : k * (half + 1) + half] for k in (0, 1)]
    keeps = [pieces[k * (half + 1) + half] for k in (0, 1)]
    left = [[b for b in reversed(range(bits)) if b != step_bits(bits, k)[0]] for k in (0, 1)]
    for step in range(bits):
        arrived = lax.optimization_barrier(
            [[flipped(item, peers, step_bits(bits, k)[step]) for item in sends[k]] for k in (0, 1)]
        )
        for k in (0, 1):
            got = arrived[k]
            total = jnp.stack(
                [
                    keep.astype(jnp.float32) + item.astype(jnp.float32)
                    for keep, item in zip(jnp.split(keeps[k], len(got), axis=0), got)
                ]
            )
            if step == bits - 1:
                keeps[k] = total[0]
                continue
            total = total.astype(jnp.bfloat16).reshape((2,) * len(left[k]) + (-1, width))
            bit = step_bits(bits, k)[step + 1]
            axis = left[k].index(bit)
            own = (me >> bit) & 1
            keep = lax.dynamic_index_in_dim(total, own, axis, keepdims=False)
            send = lax.dynamic_index_in_dim(total, 1 - own, axis, keepdims=False)
            keeps[k] = keep.reshape(-1, width)
            sends[k] = jnp.split(send.reshape(-1, width), len(got) // 2, axis=0)
            left[k].pop(axis)
    return keeps


def rows_pieces(blocks, peers, bits):
    current = [[item] for item in blocks]
    for step in reversed(range(bits)):
        arrived = lax.optimization_barrier(
            [[flipped(item, peers, step_bits(bits, k)[step]) for item in current[k]] for k in (0, 1)]
        )
        current = [current[k] + arrived[k] for k in (0, 1)]
    return current[0] + current[1]


def attend(mixed, length, tables):
    slots = mixed.shape[0]
    cosine, sine = tables
    query = rotate(mixed[:, 0], cosine, sine).astype(jnp.bfloat16)
    keys = rotate(mixed[:, 1], cosine, sine).astype(jnp.bfloat16)
    values = mixed[:, 2].astype(jnp.bfloat16)
    scores = jnp.einsum(
        "qhd,khd->hqk", query, keys, preferred_element_type=jnp.float32
    ) * HEAD_DIM ** (-0.5)
    scores = jnp.where(allowed_mask(slots, length)[None], scores, -jnp.inf)
    peak = jnp.max(scores, axis=-1, keepdims=True)
    expo = jnp.exp(scores - peak)
    total = jnp.sum(expo, axis=-1, keepdims=True)
    probs_low = (expo / total).astype(jnp.bfloat16)
    logsum = peak + jnp.log(total)
    heads_out = jnp.einsum("hqk,khd->qhd", probs_low, values, preferred_element_type=jnp.float32)
    return (heads_out.reshape(slots, -1).astype(jnp.bfloat16), (query, keys, values, logsum))


def attend_back(out_grad, saved, length, tables):
    query, keys, values, logsum = saved
    slots, heads = query.shape[:2]
    cosine, sine = tables
    out_grad = out_grad.reshape(slots, heads, HEAD_DIM)
    scores = jnp.einsum(
        "qhd,khd->hqk", query, keys, preferred_element_type=jnp.float32
    ) * HEAD_DIM ** (-0.5)
    probs = jnp.where(allowed_mask(slots, length)[None], jnp.exp(scores - logsum), 0.0)
    probs_low = probs.astype(jnp.bfloat16)
    prob_grad = jnp.einsum("qhd,khd->hqk", out_grad, values, preferred_element_type=jnp.float32)
    value_grad = jnp.einsum("hqk,qhd->khd", probs_low, out_grad, preferred_element_type=jnp.float32)
    score_grad = (probs * (prob_grad - jnp.sum(probs * prob_grad, axis=-1, keepdims=True))).astype(
        jnp.bfloat16
    )
    query_grad = jnp.einsum(
        "hqk,khd->qhd", score_grad, keys, preferred_element_type=jnp.float32
    ) * HEAD_DIM ** (-0.5)
    key_grad = jnp.einsum(
        "hqk,qhd->khd", score_grad, query, preferred_element_type=jnp.float32
    ) * HEAD_DIM ** (-0.5)
    query_grad = rotate_back(query_grad, cosine, sine)
    key_grad = rotate_back(key_grad, cosine, sine)
    return jnp.stack([query_grad, key_grad, value_grad], axis=1).astype(jnp.bfloat16)


def dot(left, right):
    return jnp.dot(left, right, preferred_element_type=jnp.float32)


def dot_nt(left, right):
    return lax.dot_general(
        left, right, (((1,), (1,)), ((), ())), preferred_element_type=jnp.float32
    )


def dot_tn(left, right):
    return lax.dot_general(
        left, right, (((0,), (0,)), ((), ())), preferred_element_type=jnp.float32
    )


CHEAP = pl.CostEstimate(flops=1, transcendentals=0, bytes_accessed=1)
SCALE = HEAD_DIM ** (-0.5)


def work(flops):
    return pl.CostEstimate(flops=4 * flops, transcendentals=0, bytes_accessed=flops // 256)


def call(body, grid, in_specs, out_specs, out_shape, info, args, scratch=(), cost=CHEAP):
    return pl.pallas_call(
        body,
        grid_spec=pltpu.PrefetchScalarGridSpec(
            num_scalar_prefetch=1,
            grid=grid,
            in_specs=in_specs,
            out_specs=out_specs,
            scratch_shapes=list(scratch),
        ),
        out_shape=out_shape,
        cost_estimate=cost,
        compiler_params=pltpu.CompilerParams(vmem_limit_bytes=56 << 20),
    )(info, *args)


def low_shape(*shape):
    return jax.ShapeDtypeStruct(shape, jnp.bfloat16)


def full_shape(*shape):
    return jax.ShapeDtypeStruct(shape, jnp.float32)


def fixed(shape):
    return pl.BlockSpec(
        shape, lambda *index: (0,) * len(shape), pipeline_mode=pl.Buffered(buffer_count=1)
    )


def held(width, columns, at):
    return pl.BlockSpec(
        (width, columns), lambda i, info: (0, at), pipeline_mode=pl.Buffered(buffer_count=1)
    )


def held_pieces(width, columns, start, size):
    return [held(width, size, start // size + piece) for piece in range(columns // size)]


def row_stats(rows):
    mean = jnp.mean(rows, axis=1, keepdims=True)
    center = rows - mean
    scale = lax.rsqrt(jnp.mean(center * center, axis=1, keepdims=True) + 1e-05)
    return (mean, scale)


def two_norms(rows, vec_ref, outs):
    rows = rows.astype(jnp.float32)
    mean, scale = row_stats(rows)
    normed = (rows - mean) * scale
    first = normed * vec_ref[0:1] + vec_ref[1:2]
    second = normed * vec_ref[2:3] + vec_ref[3:4]
    outs[0][...] = first.astype(jnp.bfloat16)
    outs[1][...] = second.astype(jnp.bfloat16)
    outs[2][...] = mean
    outs[3][...] = scale
    if len(outs) > 4:
        outs[4][...] = first.T.astype(jnp.bfloat16)
        outs[5][...] = second.T.astype(jnp.bfloat16)


def norms_body(info, z_ref, vec_ref, *outs):
    two_norms(z_ref[...], vec_ref, outs)


def norm_specs(tall, slots, width, row, turn):
    specs = [pl.BlockSpec((tall, width), lambda i, info: (row(i, info), 0))] * 2
    specs += [pl.BlockSpec((tall, 1), lambda i, info: (row(i, info), 0))] * 2
    shapes = [low_shape(slots, width)] * 2 + [full_shape(slots, 1)] * 2
    if turn:
        specs += [pl.BlockSpec((width, tall), lambda i, info: (0, row(i, info)))] * 2
        shapes += [low_shape(width, slots)] * 2
    return (specs, shapes)


def with_turned(out, turn):
    out = list(out)
    return out if turn else out + [out[0].T, out[1].T]


def norms_call(rows, vectors, info):
    slots, width = rows.shape
    tall = min(slots, 256)
    turn = tall % 128 == 0
    specs, shapes = norm_specs(tall, slots, width, lambda i, info: i, turn)
    out = call(
        norms_body,
        (slots // tall,),
        [pl.BlockSpec((tall, width), lambda i, info: (i, 0)), fixed(vectors.shape)],
        specs,
        shapes,
        info,
        (rows, vectors),
    )
    return with_turned(out, turn)


def target_body(info, x_ref, out_ref, *turned_ref):
    tall = x_ref.shape[0]
    place = pl.program_id(0) * tall + lax.broadcasted_iota(jnp.int32, x_ref.shape, 0)
    value = jnp.where(place < info[0], x_ref[...].astype(jnp.float32), 0.0)
    out_ref[...] = value.astype(jnp.bfloat16)
    if turned_ref:
        turned_ref[0][...] = value.T.astype(jnp.bfloat16)


def target_call(cotangent, slots, info):
    width = cotangent.shape[1]
    tall = min(slots, 256)
    steps = slots // tall
    turn = tall % 128 == 0
    out = call(
        target_body,
        (steps,),
        [pl.BlockSpec((tall, width), lambda i, info: (info[1] * steps + i, 0))],
        [pl.BlockSpec((tall, width), lambda i, info: (i, 0))]
        + [pl.BlockSpec((width, tall), lambda i, info: (0, i))] * turn,
        [low_shape(slots, width)] + [low_shape(width, slots)] * turn,
        info,
        (cotangent,),
    )
    return (out[0], out[1]) if turn else (out[0], out[0].T)


def assemble_body(count, normed, info, *refs):
    step = pl.program_id(0)
    rest = refs[count:]
    for which in range(count):

        @pl.when(step == which)
        def _():
            block = refs[which][...]
            if normed:
                rest[1][...] = block
                two_norms(block, rest[0], rest[2:])
            else:
                rest[0][...] = block
                if len(rest) > 1:
                    rest[1][...] = block.astype(jnp.float32).T.astype(jnp.bfloat16)


def assemble(pieces, peers, bits, vectors=None):
    count = len(pieces)
    tall, width = pieces[0].shape
    slots = count * tall
    turn = tall % 128 == 0
    me = lax.axis_index("tensor")
    order = [2 * (me ^ r) + k for k in (0, 1) for r in relative_order(bits, k)]
    info = jnp.stack([jnp.asarray(item, jnp.int32) for item in order])

    def row(s, info):
        return info[s]

    in_specs, args = [fixed(item.shape) for item in pieces], list(pieces)
    specs = [pl.BlockSpec((tall, width), lambda s, info: (info[s], 0))]
    shapes = [low_shape(slots, width)]
    if vectors is not None:
        in_specs.append(fixed(vectors.shape))
        args.append(vectors)
        more, more_shapes = norm_specs(tall, slots, width, row, turn)
        specs, shapes = specs + more, shapes + more_shapes
    elif turn:
        specs.append(pl.BlockSpec((width, tall), lambda s, info: (0, info[s])))
        shapes.append(low_shape(width, slots))
    out = call(
        functools.partial(assemble_body, count, vectors is not None),
        (count,),
        in_specs,
        specs,
        shapes,
        info,
        args,
    )
    if vectors is not None:
        return (out[0], with_turned(out[1:], turn))
    return (out[0], out[1] if turn else out[0].T)


def turned(block, tables, sign):
    cosine, low, high = tables
    front = block[:, :128]
    front = front * cosine + sign * (
        pltpu.roll(front, 128 - ROT // 2, 1) * low + pltpu.roll(front, ROT // 2, 1) * high
    )
    return jnp.concatenate([front, block[:, 128:]], axis=1)


def turn_tables(slots):
    cosine, sine = (item[:, 0] for item in angle_tables(slots))
    rest = 128 - ROT
    zero = jnp.zeros_like(sine)
    pad = jnp.zeros((slots, rest), jnp.float32)
    return (
        jnp.concatenate([cosine, cosine, pad + 1.0], axis=1),
        jnp.concatenate([-sine, zero, pad], axis=1),
        jnp.concatenate([zero, sine, pad], axis=1),
    )


def allowed_block(start, rows, span, length):
    query = start + lax.broadcasted_iota(jnp.int32, (rows, span), 0)
    key = lax.broadcasted_iota(jnp.int32, (rows, span), 1)
    return (key <= query) & (key < length)


def heads_body(
    steps, info, x_ref, wq_ref, wk_ref, wv_ref, cos_ref, low_ref, high_ref, out_ref, qkv_ref, lse_ref, k_ref, v_ref
):
    step = pl.program_id(0)
    rows = x_ref.shape[0]
    tables = (cos_ref[...], low_ref[...], high_ref[...])
    rows_here = x_ref[...]
    query = turned(dot(rows_here, wq_ref[...]), tables, 1.0).astype(jnp.bfloat16)
    keys = turned(dot(rows_here, wk_ref[...]), tables, 1.0).astype(jnp.bfloat16)
    values = dot(rows_here, wv_ref[...]).astype(jnp.bfloat16)
    qkv_ref[:, :HEAD_DIM] = query
    qkv_ref[:, HEAD_DIM : 2 * HEAD_DIM] = keys
    qkv_ref[:, 2 * HEAD_DIM :] = values
    place = pl.multiple_of(step * rows, rows)
    k_ref[pl.ds(place, rows), :] = keys
    v_ref[pl.ds(place, rows), :] = values
    for now in range(steps):

        @pl.when(step == now)
        def _():
            span = (now + 1) * rows
            scores = dot_nt(query, k_ref[:span]) * SCALE
            scores = jnp.where(allowed_block(now * rows, rows, span, info[0]), scores, -jnp.inf)
            peak = jnp.max(scores, axis=1, keepdims=True)
            expo = jnp.exp(scores - peak)
            total = jnp.sum(expo, axis=1, keepdims=True)
            probs = (expo / total).astype(jnp.bfloat16)
            out_ref[...] = dot(probs, v_ref[:span]).astype(jnp.bfloat16)
            lse_ref[...] = peak + jnp.log(total)


def heads_call(first_in, inward, tables, info):
    slots, width = first_in.shape
    rows = min(slots, 256)
    steps = slots // rows
    columns = 3 * HEAD_DIM

    def tall(size):
        return pl.BlockSpec((rows, size), lambda i, info: (i, 0))

    out, qkv, lse = call(
        functools.partial(heads_body, steps),
        (steps,),
        [tall(width)] + [held(width, HEAD_DIM, part) for part in range(3)] + [tall(128)] * 3,
        [tall(HEAD_DIM), tall(columns), tall(1)],
        [low_shape(slots, HEAD_DIM), low_shape(slots, columns), full_shape(slots, 1)],
        info,
        (first_in, inward, inward, inward, *tables),
        [pltpu.VMEM((slots, HEAD_DIM), jnp.bfloat16)] * 2,
    )
    return (out, (qkv, lse))


def heads_back_body(
    steps, info, qkv_ref, lse_ref, grad_ref, cos_ref, low_ref, high_ref, out_ref, dk_ref, dv_ref
):
    step = pl.program_id(0)
    slots = qkv_ref.shape[0]
    rows = slots // steps

    def tables(start, size):
        return tuple(ref[start : start + size] for ref in (cos_ref, low_ref, high_ref))

    @pl.when(step == 0)
    def _():
        dk_ref[...] = jnp.zeros_like(dk_ref)
        dv_ref[...] = jnp.zeros_like(dv_ref)

    for now in range(steps):

        @pl.when(step == now)
        def _():
            span, start = (now + 1) * rows, now * rows
            query = qkv_ref[start:span, :HEAD_DIM]
            keys = qkv_ref[:span, HEAD_DIM : 2 * HEAD_DIM]
            values = qkv_ref[:span, 2 * HEAD_DIM :]
            grad = grad_ref[...]
            scores = dot_nt(query, keys) * SCALE
            allowed = allowed_block(start, rows, span, info[0])
            probs = jnp.where(allowed, jnp.exp(scores - lse_ref[...]), 0.0)
            prob_grad = dot_nt(grad, values)
            spread = jnp.sum(probs * prob_grad, axis=1, keepdims=True)
            score_grad = (probs * (prob_grad - spread)).astype(jnp.bfloat16)
            query_grad = dot(score_grad, keys) * SCALE
            out_ref[start:span, :HEAD_DIM] = turned(
                query_grad, tables(start, rows), -1.0
            ).astype(jnp.bfloat16)
            dv_ref[:span] += dot_tn(probs.astype(jnp.bfloat16), grad)
            dk_ref[:span] += dot_tn(score_grad, query)

    @pl.when(step == steps - 1)
    def _():
        out_ref[:, HEAD_DIM : 2 * HEAD_DIM] = turned(
            dk_ref[...] * SCALE, tables(0, slots), -1.0
        ).astype(jnp.bfloat16)
        out_ref[:, 2 * HEAD_DIM :] = dv_ref[...].astype(jnp.bfloat16)


def heads_back_call(saved, out_grad, tables, info, cost=CHEAP):
    qkv, lse = saved
    slots, columns = qkv.shape
    rows = min(slots, 256)
    steps = slots // rows
    return call(
        functools.partial(heads_back_body, steps),
        (steps,),
        [
            fixed(qkv.shape),
            pl.BlockSpec((rows, 1), lambda i, info: (i, 0)),
            pl.BlockSpec((rows, HEAD_DIM), lambda i, info: (i, 0)),
        ]
        + [fixed((slots, 128))] * 3,
        pl.BlockSpec((slots, columns), lambda i, info: (0, 0)),
        low_shape(slots, columns),
        info,
        (qkv, lse, out_grad, *tables),
        [pltpu.VMEM((slots, HEAD_DIM), jnp.float32)] * 2,
        cost,
    )


def units_body(pieces, info, x_ref, *refs):
    weights, (offset_ref, act_ref, slope_ref) = refs[:pieces], refs[pieces:]
    size = weights[0].shape[1]
    for piece in range(pieces):
        here = slice(piece * size, (piece + 1) * size)
        hidden = dot(x_ref[...], weights[piece][...]) + offset_ref[:, here]
        cdf = 0.5 * (1.0 + lax.erf(hidden * 0.7071067811865476))
        act_ref[:, here] = (hidden * cdf).astype(jnp.bfloat16)
        bell = jnp.exp(-0.5 * hidden * hidden) * 0.3989422804014327
        slope_ref[:, here] = (cdf + hidden * bell).astype(jnp.bfloat16)


def units_call(second_in, expand, start, offsets, unit, info):
    slots, width = second_in.shape
    columns = offsets.shape[0]
    tall = min(slots, 256)
    spec = pl.BlockSpec((tall, columns), lambda i, info: (i, 0))
    weights = held_pieces(width, columns, start * unit, unit)
    return call(
        functools.partial(units_body, len(weights)),
        (slots // tall,),
        [pl.BlockSpec((tall, width), lambda i, info: (i, 0))] + weights + [fixed((1, columns))],
        [spec, spec],
        [low_shape(slots, columns)] * 2,
        info,
        (second_in, *[expand] * len(weights), offsets[None]),
    )


def halving_blocks(half, tall):
    return ([tall] * half + [half * tall]) * 2


def place_rows(info, value_ref, outs, half, tall):
    for which in range(4):
        stream, kept = which // 2, which % 2
        for place in range(half):
            start = (2 * info[which * half + place] + stream) * tall
            rows = value_ref[pl.ds(pl.multiple_of(start, tall), tall)]
            if kept:
                outs[stream * (half + 1) + half][place * tall : (place + 1) * tall] = rows
            else:
                outs[stream * (half + 1) + place][...] = rows


def partial_body(half, tall, parts, info, *refs):
    lefts, rights = [refs[k * parts : (k + 1) * parts] for k in range(4)], refs[4 * parts :][:4]
    outs, value_ref = refs[4 * parts + 4 : -1], refs[-1]
    rows = lefts[0][0].shape[0]
    for part in range(parts):
        value = None
        for left, right in zip(lefts, rights):
            term = dot_nt(left[part][...], right[...])
            value = term if value is None else value + term
        value_ref[part * rows : (part + 1) * rows] = value.astype(jnp.bfloat16)
    if half:
        place_rows(info, value_ref, outs, half, tall)
    else:
        outs[0][...] = value_ref[...]


def partial_call(heads, acts, outward, contract, outward_at, contract_at, places, cost=CHEAP):
    slots, unit = heads[0].shape
    wide = acts[0].shape[1]
    width = outward[0].shape[0]
    block = min(width, 512)
    parts = max(slots // 256, 1)
    rows = slots // parts
    half = len(places) // 4
    tall = slots // (4 * half) if half else 0
    heights = halving_blocks(half, tall) if half else [slots]
    info = jnp.stack([jnp.asarray(item, jnp.int32) for item in (places or [0])])

    def row_blocks(columns):
        return [
            pl.BlockSpec(
                (rows, columns),
                lambda j, info, part=part: (part, 0),
                pipeline_mode=pl.Buffered(buffer_count=1),
            )
            for part in range(parts)
        ]

    return call(
        functools.partial(partial_body, half, tall, parts),
        (width // block,),
        row_blocks(unit) * 2
        + row_blocks(wide) * 2
        + [pl.BlockSpec((block, unit), lambda j, info: (j, outward_at))] * 2
        + [pl.BlockSpec((block, wide), lambda j, info: (j, contract_at * unit // wide))] * 2,
        [pl.BlockSpec((height, block), lambda j, info: (0, j)) for height in heights],
        [low_shape(height, width) for height in heights],
        info,
        [item for item in (*heads, *acts) for part in range(parts)] + [*outward, *contract],
        [pltpu.VMEM((slots, block), jnp.bfloat16)],
        cost,
    )


def grads_body(plan, split, info, *refs):
    lefts = refs[: max(plan) + 1]
    rights = refs[len(lefts) : len(lefts) + len(plan)]
    rest = refs[len(lefts) + len(plan) :]
    got, outs = ((), rest) if split else (rest[:-1], rest[-1:])
    size = rights[0].shape[1]
    for place, right in enumerate(rights):
        value = dot(lefts[plan[place]][...], right[...])
        if split:
            outs[place][...] = value.astype(jnp.bfloat16)
        else:
            value = value + got[place][...].astype(jnp.float32)
            outs[0][:, place * size : (place + 1) * size] = value.astype(jnp.bfloat16)


def grads_call(lefts, rights, size, info, got=None, cost=CHEAP):
    width, slots = lefts[0].shape
    columns = sum(item.shape[1] for item in rights)
    block = min(width, 256)
    split = got is None
    spec = pl.BlockSpec((block, columns), lambda j, info: (j, 0))
    pieces = columns // size
    piece_specs = [pl.BlockSpec((block, size), lambda j, info: (j, 0))] * pieces
    plan, specs, args = [], [], []
    for which, right in enumerate(rights):
        for piece in held_pieces(slots, right.shape[1], 0, size):
            plan.append(which)
            specs.append(piece)
            args.append(right)
    return call(
        functools.partial(grads_body, plan, split),
        (width // block,),
        [pl.BlockSpec((block, slots), lambda j, info: (j, 0))] * len(lefts)
        + specs
        + ([] if split else piece_specs),
        piece_specs if split else spec,
        [low_shape(width, size)] * pieces if split else low_shape(width, columns),
        info,
        (*lefts, *args, *(got or ())),
        cost=cost,
    )


def lifted_body(pieces, info, g_ref, outward_ref, *refs):
    weights, (slope_ref, out_ref, hidden_ref, sum_ref) = refs[:pieces], refs[pieces:]
    size = weights[0].shape[1]

    @pl.when(pl.program_id(0) == 0)
    def _():
        sum_ref[...] = jnp.zeros_like(sum_ref)

    for piece in range(pieces):
        here = slice(piece * size, (piece + 1) * size)
        value = dot(g_ref[...], weights[piece][...]) * slope_ref[:, here].astype(jnp.float32)
        value = value.astype(jnp.bfloat16)
        hidden_ref[:, here] = value
        sum_ref[:, here] += jnp.sum(value.astype(jnp.float32), axis=0, keepdims=True)
    out_ref[...] = dot(g_ref[...], outward_ref[...]).astype(jnp.bfloat16)


def lifted_call(grad, outward, contract, outward_at, contract_at, slope, unit, info, cost=CHEAP):
    slots, width = grad.shape
    columns = slope.shape[1]
    tall = min(slots, 256)
    weights = held_pieces(width, columns, contract_at * unit, unit)

    def rows(size):
        return pl.BlockSpec((tall, size), lambda i, info: (i, 0))

    return call(
        functools.partial(lifted_body, len(weights)),
        (slots // tall,),
        [rows(width), held(width, unit, outward_at)] + weights + [rows(columns)],
        [rows(unit), rows(columns), pl.BlockSpec((1, columns), lambda i, info: (0, 0))],
        [low_shape(slots, unit), low_shape(slots, columns), full_shape(1, columns)],
        info,
        (grad, outward, *[contract] * len(weights), slope),
        cost=cost,
    )


def back_body(half, tall, info, *refs):
    z_ref, mean_ref, scale_ref, vec_ref = refs[:4]
    mixed, hidden, inward, expand = refs[4:6], refs[6:8], refs[8:10], refs[10:12]
    outs, sums_ref, hat_ref, total_ref, along_ref = refs[12:-4], *refs[-4:]
    part, block = pl.program_id(0), pl.program_id(1)
    size = inward[0].shape[0]
    width = z_ref.shape[1]
    columns = pl.ds(pl.multiple_of(block * size, size), size)
    mean, scale = mean_ref[...], scale_ref[...]
    first = dot_nt(mixed[0][...], inward[0][...]) + dot_nt(mixed[1][...], inward[1][...])
    second = dot_nt(hidden[0][...], expand[0][...]) + dot_nt(hidden[1][...], expand[1][...])
    normed = (z_ref[:, columns].astype(jnp.float32) - mean) * scale
    sums = [
        jnp.sum(value, axis=0, keepdims=True)
        for value in (first * normed, first, second * normed, second)
    ]

    @pl.when(part == 0)
    def _():
        for row in range(4):
            sums_ref[row : row + 1, columns] = sums[row]

    @pl.when(part > 0)
    def _():
        for row in range(4):
            sums_ref[row : row + 1, columns] += sums[row]

    hat = first * vec_ref[0:1] + second * vec_ref[2:3]
    hat_ref[:, columns] = hat
    total = jnp.sum(hat, axis=1, keepdims=True)
    along = jnp.sum(hat * normed, axis=1, keepdims=True)

    @pl.when(block == 0)
    def _():
        total_ref[...] = total
        along_ref[...] = along

    @pl.when(block > 0)
    def _():
        total_ref[...] += total
        along_ref[...] += along

    @pl.when(block == pl.num_programs(1) - 1)
    def _():
        rows = hat_ref.shape[0]
        step = tall if half else min(rows, 256)
        for start in range(0, rows, step):
            here = slice(start, start + step)
            normed_here = (z_ref[here].astype(jnp.float32) - mean_ref[here]) * scale_ref[here]
            result = scale_ref[here] * (
                hat_ref[here]
                - total_ref[here] / width
                - normed_here * (along_ref[here] / width)
            )
            result = result.astype(jnp.bfloat16)
            if not half:
                outs[0][pl.ds(part * rows + start, step)] = result
                continue
            stream = start // tall % 2
            peer = part * (rows // (2 * tall)) + start // (2 * tall)
            at = 2 * (2 * peer + stream)
            own_outs = outs[stream * (half + 1) : (stream + 1) * (half + 1)]

            @pl.when(info[at] == 0)
            def _():
                own_outs[half][pl.ds(pl.multiple_of(info[at + 1] * tall, tall), tall)] = result

            for place in range(half):

                @pl.when((info[at] == 1) & (info[at + 1] == place))
                def _():
                    own_outs[place][...] = result


def back_call(rows, stats, vectors, mixed_grads, hidden_grads, inward, expand, expand_at, me, peers, bits):
    slots, width = rows.shape
    parts = 2 if bits else 1
    rows_each = slots // parts
    block = min(width, 512)
    half = peers // 2 if bits else 0
    tall = slots // (2 * peers) if bits else 0
    heads_columns, wide = mixed_grads[0].shape[1], hidden_grads[0].shape[1]
    table = []
    for peer in range(peers if bits else 0):
        for stream in (0, 1):
            bit = step_bits(bits, stream)[0]
            own = (me >> bit) & 1
            place = (peer & ((1 << bit) - 1)) | ((peer >> (bit + 1)) << bit)
            table.append(jnp.asarray(((peer >> bit) & 1) != own, jnp.int32))
            table.append(jnp.asarray(place, jnp.int32))
    info = jnp.stack(table or [jnp.asarray(0, jnp.int32)])
    heights = halving_blocks(half, tall) if half else [slots]

    def spec(columns):
        return pl.BlockSpec((rows_each, columns), lambda i, j, info: (i, 0))

    def weights(columns, at):
        return pl.BlockSpec((block, columns), lambda i, j, info: (j, at))

    def whole(*shape):
        return pl.BlockSpec(shape, lambda i, j, info: (0, 0))

    out = call(
        functools.partial(back_body, half, tall),
        (parts, width // block),
        [spec(width), spec(1), spec(1)]
        + [pl.BlockSpec((vectors.shape[0], block), lambda i, j, info: (0, j))]
        + [spec(item.shape[1]) for item in (*mixed_grads, *hidden_grads)]
        + [weights(heads_columns, 0)] * 2
        + [weights(wide, expand_at * heads_columns // (3 * wide))] * 2,
        [whole(height, width) for height in heights] + [whole(4, width)],
        [low_shape(height, width) for height in heights] + [full_shape(4, width)],
        info,
        (rows, *stats, vectors, *mixed_grads, *hidden_grads, *inward, *expand),
        [pltpu.VMEM((rows_each, width), jnp.float32)]
        + [pltpu.VMEM((rows_each, 1), jnp.float32)] * 2,
    )
    return out[:-1], out[-1]


def share_of(total):
    return lax.psum_scatter(total, "dp", scatter_dimension=0, tiled=True)


def adam_kernel(rate, decay, arrange, info, *refs):
    grads, (master, first, second), outs = refs[:4], refs[4:7], refs[7:]

    def run(half, region, turn):
        grad = jnp.where(info[0] == 0, grads[half][...], grads[2 + half][...]).astype(jnp.float32)
        grad = grad.T if turn else grad
        new = adam_update(master[region], grad, first[region], second[region], rate, decay)
        for out, value in zip(outs, new):
            out[region] = value

    arrange(run)


def adam_columns(index, grads, arrays, depth, starts, core):
    parts, _, columns = arrays[0].shape
    half = columns // 2
    tall = depth // 2

    def arrange(run):
        for which in (0, 1):
            run(which, (0, slice(None), pl.ds(which * half, half)), False)

    def grad_spec(start):
        return pl.BlockSpec((tall, half), lambda i, j, info: (j, start + i))

    block_spec = pl.BlockSpec((1, tall, columns), lambda i, j, info: (i, j, 0))
    return call(
        functools.partial(adam_kernel, RATES[index], DECAYS[index], arrange),
        (parts, depth // tall),
        [grad_spec(starts[which // 2]) for which in range(4)] + [block_spec] * 3,
        [block_spec] * 3,
        [jax.ShapeDtypeStruct(arrays[0].shape, jnp.float32)] * 3,
        core,
        (*grads, *arrays),
    )


def adam_rows(index, grads, arrays, starts, block, core, cost=CHEAP):
    units, depth = arrays[0].shape
    each = units // 2 // block

    def arrange(run):
        for half in (0, 1):

            @pl.when(pl.program_id(0) == half)
            def _():
                run(half, Ellipsis, True)

    def grad_spec(half, start):
        def place(h, j, info):
            return (0, start + jnp.where(h == half, j, (each - 1) * (1 - half)))

        return pl.BlockSpec((depth, block), place)

    block_spec = pl.BlockSpec((block, depth), lambda h, j, info: (h * each + j, 0))
    return call(
        functools.partial(adam_kernel, RATES[index], DECAYS[index], arrange),
        (2, each),
        [grad_spec(which % 2, starts[which // 2]) for which in range(4)] + [block_spec] * 3,
        [block_spec] * 3,
        [jax.ShapeDtypeStruct(arrays[0].shape, jnp.float32)] * 3,
        core,
        (*grads, *arrays),
        cost=cost,
    )


def adam_update(master, grad, first, second, rate, decay):
    new_first = 0.9 * first + 0.1 * grad
    new_second = 0.95 * second + 0.05 * grad * grad
    corrected = new_first / (1.0 - 0.9**STEP)
    spread = jnp.sqrt(new_second / (1.0 - 0.95**STEP))
    return (master - rate * (corrected / (spread + 1e-08) + decay * master), new_first, new_second)


def local(
    tokens,
    cotangent,
    lengths,
    inward,
    outward,
    expand,
    contract,
    vectors,
    offsets,
    inward_first,
    inward_second,
    outward_first,
    outward_second,
    expand_first,
    expand_second,
    contract_first,
    contract_second,
    vectors_first,
    vectors_second,
    offsets_first,
    offsets_second,
):
    core = lax.axis_index("pipe")
    peers = lax.axis_size("tensor")
    groups = lax.axis_size("dp")
    place = lax.axis_index("tensor")
    depth = inward.shape[1]
    heads_local = inward.shape[3] // HEAD_DIM
    lone = heads_local == 2
    head_share = inward.shape[3] // 2
    unit_share = expand.shape[2] // 2
    batches = lengths.shape[0]
    width = tokens.shape[1]
    slots = tokens.shape[0] // batches
    row_share = slots // peers

    bits = halving(peers, slots)

    def packed(shard):
        mine, theirs = (item.astype(jnp.bfloat16).reshape(depth, -1) for item in halves(shard, core))
        got = swap(theirs)
        return (jnp.where(core == 0, mine, got), jnp.where(core == 0, got, mine))

    packs = [packed(item) for item in (inward[0], expand[0], outward[0].T, contract[0].T)]
    count = unit_share // head_share

    small = jnp.concatenate([vectors.reshape(-1), offsets.reshape(-1)]).astype(jnp.bfloat16)
    small = lax.all_gather(small, ("pipe", "dp"), axis=0, tiled=False).reshape(2, groups, -1)
    small = small.astype(jnp.float32)
    vector_values = [
        small[layer, :, : 5 * depth].reshape(groups, 5, depth).transpose(1, 0, 2).reshape(5, width)
        for layer in (0, 1)
    ]
    offset_pairs = [halves(small[layer, :, 5 * depth :].reshape(-1), core) for layer in (0, 1)]

    tables = angle_tables(slots)
    turns = turn_tables(slots)
    length = lax.dynamic_index_in_dim(lengths, core, 0, keepdims=False)
    info = length[None]
    own = lax.dynamic_slice_in_dim(tokens, core * slots, slots, 0)
    target, target_turned = target_call(cotangent, slots, jnp.stack([length, core]))
    places = scatter_places(place, peers, bits) if bits else []

    def whole_of(shard):
        return lax.all_gather(shard, "dp", axis=0, tiled=True)

    def pair_of(whole, *earlier):
        whole = after(whole, *earlier)
        return (whole, swap(whole))

    def block_of(array):
        block = lax.dynamic_slice_in_dim(array, place * row_share, row_share, 0)
        return block.astype(jnp.float32)

    def summed(pieces):
        if bits:
            return jnp.concatenate(sum_scatter(pieces, peers, bits), axis=0)
        return lax.psum_scatter(pieces[0], "tensor", scatter_dimension=0, tiled=True).astype(
            jnp.float32
        )

    def spread(block):
        tall = row_share // 2
        return rows_pieces((block[:tall], block[tall:]), peers, bits)

    def heads_of(first_in, inward_pair):
        if lone:
            done = [heads_call(first_in, item, turns, info) for item in inward_pair]
            return ([item[0] for item in done], [item[1] for item in done])
        mixed = [dot(first_in, w[:, : 3 * head_share]).reshape(slots, 3, -1) for w in inward_pair]
        mixed = ordered(mixed[0], mixed[1], core).reshape(slots, 3, -1, HEAD_DIM)
        out, saved = attend(mixed, length, tables)
        return (list(halves(out, core)), saved)

    def heads_back(which, out_grads, saved, cost=CHEAP):
        if lone:
            return heads_back_call(saved[which], out_grads[which], turns, info, cost)
        grad = ordered(out_grads[0], out_grads[1], core)
        mixed_grad = attend_back(grad, saved, length, tables).reshape(slots, 3, -1)
        return halves(mixed_grad, core)[which].reshape(slots, -1)

    def units_of(second_in, expand_pair, start, layer):
        done = [
            units_call(
                second_in, expand_pair[which], start, offset_pairs[layer][which], head_share, info
            )
            for which in (0, 1)
        ]
        return ([item[0] for item in done], [item[1] for item in done])

    def layer_output(layer, outward_pair, contract_pair, heads, acts, cost=CHEAP):
        pieces = partial_call(
            heads,
            acts,
            outward_pair,
            contract_pair,
            outward_at[layer],
            contract_at[layer],
            places,
            cost,
        )
        block = summed(pieces) + block_of(inputs[layer]) + vector_values[layer][4]
        return block.astype(jnp.bfloat16)

    outward_at, contract_at, expand_at = (2 * count, 3), (0, 0), (count, 4)
    shards = [packs[0][0], jnp.concatenate([packs[3][0], packs[1][0], packs[2][0]], axis=1)]
    shards.append(jnp.concatenate([after(packs[0][1], shards[1]), packs[2][1], packs[1][1]], axis=1))
    shards.append(after(packs[3][1], shards[2]))
    shards[1] = after(shards[1], shards[0])
    wholes = [whole_of(item) for item in shards]
    inputs = [own]
    normed = norms_call(own, vector_values[0], info)
    first_in, second_in = normed[:2]
    inward_pairs = [pair_of(wholes[0], first_in, second_in, target_turned)]
    heads, saved = heads_of(first_in, inward_pairs[0])
    rest_pair = pair_of(wholes[1], *heads)
    acts, slopes = units_of(second_in, rest_pair, expand_at[0], 0)
    kept = [(normed, heads, saved, acts, slopes)]
    outward_pairs, contract_pairs, expand_pairs = [rest_pair], [rest_pair], [rest_pair]
    results = [layer_output(0, rest_pair, rest_pair, heads, acts)]
    if bits:
        rows, normed = assemble(
            spread(results[0]), peers, bits, vector_values[1]
        )
        inputs.append(rows)
    else:
        inputs.append(lax.all_gather(results[0], "tensor", axis=0, tiled=True))
        normed = norms_call(inputs[1], vector_values[1], info)
    first_in, second_in = normed[:2]
    rest_pair = pair_of(wholes[2], first_in, second_in)
    for store in (inward_pairs, outward_pairs, expand_pairs):
        store.append(rest_pair)
    acts, slopes = units_of(second_in, rest_pair, expand_at[1], 1)

    grad_low, grad_turned = target, target_turned
    shares, row_grads, vector_grads, offset_grads = [None] * 2, [None] * 2, [None] * 2, [None] * 2
    for layer in (1, 0):
        if layer == 0:
            normed, heads, saved, acts, slopes = kept[0]
        dense = 2 * slots * width * unit_share
        theirs = grads_call([grad_turned], [acts[1]], head_share, info)
        if layer == 1:
            mine = grads_call([grad_turned], [acts[0]], head_share, info)
            heads, saved = heads_of(after(first_in, *theirs, *mine), rest_pair)
            theirs = [after(after(item, *mine, *heads), wholes[3]) for item in theirs]
            contract_pairs.append(pair_of(wholes[3], *theirs))
        got = [swap(item) for item in theirs]

        def lift(which, grad, cost=CHEAP):
            return lifted_call(
                grad,
                outward_pairs[layer][which],
                contract_pairs[layer][which],
                outward_at[layer],
                contract_at[layer],
                slopes[which],
                head_share,
                info,
                cost,
            )

        def total_of(lefts, theirs, mine, cost=CHEAP, between=None):
            got = [swap(item) for item in grads_call(lefts, theirs, head_share, info, cost=cost)]
            if between is not None:
                mine = [after(mine[0], between), *mine[1:]]
            return grads_call(lefts, mine, head_share, info, got, cost)

        lifted = [lift(0, after(grad_low, *theirs), work(dense))]
        if layer == 1:
            mine = [after(item, lifted[0][1]) for item in mine]
            contract_total = jnp.concatenate(
                [
                    (own.astype(jnp.float32) + item.astype(jnp.float32)).astype(jnp.bfloat16)
                    for own, item in zip(mine, got)
                ],
                axis=1,
            )
        else:
            contract_total = grads_call(
                [grad_turned], [after(acts[0], lifted[0][1])], head_share, info, got
            )
        contract_share = share_of(contract_total)
        lifted.append(lift(1, after(grad_low, contract_total)))
        out_grads = [item[0] for item in lifted]
        hidden_grads = [item[1] for item in lifted]
        offset_grads[layer] = [item[2][0] for item in lifted]
        first_turned, second_turned = normed[4:]
        lefts = [first_turned, grad_turned]
        small_work = work(dense // 2)
        if layer == 1:
            mixed_first = heads_back(0, out_grads, saved, small_work)
            expand_total = total_of(
                [second_turned], [hidden_grads[1]], [hidden_grads[0]], between=mixed_first
            )
            expand_share = share_of(expand_total)
            out_grads = [after(item, expand_total) for item in out_grads]
            mixed_grads = [mixed_first, heads_back(1, out_grads, saved)]
            ahead = [contract_share, *mixed_grads]
        else:
            mixed_last = heads_back(1, out_grads, saved)
            mixed_first = heads_back(0, out_grads, saved, small_work)
            mixed_grads = [mixed_first, mixed_last]
            hidden_here = [after(item, *shares[1]) for item in hidden_grads]
            other_total = total_of(
                [second_turned, first_turned],
                [hidden_here[1], mixed_last],
                [hidden_here[0], mixed_first],
                between=mixed_first,
            )
            ahead = [other_total]
        pieces, norm_part = back_call(
            after(inputs[layer], *ahead),
            normed[2:4],
            vector_values[layer],
            mixed_grads,
            hidden_grads,
            inward_pairs[layer],
            expand_pairs[layer],
            expand_at[layer],
            place,
            peers,
            bits,
        )
        rights = [[mixed_grads[which], heads[which]] for which in (1, 0)]
        if layer == 1:
            lefts[0] = after(lefts[0], *pieces)
            shares[1] = (share_of(total_of(lefts, *rights, work(dense))), expand_share, contract_share)
        else:
            outward_total = total_of(
                [after(grad_turned, other_total)], [rights[0][1]], [rights[1][1]]
            )
            pairs = [
                [after(item, outward_total) for item in pair]
                for pair in (outward_pairs[1], contract_pairs[1])
            ]
            pieces = [after(item, contract_share) for item in pieces]
            shares[0] = (share_of(other_total), share_of(outward_total), contract_share)
            results.append(layer_output(1, *pairs, *last))
        upstream = block_of(grad_low)
        vector_grads[layer] = jnp.concatenate(
            [norm_part, jnp.sum(upstream, axis=0)[None]], axis=0
        )
        row_grads[layer] = upstream + summed(pieces)
        if layer == 1:
            block = row_grads[layer].astype(jnp.bfloat16)
            if bits:
                grad_low, grad_turned = assemble(
                    [after(item, expand_share) for item in spread(block)], peers, bits
                )
            else:
                grad_low = lax.all_gather(block, "tensor", axis=0, tiled=True)
                grad_turned = grad_low.T
            last = (heads, acts)

    activations = jnp.where(core == 0, results[0], results[1])
    got = swap(jnp.where(core == 0, results[1], results[0]))
    activations = jnp.where(
        core == 0, jnp.stack([activations, got]), jnp.stack([got, activations])
    )[None]
    gradients = jnp.where(core == 0, row_grads[0], row_grads[1])
    got = swap(jnp.where(core == 0, row_grads[1], row_grads[0]))
    gradients = jnp.where(core == 0, jnp.stack([gradients, got]), jnp.stack([got, gradients]))[None]

    def to_owner(first, second):
        return (first, swap(first), swap(second), second)

    vector_sum = added(jnp.stack(vector_grads), "tensor")
    offset_sum = jnp.stack([ordered(item[0], item[1], core) for item in offset_grads])
    small_sum = jnp.concatenate([vector_sum.reshape(2, -1), offset_sum], axis=1)
    small_sum = added(added(small_sum, "pipe"), "dp")
    small_sum = lax.dynamic_index_in_dim(small_sum, core, 0, keepdims=False)
    where = lax.axis_index("dp")
    vector_grad = lax.dynamic_slice_in_dim(
        small_sum[: 5 * width].reshape(5, width), where * depth, depth, 1
    )
    offset_size = offsets.shape[1]
    offset_grad = lax.dynamic_slice_in_dim(
        small_sum, 5 * width + where * offset_size, offset_size, 0
    )

    def viewed(*arrays):
        return [item[0] for item in arrays]

    def parts_first(*arrays):
        return [item[0].transpose(1, 0, 2) for item in arrays]

    which = core[None]
    expand_1, heads_1 = swap(shares[1][1]), swap(shares[1][0])
    contract_out = adam_rows(
        3,
        to_owner(shares[0][2], shares[1][2]),
        viewed(contract, contract_first, contract_second),
        (0, 0),
        head_share,
        which,
    )
    vectors_out = adam_update(
        vectors, vector_grad[None], vectors_first, vectors_second, RATES[4], DECAYS[4]
    )
    offsets_out = adam_update(
        offsets, offset_grad[None], offsets_first, offsets_second, RATES[5], DECAYS[5]
    )
    other_share = after(shares[0][0], contract_out[0])
    other_0 = swap(other_share)
    expand_out = adam_columns(
        2,
        (other_share, other_0, expand_1, shares[1][1]),
        [expand, expand_first, expand_second],
        depth,
        (0, 0),
        which,
    )
    inward_out = adam_columns(
        0,
        (other_share, other_0, heads_1, shares[1][0]),
        parts_first(inward, inward_first, inward_second),
        depth,
        (count, 0),
        which,
    )
    outward_share = after(shares[0][1], expand_out[0], inward_out[0])
    outward_out = adam_rows(
        1,
        (outward_share, swap(outward_share), heads_1, shares[1][0]),
        viewed(outward, outward_first, outward_second),
        (0, 3),
        head_share,
        which,
    )
    outputs = [activations, gradients]
    outputs.extend([item.transpose(1, 0, 2)[None] for item in inward_out])
    outputs.extend([item[None] for item in outward_out])
    outputs.extend(expand_out)
    outputs.extend([item[None] for item in contract_out])
    outputs.extend(vectors_out)
    outputs.extend(offsets_out)
    return tuple(outputs)


def solution(mesh):
    return jax.shard_map(
        local,
        mesh=mesh,
        in_specs=(
            P("dp", None),
            P("dp", None),
            P("dp"),
            P("pipe", "dp", None, "tensor"),
            P("pipe", "tensor", "dp"),
            P("pipe", "dp", "tensor"),
            P("pipe", "tensor", "dp"),
            P("pipe", None, "dp"),
            P("pipe", ("tensor", "dp")),
            P("pipe", "dp", None, "tensor"),
            P("pipe", "dp", None, "tensor"),
            P("pipe", "tensor", "dp"),
            P("pipe", "tensor", "dp"),
            P("pipe", "dp", "tensor"),
            P("pipe", "dp", "tensor"),
            P("pipe", "tensor", "dp"),
            P("pipe", "tensor", "dp"),
            P("pipe", None, "dp"),
            P("pipe", None, "dp"),
            P("pipe", ("tensor", "dp")),
            P("pipe", ("tensor", "dp")),
        ),
        out_specs=(
            P("pipe", "dp", "tensor", None),
            P("pipe", "dp", "tensor", None),
            P("pipe", "dp", None, "tensor"),
            P("pipe", "dp", None, "tensor"),
            P("pipe", "dp", None, "tensor"),
            P("pipe", "tensor", "dp"),
            P("pipe", "tensor", "dp"),
            P("pipe", "tensor", "dp"),
            P("pipe", "dp", "tensor"),
            P("pipe", "dp", "tensor"),
            P("pipe", "dp", "tensor"),
            P("pipe", "tensor", "dp"),
            P("pipe", "tensor", "dp"),
            P("pipe", "tensor", "dp"),
            P("pipe", None, "dp"),
            P("pipe", None, "dp"),
            P("pipe", None, "dp"),
            P("pipe", ("tensor", "dp")),
            P("pipe", ("tensor", "dp")),
            P("pipe", ("tensor", "dp")),
        ),
        check_vma=False,
    )
```

```python
import functools

import jax
import jax.numpy as jnp
from jax import lax
from jax.experimental import pallas as pl
from jax.experimental.pallas import tpu as pltpu
from jax.sharding import PartitionSpec as P

HEAD_DIM = 256
ROT = 64
STEP = 10


RATES = (0.03, 0.2, 0.03, 0.015, 0.3, 0.3)
DECAYS = (0.01, 0.01, 0.01, 0.01, 0.0, 0.0)


def angle_tables(slots):
    half = ROT // 2
    positions = jnp.arange(slots).astype(jnp.float32)
    frequency = 10000.0 ** (-(2.0 * jnp.arange(half).astype(jnp.float32)) / ROT)
    angles = positions[:, None] * frequency[None, :]
    return (jnp.cos(angles)[:, None, :], jnp.sin(angles)[:, None, :])


def rotate(block, cosine, sine):
    half = cosine.shape[-1]
    first = block[..., :half]
    second = block[..., half : 2 * half]
    return jnp.concatenate(
        [first * cosine - second * sine, second * cosine + first * sine, block[..., 2 * half :]],
        axis=-1,
    )


def rotate_back(grad, cosine, sine):
    half = cosine.shape[-1]
    first = grad[..., :half]
    second = grad[..., half : 2 * half]
    return jnp.concatenate(
        [first * cosine + second * sine, second * cosine - first * sine, grad[..., 2 * half :]],
        axis=-1,
    )


def norm_parts(rows, gain, shift):
    center = rows - jnp.mean(rows, axis=1, keepdims=True)
    scale = lax.rsqrt(jnp.mean(center * center, axis=1, keepdims=True) + 1e-05)
    normed = center * scale
    return (normed * gain + shift, normed, scale)


def norm_back(back, rows, gain):
    unused, normed, scale = norm_parts(rows, gain, 0.0)
    hat = back * gain
    row_grad = scale * (
        hat
        - jnp.mean(hat, axis=1, keepdims=True)
        - normed * jnp.mean(hat * normed, axis=1, keepdims=True)
    )
    return (row_grad, jnp.sum(back * normed, axis=0), jnp.sum(back, axis=0))


def gelu_slope(hidden):
    return (
        0.5 * (1.0 + lax.erf(hidden * 0.7071067811865476))
        + hidden * jnp.exp(-0.5 * hidden * hidden) * 0.3989422804014327
    )


def allowed_mask(slots, length):
    places = jnp.arange(slots)
    return (places[None, :] <= places[:, None]) & (places[None, :] < length)


def after(array, *earlier):
    return lax.optimization_barrier((array, *earlier))[0]


def added(array, axis):
    peers = lax.axis_size(axis)
    bits = peers.bit_length() - 1
    if peers != 1 << bits:
        return lax.psum(array, axis)
    for bit in range(bits):
        array = array + lax.ppermute(array, axis, [(i, i ^ (1 << bit)) for i in range(peers)])
    return array


def swap(array):
    return lax.ppermute(array, "pipe", [(0, 1), (1, 0)])


def halves(array, core):
    size = array.shape[-1] // 2
    axis = array.ndim - 1
    mine = lax.dynamic_slice_in_dim(array, core * size, size, axis)
    theirs = lax.dynamic_slice_in_dim(array, (1 - core) * size, size, axis)
    return (mine, theirs)


def ordered(mine, theirs, core):
    return jnp.where(
        core == 0,
        jnp.concatenate([mine, theirs], axis=-1),
        jnp.concatenate([theirs, mine], axis=-1),
    )


def flipped(array, peers, bit):
    return lax.ppermute(array, "tensor", [(i, i ^ (1 << bit)) for i in range(peers)])


def halving(peers, rows):
    bits = peers.bit_length() - 1
    return bits if peers == 1 << bits and bits > 0 and rows % (16 * peers) == 0 else 0


def step_bits(bits, stream):
    return [step if stream == 0 else bits - 1 - step for step in range(bits)]


def relative_order(bits, stream):
    order = [0]
    for bit in reversed(step_bits(bits, stream)):
        order = order + [other ^ (1 << bit) for other in order]
    return order


def scatter_places(me, peers, bits):
    half = peers // 2
    places = []
    for stream in (0, 1):
        bit = step_bits(bits, stream)[0]
        own = (me >> bit) & 1
        for value in (1 - own, own):
            for place in range(half):
                low = place & ((1 << bit) - 1)
                high = (place >> bit) << (bit + 1)
                places.append(high | (value << bit) | low)
    return places


def sum_scatter(pieces, peers, bits, beside=()):
    me = lax.axis_index("tensor")
    half = peers // 2
    width = pieces[0].shape[1]
    sends = [pieces[k * (half + 1) : k * (half + 1) + half] for k in (0, 1)]
    keeps = [pieces[k * (half + 1) + half] for k in (0, 1)]
    left = [[b for b in reversed(range(bits)) if b != step_bits(bits, k)[0]] for k in (0, 1)]
    for step in range(bits):
        arrived, unused = lax.optimization_barrier(
            (
                [
                    [flipped(item, peers, step_bits(bits, k)[step]) for item in sends[k]]
                    for k in (0, 1)
                ],
                list(beside) if step == bits - 1 else [],
            )
        )
        for k in (0, 1):
            got = arrived[k]
            total = jnp.stack(
                [
                    keep.astype(jnp.float32) + item.astype(jnp.float32)
                    for keep, item in zip(jnp.split(keeps[k], len(got), axis=0), got)
                ]
            )
            if step == bits - 1:
                keeps[k] = total[0]
                continue
            total = total.astype(jnp.bfloat16).reshape((2,) * len(left[k]) + (-1, width))
            bit = step_bits(bits, k)[step + 1]
            axis = left[k].index(bit)
            own = (me >> bit) & 1
            keep = lax.dynamic_index_in_dim(total, own, axis, keepdims=False)
            send = lax.dynamic_index_in_dim(total, 1 - own, axis, keepdims=False)
            keeps[k] = keep.reshape(-1, width)
            sends[k] = jnp.split(send.reshape(-1, width), len(got) // 2, axis=0)
            left[k].pop(axis)
    return keeps


def rows_pieces(blocks, peers, bits):
    current = [[item] for item in blocks]
    for step in reversed(range(bits)):
        arrived = lax.optimization_barrier(
            [[flipped(item, peers, step_bits(bits, k)[step]) for item in current[k]] for k in (0, 1)]
        )
        current = [current[k] + arrived[k] for k in (0, 1)]
    return current[0] + current[1]


def attend(mixed, length, tables):
    slots = mixed.shape[0]
    cosine, sine = tables
    query = rotate(mixed[:, 0], cosine, sine).astype(jnp.bfloat16)
    keys = rotate(mixed[:, 1], cosine, sine).astype(jnp.bfloat16)
    values = mixed[:, 2].astype(jnp.bfloat16)
    scores = jnp.einsum(
        "qhd,khd->hqk", query, keys, preferred_element_type=jnp.float32
    ) * HEAD_DIM ** (-0.5)
    scores = jnp.where(allowed_mask(slots, length)[None], scores, -jnp.inf)
    peak = jnp.max(scores, axis=-1, keepdims=True)
    expo = jnp.exp(scores - peak)
    total = jnp.sum(expo, axis=-1, keepdims=True)
    probs_low = (expo / total).astype(jnp.bfloat16)
    logsum = peak + jnp.log(total)
    heads_out = jnp.einsum("hqk,khd->qhd", probs_low, values, preferred_element_type=jnp.float32)
    return (heads_out.reshape(slots, -1).astype(jnp.bfloat16), (query, keys, values, logsum))


def attend_back(out_grad, saved, length, tables):
    query, keys, values, logsum = saved
    slots, heads = query.shape[:2]
    cosine, sine = tables
    out_grad = out_grad.reshape(slots, heads, HEAD_DIM)
    scores = jnp.einsum(
        "qhd,khd->hqk", query, keys, preferred_element_type=jnp.float32
    ) * HEAD_DIM ** (-0.5)
    probs = jnp.where(allowed_mask(slots, length)[None], jnp.exp(scores - logsum), 0.0)
    probs_low = probs.astype(jnp.bfloat16)
    prob_grad = jnp.einsum("qhd,khd->hqk", out_grad, values, preferred_element_type=jnp.float32)
    value_grad = jnp.einsum("hqk,qhd->khd", probs_low, out_grad, preferred_element_type=jnp.float32)
    score_grad = (probs * (prob_grad - jnp.sum(probs * prob_grad, axis=-1, keepdims=True))).astype(
        jnp.bfloat16
    )
    query_grad = jnp.einsum(
        "hqk,khd->qhd", score_grad, keys, preferred_element_type=jnp.float32
    ) * HEAD_DIM ** (-0.5)
    key_grad = jnp.einsum(
        "hqk,qhd->khd", score_grad, query, preferred_element_type=jnp.float32
    ) * HEAD_DIM ** (-0.5)
    query_grad = rotate_back(query_grad, cosine, sine)
    key_grad = rotate_back(key_grad, cosine, sine)
    return jnp.stack([query_grad, key_grad, value_grad], axis=1).astype(jnp.bfloat16)


def dot(left, right):
    return jnp.dot(left, right, preferred_element_type=jnp.float32)


def dot_nt(left, right):
    return lax.dot_general(
        left, right, (((1,), (1,)), ((), ())), preferred_element_type=jnp.float32
    )


def dot_tn(left, right):
    return lax.dot_general(
        left, right, (((0,), (0,)), ((), ())), preferred_element_type=jnp.float32
    )


CHEAP = pl.CostEstimate(flops=1, transcendentals=0, bytes_accessed=1)
SCALE = HEAD_DIM ** (-0.5)


def work(flops):
    return pl.CostEstimate(flops=4 * flops, transcendentals=0, bytes_accessed=flops // 256)


def call(body, grid, in_specs, out_specs, out_shape, info, args, scratch=(), cost=CHEAP):
    return pl.pallas_call(
        body,
        grid_spec=pltpu.PrefetchScalarGridSpec(
            num_scalar_prefetch=1,
            grid=grid,
            in_specs=in_specs,
            out_specs=out_specs,
            scratch_shapes=list(scratch),
        ),
        out_shape=out_shape,
        cost_estimate=cost,
        compiler_params=pltpu.CompilerParams(vmem_limit_bytes=56 << 20),
    )(info, *args)


def low_shape(*shape):
    return jax.ShapeDtypeStruct(shape, jnp.bfloat16)


def full_shape(*shape):
    return jax.ShapeDtypeStruct(shape, jnp.float32)


def fixed(shape):
    return pl.BlockSpec(
        shape, lambda *index: (0,) * len(shape), pipeline_mode=pl.Buffered(buffer_count=1)
    )


def held(width, columns, at):
    return pl.BlockSpec(
        (width, columns), lambda i, info: (0, at), pipeline_mode=pl.Buffered(buffer_count=1)
    )


def held_pieces(width, columns, start, size):
    return [held(width, size, start // size + piece) for piece in range(columns // size)]


def row_stats(rows):
    mean = jnp.mean(rows, axis=1, keepdims=True)
    center = rows - mean
    scale = lax.rsqrt(jnp.mean(center * center, axis=1, keepdims=True) + 1e-05)
    return (mean, scale)


def two_norms(rows, vec_ref, outs):
    rows = rows.astype(jnp.float32)
    mean, scale = row_stats(rows)
    normed = (rows - mean) * scale
    first = normed * vec_ref[0:1] + vec_ref[1:2]
    second = normed * vec_ref[2:3] + vec_ref[3:4]
    outs[0][...] = first.astype(jnp.bfloat16)
    outs[1][...] = second.astype(jnp.bfloat16)
    outs[2][...] = mean
    outs[3][...] = scale
    if len(outs) > 4:
        outs[4][...] = first.T.astype(jnp.bfloat16)
        outs[5][...] = second.T.astype(jnp.bfloat16)


def norms_body(info, z_ref, vec_ref, *outs):
    two_norms(z_ref[...], vec_ref, outs)


def norm_specs(tall, slots, width, row, turn):
    specs = [pl.BlockSpec((tall, width), lambda i, info: (row(i, info), 0))] * 2
    specs += [pl.BlockSpec((tall, 1), lambda i, info: (row(i, info), 0))] * 2
    shapes = [low_shape(slots, width)] * 2 + [full_shape(slots, 1)] * 2
    if turn:
        specs += [pl.BlockSpec((width, tall), lambda i, info: (0, row(i, info)))] * 2
        shapes += [low_shape(width, slots)] * 2
    return (specs, shapes)


def with_turned(out, turn):
    out = list(out)
    return out if turn else out + [out[0].T, out[1].T]


def norms_call(rows, vectors, info):
    slots, width = rows.shape
    tall = min(slots, 256)
    turn = tall % 128 == 0
    specs, shapes = norm_specs(tall, slots, width, lambda i, info: i, turn)
    out = call(
        norms_body,
        (slots // tall,),
        [pl.BlockSpec((tall, width), lambda i, info: (i, 0)), fixed(vectors.shape)],
        specs,
        shapes,
        info,
        (rows, vectors),
    )
    return with_turned(out, turn)


def target_body(info, x_ref, out_ref, *turned_ref):
    tall = x_ref.shape[0]
    place = pl.program_id(0) * tall + lax.broadcasted_iota(jnp.int32, x_ref.shape, 0)
    value = jnp.where(place < info[0], x_ref[...].astype(jnp.float32), 0.0)
    out_ref[...] = value.astype(jnp.bfloat16)
    if turned_ref:
        turned_ref[0][...] = value.T.astype(jnp.bfloat16)


def target_call(cotangent, slots, info):
    width = cotangent.shape[1]
    tall = min(slots, 256)
    steps = slots // tall
    turn = tall % 128 == 0
    out = call(
        target_body,
        (steps,),
        [pl.BlockSpec((tall, width), lambda i, info: (info[1] * steps + i, 0))],
        [pl.BlockSpec((tall, width), lambda i, info: (i, 0))]
        + [pl.BlockSpec((width, tall), lambda i, info: (0, i))] * turn,
        [low_shape(slots, width)] + [low_shape(width, slots)] * turn,
        info,
        (cotangent,),
    )
    return (out[0], out[1]) if turn else (out[0], out[0].T)


def assemble_body(count, normed, info, *refs):
    step = pl.program_id(0)
    rest = refs[count:]
    for which in range(count):

        @pl.when(step == which)
        def _():
            block = refs[which][...]
            if normed:
                rest[1][...] = block
                two_norms(block, rest[0], rest[2:])
            else:
                rest[0][...] = block
                if len(rest) > 1:
                    rest[1][...] = block.astype(jnp.float32).T.astype(jnp.bfloat16)


def assemble(pieces, peers, bits, vectors=None):
    count = len(pieces)
    tall, width = pieces[0].shape
    slots = count * tall
    turn = tall % 128 == 0
    me = lax.axis_index("tensor")
    order = [2 * (me ^ r) + k for k in (0, 1) for r in relative_order(bits, k)]
    info = jnp.stack([jnp.asarray(item, jnp.int32) for item in order])

    def row(s, info):
        return info[s]

    in_specs, args = [fixed(item.shape) for item in pieces], list(pieces)
    specs = [pl.BlockSpec((tall, width), lambda s, info: (info[s], 0))]
    shapes = [low_shape(slots, width)]
    if vectors is not None:
        in_specs.append(fixed(vectors.shape))
        args.append(vectors)
        more, more_shapes = norm_specs(tall, slots, width, row, turn)
        specs, shapes = specs + more, shapes + more_shapes
    elif turn:
        specs.append(pl.BlockSpec((width, tall), lambda s, info: (0, info[s])))
        shapes.append(low_shape(width, slots))
    out = call(
        functools.partial(assemble_body, count, vectors is not None),
        (count,),
        in_specs,
        specs,
        shapes,
        info,
        args,
    )
    if vectors is not None:
        return (out[0], with_turned(out[1:], turn))
    return (out[0], out[1] if turn else out[0].T)


def turned(block, tables, sign):
    cosine, low, high = tables
    front = block[:, :128]
    front = front * cosine + sign * (
        pltpu.roll(front, 128 - ROT // 2, 1) * low + pltpu.roll(front, ROT // 2, 1) * high
    )
    return jnp.concatenate([front, block[:, 128:]], axis=1)


def turn_tables(slots):
    cosine, sine = (item[:, 0] for item in angle_tables(slots))
    rest = 128 - ROT
    zero = jnp.zeros_like(sine)
    pad = jnp.zeros((slots, rest), jnp.float32)
    return (
        jnp.concatenate([cosine, cosine, pad + 1.0], axis=1),
        jnp.concatenate([-sine, zero, pad], axis=1),
        jnp.concatenate([zero, sine, pad], axis=1),
    )


def allowed_block(start, rows, span, length):
    query = start + lax.broadcasted_iota(jnp.int32, (rows, span), 0)
    key = lax.broadcasted_iota(jnp.int32, (rows, span), 1)
    return (key <= query) & (key < length)


def heads_body(
    steps, info, x_ref, wq_ref, wk_ref, wv_ref, cos_ref, low_ref, high_ref, out_ref, qkv_ref, lse_ref, k_ref, v_ref
):
    step = pl.program_id(0)
    rows = x_ref.shape[0]
    tables = (cos_ref[...], low_ref[...], high_ref[...])
    rows_here = x_ref[...]
    query = turned(dot(rows_here, wq_ref[...]), tables, 1.0).astype(jnp.bfloat16)
    keys = turned(dot(rows_here, wk_ref[...]), tables, 1.0).astype(jnp.bfloat16)
    values = dot(rows_here, wv_ref[...]).astype(jnp.bfloat16)
    qkv_ref[:, :HEAD_DIM] = query
    qkv_ref[:, HEAD_DIM : 2 * HEAD_DIM] = keys
    qkv_ref[:, 2 * HEAD_DIM :] = values
    place = pl.multiple_of(step * rows, rows)
    k_ref[pl.ds(place, rows), :] = keys
    v_ref[pl.ds(place, rows), :] = values
    for now in range(steps):

        @pl.when(step == now)
        def _():
            span = (now + 1) * rows
            scores = dot_nt(query, k_ref[:span]) * SCALE
            scores = jnp.where(allowed_block(now * rows, rows, span, info[0]), scores, -jnp.inf)
            peak = jnp.max(scores, axis=1, keepdims=True)
            expo = jnp.exp(scores - peak)
            total = jnp.sum(expo, axis=1, keepdims=True)
            probs = (expo / total).astype(jnp.bfloat16)
            out_ref[...] = dot(probs, v_ref[:span]).astype(jnp.bfloat16)
            lse_ref[...] = peak + jnp.log(total)


def heads_call(first_in, inward, tables, info):
    slots, width = first_in.shape
    rows = min(slots, 256)
    steps = slots // rows
    columns = 3 * HEAD_DIM

    def tall(size):
        return pl.BlockSpec((rows, size), lambda i, info: (i, 0))

    out, qkv, lse = call(
        functools.partial(heads_body, steps),
        (steps,),
        [tall(width)] + [held(width, HEAD_DIM, part) for part in range(3)] + [tall(128)] * 3,
        [tall(HEAD_DIM), tall(columns), tall(1)],
        [low_shape(slots, HEAD_DIM), low_shape(slots, columns), full_shape(slots, 1)],
        info,
        (first_in, inward, inward, inward, *tables),
        [pltpu.VMEM((slots, HEAD_DIM), jnp.bfloat16)] * 2,
    )
    return (out, (qkv, lse))


def heads_back_body(
    steps, info, qkv_ref, lse_ref, grad_ref, cos_ref, low_ref, high_ref, out_ref, dk_ref, dv_ref
):
    step = pl.program_id(0)
    slots = qkv_ref.shape[0]
    rows = slots // steps

    def tables(start, size):
        return tuple(ref[start : start + size] for ref in (cos_ref, low_ref, high_ref))

    @pl.when(step == 0)
    def _():
        dk_ref[...] = jnp.zeros_like(dk_ref)
        dv_ref[...] = jnp.zeros_like(dv_ref)

    for now in range(steps):

        @pl.when(step == now)
        def _():
            span, start = (now + 1) * rows, now * rows
            query = qkv_ref[start:span, :HEAD_DIM]
            keys = qkv_ref[:span, HEAD_DIM : 2 * HEAD_DIM]
            values = qkv_ref[:span, 2 * HEAD_DIM :]
            grad = grad_ref[...]
            scores = dot_nt(query, keys) * SCALE
            allowed = allowed_block(start, rows, span, info[0])
            probs = jnp.where(allowed, jnp.exp(scores - lse_ref[...]), 0.0)
            prob_grad = dot_nt(grad, values)
            spread = jnp.sum(probs * prob_grad, axis=1, keepdims=True)
            score_grad = (probs * (prob_grad - spread)).astype(jnp.bfloat16)
            query_grad = dot(score_grad, keys) * SCALE
            out_ref[start:span, :HEAD_DIM] = turned(
                query_grad, tables(start, rows), -1.0
            ).astype(jnp.bfloat16)
            dv_ref[:span] += dot_tn(probs.astype(jnp.bfloat16), grad)
            dk_ref[:span] += dot_tn(score_grad, query)

    @pl.when(step == steps - 1)
    def _():
        out_ref[:, HEAD_DIM : 2 * HEAD_DIM] = turned(
            dk_ref[...] * SCALE, tables(0, slots), -1.0
        ).astype(jnp.bfloat16)
        out_ref[:, 2 * HEAD_DIM :] = dv_ref[...].astype(jnp.bfloat16)


def heads_back_call(saved, out_grad, tables, info, cost=CHEAP):
    qkv, lse = saved
    slots, columns = qkv.shape
    rows = min(slots, 256)
    steps = slots // rows
    return call(
        functools.partial(heads_back_body, steps),
        (steps,),
        [
            fixed(qkv.shape),
            pl.BlockSpec((rows, 1), lambda i, info: (i, 0)),
            pl.BlockSpec((rows, HEAD_DIM), lambda i, info: (i, 0)),
        ]
        + [fixed((slots, 128))] * 3,
        pl.BlockSpec((slots, columns), lambda i, info: (0, 0)),
        low_shape(slots, columns),
        info,
        (qkv, lse, out_grad, *tables),
        [pltpu.VMEM((slots, HEAD_DIM), jnp.float32)] * 2,
        cost,
    )


def units_body(pieces, info, x_ref, *refs):
    weights, (offset_ref, act_ref, slope_ref) = refs[:pieces], refs[pieces:]
    size = weights[0].shape[1]
    for piece in range(pieces):
        here = slice(piece * size, (piece + 1) * size)
        hidden = dot(x_ref[...], weights[piece][...]) + offset_ref[:, here]
        cdf = 0.5 * (1.0 + lax.erf(hidden * 0.7071067811865476))
        act_ref[:, here] = (hidden * cdf).astype(jnp.bfloat16)
        bell = jnp.exp(-0.5 * hidden * hidden) * 0.3989422804014327
        slope_ref[:, here] = (cdf + hidden * bell).astype(jnp.bfloat16)


def units_call(second_in, expand, start, offsets, unit, info):
    slots, width = second_in.shape
    columns = offsets.shape[0]
    tall = min(slots, 256)
    spec = pl.BlockSpec((tall, columns), lambda i, info: (i, 0))
    weights = held_pieces(width, columns, start * unit, unit)
    return call(
        functools.partial(units_body, len(weights)),
        (slots // tall,),
        [pl.BlockSpec((tall, width), lambda i, info: (i, 0))] + weights + [fixed((1, columns))],
        [spec, spec],
        [low_shape(slots, columns)] * 2,
        info,
        (second_in, *[expand] * len(weights), offsets[None]),
    )


def halving_blocks(half, tall):
    return ([tall] * half + [half * tall]) * 2


def place_rows(info, value_ref, outs, half, tall):
    for which in range(4):
        stream, kept = which // 2, which % 2
        for place in range(half):
            start = (2 * info[which * half + place] + stream) * tall
            rows = value_ref[pl.ds(pl.multiple_of(start, tall), tall)]
            if kept:
                outs[stream * (half + 1) + half][place * tall : (place + 1) * tall] = rows
            else:
                outs[stream * (half + 1) + place][...] = rows


def partial_body(half, tall, parts, info, *refs):
    lefts, rights = [refs[k * parts : (k + 1) * parts] for k in range(4)], refs[4 * parts :][:4]
    outs, value_ref = refs[4 * parts + 4 : -1], refs[-1]
    rows = lefts[0][0].shape[0]
    for part in range(parts):
        value = None
        for left, right in zip(lefts, rights):
            term = dot_nt(left[part][...], right[...])
            value = term if value is None else value + term
        value_ref[part * rows : (part + 1) * rows] = value.astype(jnp.bfloat16)
    if half:
        place_rows(info, value_ref, outs, half, tall)
    else:
        outs[0][...] = value_ref[...]


def partial_call(heads, acts, outward, contract, outward_at, contract_at, places, cost=CHEAP):
    slots, unit = heads[0].shape
    wide = acts[0].shape[1]
    width = outward[0].shape[0]
    block = min(width, 512)
    parts = max(slots // 256, 1)
    rows = slots // parts
    half = len(places) // 4
    tall = slots // (4 * half) if half else 0
    heights = halving_blocks(half, tall) if half else [slots]
    info = jnp.stack([jnp.asarray(item, jnp.int32) for item in (places or [0])])

    def row_blocks(columns):
        return [
            pl.BlockSpec(
                (rows, columns),
                lambda j, info, part=part: (part, 0),
                pipeline_mode=pl.Buffered(buffer_count=1),
            )
            for part in range(parts)
        ]

    return call(
        functools.partial(partial_body, half, tall, parts),
        (width // block,),
        row_blocks(unit) * 2
        + row_blocks(wide) * 2
        + [pl.BlockSpec((block, unit), lambda j, info: (j, outward_at))] * 2
        + [pl.BlockSpec((block, wide), lambda j, info: (j, contract_at * unit // wide))] * 2,
        [pl.BlockSpec((height, block), lambda j, info: (0, j)) for height in heights],
        [low_shape(height, width) for height in heights],
        info,
        [item for item in (*heads, *acts) for part in range(parts)] + [*outward, *contract],
        [pltpu.VMEM((slots, block), jnp.bfloat16)],
        cost,
    )


def grads_body(plan, split, info, *refs):
    lefts = refs[: max(plan) + 1]
    rights = refs[len(lefts) : len(lefts) + len(plan)]
    rest = refs[len(lefts) + len(plan) :]
    got, outs = ((), rest) if split else (rest[:-1], rest[-1:])
    size = rights[0].shape[1]
    for place, right in enumerate(rights):
        value = dot(lefts[plan[place]][...], right[...])
        if split:
            outs[place][...] = value.astype(jnp.bfloat16)
        else:
            value = value + got[place][...].astype(jnp.float32)
            outs[0][:, place * size : (place + 1) * size] = value.astype(jnp.bfloat16)


def grads_call(lefts, rights, size, info, got=None, cost=CHEAP):
    width, slots = lefts[0].shape
    columns = sum(item.shape[1] for item in rights)
    block = min(width, 256)
    split = got is None
    spec = pl.BlockSpec((block, columns), lambda j, info: (j, 0))
    pieces = columns // size
    piece_specs = [pl.BlockSpec((block, size), lambda j, info: (j, 0))] * pieces
    plan, specs, args = [], [], []
    for which, right in enumerate(rights):
        for piece in held_pieces(slots, right.shape[1], 0, size):
            plan.append(which)
            specs.append(piece)
            args.append(right)
    return call(
        functools.partial(grads_body, plan, split),
        (width // block,),
        [pl.BlockSpec((block, slots), lambda j, info: (j, 0))] * len(lefts)
        + specs
        + ([] if split else piece_specs),
        piece_specs if split else spec,
        [low_shape(width, size)] * pieces if split else low_shape(width, columns),
        info,
        (*lefts, *args, *(got or ())),
        cost=cost,
    )


def lifted_body(pieces, info, g_ref, outward_ref, *refs):
    weights, (slope_ref, out_ref, hidden_ref, sum_ref) = refs[:pieces], refs[pieces:]
    size = weights[0].shape[1]

    @pl.when(pl.program_id(0) == 0)
    def _():
        sum_ref[...] = jnp.zeros_like(sum_ref)

    for piece in range(pieces):
        here = slice(piece * size, (piece + 1) * size)
        value = dot(g_ref[...], weights[piece][...]) * slope_ref[:, here].astype(jnp.float32)
        value = value.astype(jnp.bfloat16)
        hidden_ref[:, here] = value
        sum_ref[:, here] += jnp.sum(value.astype(jnp.float32), axis=0, keepdims=True)
    out_ref[...] = dot(g_ref[...], outward_ref[...]).astype(jnp.bfloat16)


def lifted_call(grad, outward, contract, outward_at, contract_at, slope, unit, info, cost=CHEAP):
    slots, width = grad.shape
    columns = slope.shape[1]
    tall = min(slots, 256)
    weights = held_pieces(width, columns, contract_at * unit, unit)

    def rows(size):
        return pl.BlockSpec((tall, size), lambda i, info: (i, 0))

    return call(
        functools.partial(lifted_body, len(weights)),
        (slots // tall,),
        [rows(width), held(width, unit, outward_at)] + weights + [rows(columns)],
        [rows(unit), rows(columns), pl.BlockSpec((1, columns), lambda i, info: (0, 0))],
        [low_shape(slots, unit), low_shape(slots, columns), full_shape(1, columns)],
        info,
        (grad, outward, *[contract] * len(weights), slope),
        cost=cost,
    )


def back_body(half, tall, info, *refs):
    z_ref, mean_ref, scale_ref, vec_ref = refs[:4]
    mixed, hidden, inward, expand = refs[4:6], refs[6:8], refs[8:10], refs[10:12]
    outs, sums_ref, hat_ref, total_ref, along_ref = refs[12:-4], *refs[-4:]
    part, block = pl.program_id(0), pl.program_id(1)
    size = inward[0].shape[0]
    width = z_ref.shape[1]
    columns = pl.ds(pl.multiple_of(block * size, size), size)
    mean, scale = mean_ref[...], scale_ref[...]
    first = dot_nt(mixed[0][...], inward[0][...]) + dot_nt(mixed[1][...], inward[1][...])
    second = dot_nt(hidden[0][...], expand[0][...]) + dot_nt(hidden[1][...], expand[1][...])
    normed = (z_ref[:, columns].astype(jnp.float32) - mean) * scale
    sums = [
        jnp.sum(value, axis=0, keepdims=True)
        for value in (first * normed, first, second * normed, second)
    ]

    @pl.when(part == 0)
    def _():
        for row in range(4):
            sums_ref[row : row + 1, columns] = sums[row]

    @pl.when(part > 0)
    def _():
        for row in range(4):
            sums_ref[row : row + 1, columns] += sums[row]

    hat = first * vec_ref[0:1] + second * vec_ref[2:3]
    hat_ref[:, columns] = hat
    total = jnp.sum(hat, axis=1, keepdims=True)
    along = jnp.sum(hat * normed, axis=1, keepdims=True)

    @pl.when(block == 0)
    def _():
        total_ref[...] = total
        along_ref[...] = along

    @pl.when(block > 0)
    def _():
        total_ref[...] += total
        along_ref[...] += along

    @pl.when(block == pl.num_programs(1) - 1)
    def _():
        rows = hat_ref.shape[0]
        step = tall if half else min(rows, 256)
        for start in range(0, rows, step):
            here = slice(start, start + step)
            normed_here = (z_ref[here].astype(jnp.float32) - mean_ref[here]) * scale_ref[here]
            result = scale_ref[here] * (
                hat_ref[here]
                - total_ref[here] / width
                - normed_here * (along_ref[here] / width)
            )
            result = result.astype(jnp.bfloat16)
            if not half:
                outs[0][pl.ds(part * rows + start, step)] = result
                continue
            stream = start // tall % 2
            peer = part * (rows // (2 * tall)) + start // (2 * tall)
            at = 2 * (2 * peer + stream)
            own_outs = outs[stream * (half + 1) : (stream + 1) * (half + 1)]

            @pl.when(info[at] == 0)
            def _():
                own_outs[half][pl.ds(pl.multiple_of(info[at + 1] * tall, tall), tall)] = result

            for place in range(half):

                @pl.when((info[at] == 1) & (info[at + 1] == place))
                def _():
                    own_outs[place][...] = result


def back_call(rows, stats, vectors, mixed_grads, hidden_grads, inward, expand, expand_at, me, peers, bits):
    slots, width = rows.shape
    parts = 2 if bits else 1
    rows_each = slots // parts
    block = min(width, 512)
    half = peers // 2 if bits else 0
    tall = slots // (2 * peers) if bits else 0
    heads_columns, wide = mixed_grads[0].shape[1], hidden_grads[0].shape[1]
    table = []
    for peer in range(peers if bits else 0):
        for stream in (0, 1):
            bit = step_bits(bits, stream)[0]
            own = (me >> bit) & 1
            place = (peer & ((1 << bit) - 1)) | ((peer >> (bit + 1)) << bit)
            table.append(jnp.asarray(((peer >> bit) & 1) != own, jnp.int32))
            table.append(jnp.asarray(place, jnp.int32))
    info = jnp.stack(table or [jnp.asarray(0, jnp.int32)])
    heights = halving_blocks(half, tall) if half else [slots]

    def spec(columns):
        return pl.BlockSpec((rows_each, columns), lambda i, j, info: (i, 0))

    def weights(columns, at):
        return pl.BlockSpec((block, columns), lambda i, j, info: (j, at))

    def whole(*shape):
        return pl.BlockSpec(shape, lambda i, j, info: (0, 0))

    out = call(
        functools.partial(back_body, half, tall),
        (parts, width // block),
        [spec(width), spec(1), spec(1)]
        + [pl.BlockSpec((vectors.shape[0], block), lambda i, j, info: (0, j))]
        + [spec(item.shape[1]) for item in (*mixed_grads, *hidden_grads)]
        + [weights(heads_columns, 0)] * 2
        + [weights(wide, expand_at * heads_columns // (3 * wide))] * 2,
        [whole(height, width) for height in heights] + [whole(4, width)],
        [low_shape(height, width) for height in heights] + [full_shape(4, width)],
        info,
        (rows, *stats, vectors, *mixed_grads, *hidden_grads, *inward, *expand),
        [pltpu.VMEM((rows_each, width), jnp.float32)]
        + [pltpu.VMEM((rows_each, 1), jnp.float32)] * 2,
    )
    return out[:-1], out[-1]


def share_of(total):
    return lax.psum_scatter(total, "dp", scatter_dimension=0, tiled=True)


def adam_kernel(rate, decay, arrange, info, *refs):
    grads, (master, first, second), outs = refs[:4], refs[4:7], refs[7:]

    def run(half, region, turn):
        grad = jnp.where(info[0] == 0, grads[half][...], grads[2 + half][...]).astype(jnp.float32)
        grad = grad.T if turn else grad
        new = adam_update(master[region], grad, first[region], second[region], rate, decay)
        for out, value in zip(outs, new):
            out[region] = value

    arrange(run)


def adam_columns(index, grads, arrays, depth, starts, core):
    parts, _, columns = arrays[0].shape
    half = columns // 2
    tall = depth // 2

    def arrange(run):
        for which in (0, 1):
            run(which, (0, slice(None), pl.ds(which * half, half)), False)

    def grad_spec(start):
        return pl.BlockSpec((tall, half), lambda i, j, info: (j, start + i))

    block_spec = pl.BlockSpec((1, tall, columns), lambda i, j, info: (i, j, 0))
    return call(
        functools.partial(adam_kernel, RATES[index], DECAYS[index], arrange),
        (parts, depth // tall),
        [grad_spec(starts[which // 2]) for which in range(4)] + [block_spec] * 3,
        [block_spec] * 3,
        [jax.ShapeDtypeStruct(arrays[0].shape, jnp.float32)] * 3,
        core,
        (*grads, *arrays),
    )


def adam_rows(index, grads, arrays, starts, block, core, cost=CHEAP):
    units, depth = arrays[0].shape
    each = units // 2 // block

    def arrange(run):
        for half in (0, 1):

            @pl.when(pl.program_id(0) == half)
            def _():
                run(half, Ellipsis, True)

    def grad_spec(half, start):
        def place(h, j, info):
            return (0, start + jnp.where(h == half, j, (each - 1) * (1 - half)))

        return pl.BlockSpec((depth, block), place)

    block_spec = pl.BlockSpec((block, depth), lambda h, j, info: (h * each + j, 0))
    return call(
        functools.partial(adam_kernel, RATES[index], DECAYS[index], arrange),
        (2, each),
        [grad_spec(which % 2, starts[which // 2]) for which in range(4)] + [block_spec] * 3,
        [block_spec] * 3,
        [jax.ShapeDtypeStruct(arrays[0].shape, jnp.float32)] * 3,
        core,
        (*grads, *arrays),
        cost=cost,
    )


def adam_update(master, grad, first, second, rate, decay):
    new_first = 0.9 * first + 0.1 * grad
    new_second = 0.95 * second + 0.05 * grad * grad
    corrected = new_first / (1.0 - 0.9**STEP)
    spread = jnp.sqrt(new_second / (1.0 - 0.95**STEP))
    return (master - rate * (corrected / (spread + 1e-08) + decay * master), new_first, new_second)


def local(
    tokens,
    cotangent,
    lengths,
    inward,
    outward,
    expand,
    contract,
    vectors,
    offsets,
    inward_first,
    inward_second,
    outward_first,
    outward_second,
    expand_first,
    expand_second,
    contract_first,
    contract_second,
    vectors_first,
    vectors_second,
    offsets_first,
    offsets_second,
):
    core = lax.axis_index("pipe")
    peers = lax.axis_size("tensor")
    groups = lax.axis_size("dp")
    place = lax.axis_index("tensor")
    depth = inward.shape[1]
    heads_local = inward.shape[3] // HEAD_DIM
    lone = heads_local == 2
    head_share = inward.shape[3] // 2
    unit_share = expand.shape[2] // 2
    batches = lengths.shape[0]
    width = tokens.shape[1]
    slots = tokens.shape[0] // batches
    row_share = slots // peers

    bits = halving(peers, slots)

    def packed(shard):
        mine, theirs = (item.astype(jnp.bfloat16).reshape(depth, -1) for item in halves(shard, core))
        got = swap(theirs)
        return (jnp.where(core == 0, mine, got), jnp.where(core == 0, got, mine))

    packs = [packed(item) for item in (inward[0], expand[0], outward[0].T, contract[0].T)]
    count = unit_share // head_share

    small = jnp.concatenate([vectors.reshape(-1), offsets.reshape(-1)]).astype(jnp.bfloat16)
    small = lax.all_gather(small, ("pipe", "dp"), axis=0, tiled=False).reshape(2, groups, -1)
    small = small.astype(jnp.float32)
    vector_values = [
        small[layer, :, : 5 * depth].reshape(groups, 5, depth).transpose(1, 0, 2).reshape(5, width)
        for layer in (0, 1)
    ]
    offset_pairs = [halves(small[layer, :, 5 * depth :].reshape(-1), core) for layer in (0, 1)]

    tables = angle_tables(slots)
    turns = turn_tables(slots)
    length = lax.dynamic_index_in_dim(lengths, core, 0, keepdims=False)
    info = length[None]
    own = lax.dynamic_slice_in_dim(tokens, core * slots, slots, 0)
    target, target_turned = target_call(cotangent, slots, jnp.stack([length, core]))
    places = scatter_places(place, peers, bits) if bits else []

    def whole_of(shard):
        return lax.all_gather(shard, "dp", axis=0, tiled=True)

    def pair_of(whole, *earlier):
        whole = after(whole, *earlier)
        return (whole, swap(whole))

    def block_of(array):
        block = lax.dynamic_slice_in_dim(array, place * row_share, row_share, 0)
        return block.astype(jnp.float32)

    def summed(pieces, beside=()):
        if bits:
            return jnp.concatenate(sum_scatter(pieces, peers, bits, beside), axis=0)
        return lax.psum_scatter(pieces[0], "tensor", scatter_dimension=0, tiled=True).astype(
            jnp.float32
        )

    def spread(block):
        tall = row_share // 2
        return rows_pieces((block[:tall], block[tall:]), peers, bits)

    def heads_of(first_in, inward_pair):
        if lone:
            done = [heads_call(first_in, item, turns, info) for item in inward_pair]
            return ([item[0] for item in done], [item[1] for item in done])
        mixed = [dot(first_in, w[:, : 3 * head_share]).reshape(slots, 3, -1) for w in inward_pair]
        mixed = ordered(mixed[0], mixed[1], core).reshape(slots, 3, -1, HEAD_DIM)
        out, saved = attend(mixed, length, tables)
        return (list(halves(out, core)), saved)

    def heads_back(which, out_grads, saved, cost=CHEAP):
        if lone:
            return heads_back_call(saved[which], out_grads[which], turns, info, cost)
        grad = ordered(out_grads[0], out_grads[1], core)
        mixed_grad = attend_back(grad, saved, length, tables).reshape(slots, 3, -1)
        return halves(mixed_grad, core)[which].reshape(slots, -1)

    def units_of(second_in, expand_pair, start, layer):
        done = [
            units_call(
                second_in, expand_pair[which], start, offset_pairs[layer][which], head_share, info
            )
            for which in (0, 1)
        ]
        return ([item[0] for item in done], [item[1] for item in done])

    def layer_output(layer, outward_pair, contract_pair, heads, acts, cost=CHEAP):
        pieces = partial_call(
            heads,
            acts,
            outward_pair,
            contract_pair,
            outward_at[layer],
            contract_at[layer],
            places,
            cost,
        )
        block = summed(pieces) + block_of(inputs[layer]) + vector_values[layer][4]
        return block.astype(jnp.bfloat16)

    outward_at, contract_at, expand_at = (2 * count, 3), (0, 0), (count, 4)
    shards = [packs[0][0], jnp.concatenate([packs[3][0], packs[1][0], packs[2][0]], axis=1)]
    shards.append(jnp.concatenate([after(packs[0][1], shards[1]), packs[2][1], packs[1][1]], axis=1))
    shards.append(after(packs[3][1], shards[2]))
    shards[1] = after(shards[1], shards[0])
    wholes = [whole_of(item) for item in shards]
    inputs = [own]
    normed = norms_call(own, vector_values[0], info)
    first_in, second_in = normed[:2]
    inward_pairs = [pair_of(wholes[0], first_in, second_in, target_turned)]
    heads, saved = heads_of(first_in, inward_pairs[0])
    rest_pair = pair_of(wholes[1], *heads)
    acts, slopes = units_of(second_in, rest_pair, expand_at[0], 0)
    kept = [(normed, heads, saved, acts, slopes)]
    outward_pairs, contract_pairs, expand_pairs = [rest_pair], [rest_pair], [rest_pair]
    results = [layer_output(0, rest_pair, rest_pair, heads, acts)]
    if bits:
        rows, normed = assemble(
            spread(results[0]), peers, bits, vector_values[1]
        )
        inputs.append(rows)
    else:
        inputs.append(lax.all_gather(results[0], "tensor", axis=0, tiled=True))
        normed = norms_call(inputs[1], vector_values[1], info)
    first_in, second_in = normed[:2]
    rest_pair = pair_of(wholes[2], first_in, second_in)
    for store in (inward_pairs, outward_pairs, expand_pairs):
        store.append(rest_pair)
    acts, slopes = units_of(second_in, rest_pair, expand_at[1], 1)

    grad_low, grad_turned = target, target_turned
    shares, row_grads, vector_grads, offset_grads = [None] * 2, [None] * 2, [None] * 2, [None] * 2
    for layer in (1, 0):
        if layer == 0:
            normed, heads, saved, acts, slopes = kept[0]
        dense = 2 * slots * width * unit_share
        theirs = grads_call([grad_turned], [acts[1]], head_share, info)
        if layer == 1:
            mine = grads_call([grad_turned], [acts[0]], head_share, info)
            heads, saved = heads_of(after(first_in, *theirs, *mine), rest_pair)
            theirs = [after(after(item, *mine, *heads), wholes[3]) for item in theirs]
            contract_pairs.append(pair_of(wholes[3], *theirs))
        got = [swap(item) for item in theirs]

        def lift(which, grad, cost=CHEAP):
            return lifted_call(
                grad,
                outward_pairs[layer][which],
                contract_pairs[layer][which],
                outward_at[layer],
                contract_at[layer],
                slopes[which],
                head_share,
                info,
                cost,
            )

        def total_of(lefts, theirs, mine, cost=CHEAP, between=None):
            got = [swap(item) for item in grads_call(lefts, theirs, head_share, info, cost=cost)]
            if between is not None:
                mine = [after(mine[0], between), *mine[1:]]
            return grads_call(lefts, mine, head_share, info, got, cost)

        if layer == 1:
            lifted = [lift(0, after(grad_low, *theirs), work(dense))]
            mine = [after(item, lifted[0][1]) for item in mine]
            contract_total = jnp.concatenate(
                [
                    (own.astype(jnp.float32) + item.astype(jnp.float32)).astype(jnp.bfloat16)
                    for own, item in zip(mine, got)
                ],
                axis=1,
            )
        else:
            contract_total = grads_call([grad_turned], [acts[0]], head_share, info, got)
            lifted = [lift(0, after(grad_low, contract_total))]
        contract_share = share_of(contract_total)
        lifted.append(lift(1, after(grad_low, contract_total)))
        out_grads = [item[0] for item in lifted]
        hidden_grads = [item[1] for item in lifted]
        offset_grads[layer] = [item[2][0] for item in lifted]
        first_turned, second_turned = normed[4:]
        lefts = [first_turned, grad_turned]
        small_work = work(dense // 2)
        if layer == 1:
            mixed_first = heads_back(0, out_grads, saved, small_work)
            expand_total = total_of(
                [second_turned], [hidden_grads[1]], [hidden_grads[0]], between=mixed_first
            )
            expand_share = share_of(expand_total)
            out_grads = [after(item, expand_total) for item in out_grads]
            mixed_grads = [mixed_first, heads_back(1, out_grads, saved)]
            ahead = mixed_grads
        else:
            mixed_last = heads_back(1, out_grads, saved)
            mixed_first = heads_back(0, out_grads, saved, small_work)
            mixed_grads = [mixed_first, mixed_last]
            hidden_here = [after(item, *shares[1]) for item in hidden_grads]
            other_total = total_of(
                [second_turned, first_turned, grad_turned],
                [hidden_here[1], mixed_last, heads[1]],
                [hidden_here[0], mixed_first, heads[0]],
                between=mixed_first,
            )
            ahead = [other_total]
        pieces, norm_part = back_call(
            after(inputs[layer], *ahead),
            normed[2:4],
            vector_values[layer],
            mixed_grads,
            hidden_grads,
            inward_pairs[layer],
            expand_pairs[layer],
            expand_at[layer],
            place,
            peers,
            bits,
        )
        rights = [[mixed_grads[which], heads[which]] for which in (1, 0)]
        if layer == 1:
            lefts[0] = after(lefts[0], *pieces)
            heads_total = total_of(lefts, *rights, work(dense))
            shares[1] = (share_of(heads_total), expand_share, contract_share)
            pieces = [after(item, contract_share) for item in pieces]
        else:
            shares[0] = share_of(other_total)
            contract_here = after(contract_share, *pieces)
            contract_out = adam_rows(
                3,
                (contract_here, swap(contract_here), swap(shares[1][2]), shares[1][2]),
                [item[0] for item in (contract, contract_first, contract_second)],
                (0, 0),
                head_share,
                core[None],
            )
            pairs = [
                [after(item, *pieces) for item in pair]
                for pair in (outward_pairs[1], contract_pairs[1])
            ]
            results.append(layer_output(1, *pairs, *last))
        upstream = block_of(grad_low)
        vector_grads[layer] = jnp.concatenate(
            [norm_part, jnp.sum(upstream, axis=0)[None]], axis=0
        )
        row_grads[layer] = upstream + summed(pieces, contract_out[:1] if layer == 0 else ())
        if layer == 1:
            block = row_grads[layer].astype(jnp.bfloat16)
            if bits:
                grad_low, grad_turned = assemble(
                    [after(item, expand_share) for item in spread(block)], peers, bits
                )
            else:
                grad_low = lax.all_gather(block, "tensor", axis=0, tiled=True)
                grad_turned = grad_low.T
            last = (heads, acts)

    activations = jnp.where(core == 0, results[0], results[1])
    got = swap(jnp.where(core == 0, results[1], results[0]))
    activations = jnp.where(
        core == 0, jnp.stack([activations, got]), jnp.stack([got, activations])
    )[None]
    gradients = jnp.where(core == 0, row_grads[0], row_grads[1])
    got = swap(jnp.where(core == 0, row_grads[1], row_grads[0]))
    gradients = jnp.where(core == 0, jnp.stack([gradients, got]), jnp.stack([got, gradients]))[None]

    vector_sum = added(jnp.stack(vector_grads), "tensor")
    offset_sum = jnp.stack([ordered(item[0], item[1], core) for item in offset_grads])
    small_sum = jnp.concatenate([vector_sum.reshape(2, -1), offset_sum], axis=1)
    small_sum = added(added(small_sum, "pipe"), "dp")
    small_sum = lax.dynamic_index_in_dim(small_sum, core, 0, keepdims=False)
    where = lax.axis_index("dp")
    vector_grad = lax.dynamic_slice_in_dim(
        small_sum[: 5 * width].reshape(5, width), where * depth, depth, 1
    )
    offset_size = offsets.shape[1]
    offset_grad = lax.dynamic_slice_in_dim(
        small_sum, 5 * width + where * offset_size, offset_size, 0
    )

    def viewed(*arrays):
        return [item[0] for item in arrays]

    def parts_first(*arrays):
        return [item[0].transpose(1, 0, 2) for item in arrays]

    which = core[None]
    expand_1, heads_1 = swap(shares[1][1]), swap(shares[1][0])
    vectors_out = adam_update(
        vectors, vector_grad[None], vectors_first, vectors_second, RATES[4], DECAYS[4]
    )
    offsets_out = adam_update(
        offsets, offset_grad[None], offsets_first, offsets_second, RATES[5], DECAYS[5]
    )
    other_share = after(shares[0], contract_out[0], expand_1, heads_1)
    other_0 = swap(other_share)
    expand_out = adam_columns(
        2,
        (other_share, other_0, expand_1, shares[1][1]),
        [expand, expand_first, expand_second],
        depth,
        (0, 0),
        which,
    )
    inward_out = adam_columns(
        0,
        (other_share, other_0, heads_1, shares[1][0]),
        parts_first(inward, inward_first, inward_second),
        depth,
        (count, 0),
        which,
    )
    outward_out = adam_rows(
        1,
        (other_share, other_0, heads_1, shares[1][0]),
        viewed(outward, outward_first, outward_second),
        (count + 3, 3),
        head_share,
        which,
    )
    outputs = [activations, gradients]
    outputs.extend([item.transpose(1, 0, 2)[None] for item in inward_out])
    outputs.extend([item[None] for item in outward_out])
    outputs.extend(expand_out)
    outputs.extend([item[None] for item in contract_out])
    outputs.extend(vectors_out)
    outputs.extend(offsets_out)
    return tuple(outputs)


def solution(mesh):
    return jax.shard_map(
        local,
        mesh=mesh,
        in_specs=(
            P("dp", None),
            P("dp", None),
            P("dp"),
            P("pipe", "dp", None, "tensor"),
            P("pipe", "tensor", "dp"),
            P("pipe", "dp", "tensor"),
            P("pipe", "tensor", "dp"),
            P("pipe", None, "dp"),
            P("pipe", ("tensor", "dp")),
            P("pipe", "dp", None, "tensor"),
            P("pipe", "dp", None, "tensor"),
            P("pipe", "tensor", "dp"),
            P("pipe", "tensor", "dp"),
            P("pipe", "dp", "tensor"),
            P("pipe", "dp", "tensor"),
            P("pipe", "tensor", "dp"),
            P("pipe", "tensor", "dp"),
            P("pipe", None, "dp"),
            P("pipe", None, "dp"),
            P("pipe", ("tensor", "dp")),
            P("pipe", ("tensor", "dp")),
        ),
        out_specs=(
            P("pipe", "dp", "tensor", None),
            P("pipe", "dp", "tensor", None),
            P("pipe", "dp", None, "tensor"),
            P("pipe", "dp", None, "tensor"),
            P("pipe", "dp", None, "tensor"),
            P("pipe", "tensor", "dp"),
            P("pipe", "tensor", "dp"),
            P("pipe", "tensor", "dp"),
            P("pipe", "dp", "tensor"),
            P("pipe", "dp", "tensor"),
            P("pipe", "dp", "tensor"),
            P("pipe", "tensor", "dp"),
            P("pipe", "tensor", "dp"),
            P("pipe", "tensor", "dp"),
            P("pipe", None, "dp"),
            P("pipe", None, "dp"),
            P("pipe", None, "dp"),
            P("pipe", ("tensor", "dp")),
            P("pipe", ("tensor", "dp")),
            P("pipe", ("tensor", "dp")),
        ),
        check_vma=False,
    )
```

```python
import functools

import jax
import jax.numpy as jnp
from jax import lax
from jax.experimental import pallas as pl
from jax.experimental.pallas import tpu as pltpu
from jax.sharding import PartitionSpec as P

HEAD_DIM = 256
ROT = 64
STEP = 10


RATES = (0.03, 0.2, 0.03, 0.015, 0.3, 0.3)
DECAYS = (0.01, 0.01, 0.01, 0.01, 0.0, 0.0)


def angle_tables(slots):
    half = ROT // 2
    positions = jnp.arange(slots).astype(jnp.float32)
    frequency = 10000.0 ** (-(2.0 * jnp.arange(half).astype(jnp.float32)) / ROT)
    angles = positions[:, None] * frequency[None, :]
    return (jnp.cos(angles)[:, None, :], jnp.sin(angles)[:, None, :])


def rotate(block, cosine, sine):
    half = cosine.shape[-1]
    first = block[..., :half]
    second = block[..., half : 2 * half]
    return jnp.concatenate(
        [first * cosine - second * sine, second * cosine + first * sine, block[..., 2 * half :]],
        axis=-1,
    )


def rotate_back(grad, cosine, sine):
    half = cosine.shape[-1]
    first = grad[..., :half]
    second = grad[..., half : 2 * half]
    return jnp.concatenate(
        [first * cosine + second * sine, second * cosine - first * sine, grad[..., 2 * half :]],
        axis=-1,
    )


def norm_parts(rows, gain, shift):
    center = rows - jnp.mean(rows, axis=1, keepdims=True)
    scale = lax.rsqrt(jnp.mean(center * center, axis=1, keepdims=True) + 1e-05)
    normed = center * scale
    return (normed * gain + shift, normed, scale)


def norm_back(back, rows, gain):
    unused, normed, scale = norm_parts(rows, gain, 0.0)
    hat = back * gain
    row_grad = scale * (
        hat
        - jnp.mean(hat, axis=1, keepdims=True)
        - normed * jnp.mean(hat * normed, axis=1, keepdims=True)
    )
    return (row_grad, jnp.sum(back * normed, axis=0), jnp.sum(back, axis=0))


def gelu_slope(hidden):
    return (
        0.5 * (1.0 + lax.erf(hidden * 0.7071067811865476))
        + hidden * jnp.exp(-0.5 * hidden * hidden) * 0.3989422804014327
    )


def allowed_mask(slots, length):
    places = jnp.arange(slots)
    return (places[None, :] <= places[:, None]) & (places[None, :] < length)


def after(array, *earlier):
    return lax.optimization_barrier((array, *earlier))[0]


def added(array, axis):
    peers = lax.axis_size(axis)
    bits = peers.bit_length() - 1
    if peers != 1 << bits:
        return lax.psum(array, axis)
    if peers == 4:
        got = [lax.ppermute(array, axis, [(i, i ^ by) for i in range(4)]) for by in (1, 2, 3)]
        return (array + got[0]) + (got[1] + got[2])
    for bit in range(bits):
        array = array + lax.ppermute(array, axis, [(i, i ^ (1 << bit)) for i in range(peers)])
    return array


def swap(array):
    return lax.ppermute(array, "pipe", [(0, 1), (1, 0)])


def halves(array, core):
    size = array.shape[-1] // 2
    axis = array.ndim - 1
    mine = lax.dynamic_slice_in_dim(array, core * size, size, axis)
    theirs = lax.dynamic_slice_in_dim(array, (1 - core) * size, size, axis)
    return (mine, theirs)


def ordered(mine, theirs, core):
    return jnp.where(
        core == 0,
        jnp.concatenate([mine, theirs], axis=-1),
        jnp.concatenate([theirs, mine], axis=-1),
    )


def flipped(array, peers, bit):
    return lax.ppermute(array, "tensor", [(i, i ^ (1 << bit)) for i in range(peers)])


def halving(peers, rows):
    bits = peers.bit_length() - 1
    return bits if peers == 1 << bits and bits > 0 and rows % (16 * peers) == 0 else 0


def step_bits(bits, stream):
    return [step if stream == 0 else bits - 1 - step for step in range(bits)]


def relative_order(bits, stream):
    order = [0]
    for bit in reversed(step_bits(bits, stream)):
        order = order + [other ^ (1 << bit) for other in order]
    return order


def scatter_places(me, peers, bits):
    half = peers // 2
    places = []
    for stream in (0, 1):
        bit = step_bits(bits, stream)[0]
        own = (me >> bit) & 1
        for value in (1 - own, own):
            for place in range(half):
                low = place & ((1 << bit) - 1)
                high = (place >> bit) << (bit + 1)
                places.append(high | (value << bit) | low)
    return places


def sum_scatter(pieces, peers, bits, beside=()):
    me = lax.axis_index("tensor")
    half = peers // 2
    width = pieces[0].shape[1]
    sends = [pieces[k * (half + 1) : k * (half + 1) + half] for k in (0, 1)]
    keeps = [pieces[k * (half + 1) + half] for k in (0, 1)]
    left = [[b for b in reversed(range(bits)) if b != step_bits(bits, k)[0]] for k in (0, 1)]
    for step in range(bits):
        arrived, unused = lax.optimization_barrier(
            (
                [
                    [flipped(item, peers, step_bits(bits, k)[step]) for item in sends[k]]
                    for k in (0, 1)
                ],
                list(beside) if step == bits - 1 else [],
            )
        )
        for k in (0, 1):
            got = arrived[k]
            total = jnp.stack(
                [
                    keep.astype(jnp.float32) + item.astype(jnp.float32)
                    for keep, item in zip(jnp.split(keeps[k], len(got), axis=0), got)
                ]
            )
            if step == bits - 1:
                keeps[k] = total[0]
                continue
            total = total.astype(jnp.bfloat16).reshape((2,) * len(left[k]) + (-1, width))
            bit = step_bits(bits, k)[step + 1]
            axis = left[k].index(bit)
            own = (me >> bit) & 1
            keep = lax.dynamic_index_in_dim(total, own, axis, keepdims=False)
            send = lax.dynamic_index_in_dim(total, 1 - own, axis, keepdims=False)
            keeps[k] = keep.reshape(-1, width)
            sends[k] = jnp.split(send.reshape(-1, width), len(got) // 2, axis=0)
            left[k].pop(axis)
    return keeps


def rows_pieces(blocks, peers, bits):
    current = [[item] for item in blocks]
    for step in reversed(range(bits)):
        arrived = lax.optimization_barrier(
            [[flipped(item, peers, step_bits(bits, k)[step]) for item in current[k]] for k in (0, 1)]
        )
        current = [current[k] + arrived[k] for k in (0, 1)]
    return current[0] + current[1]


def attend(mixed, length, tables):
    slots = mixed.shape[0]
    cosine, sine = tables
    query = rotate(mixed[:, 0], cosine, sine).astype(jnp.bfloat16)
    keys = rotate(mixed[:, 1], cosine, sine).astype(jnp.bfloat16)
    values = mixed[:, 2].astype(jnp.bfloat16)
    scores = jnp.einsum(
        "qhd,khd->hqk", query, keys, preferred_element_type=jnp.float32
    ) * HEAD_DIM ** (-0.5)
    scores = jnp.where(allowed_mask(slots, length)[None], scores, -jnp.inf)
    peak = jnp.max(scores, axis=-1, keepdims=True)
    expo = jnp.exp(scores - peak)
    total = jnp.sum(expo, axis=-1, keepdims=True)
    probs_low = (expo / total).astype(jnp.bfloat16)
    logsum = peak + jnp.log(total)
    heads_out = jnp.einsum("hqk,khd->qhd", probs_low, values, preferred_element_type=jnp.float32)
    return (heads_out.reshape(slots, -1).astype(jnp.bfloat16), (query, keys, values, logsum))


def attend_back(out_grad, saved, length, tables):
    query, keys, values, logsum = saved
    slots, heads = query.shape[:2]
    cosine, sine = tables
    out_grad = out_grad.reshape(slots, heads, HEAD_DIM)
    scores = jnp.einsum(
        "qhd,khd->hqk", query, keys, preferred_element_type=jnp.float32
    ) * HEAD_DIM ** (-0.5)
    probs = jnp.where(allowed_mask(slots, length)[None], jnp.exp(scores - logsum), 0.0)
    probs_low = probs.astype(jnp.bfloat16)
    prob_grad = jnp.einsum("qhd,khd->hqk", out_grad, values, preferred_element_type=jnp.float32)
    value_grad = jnp.einsum("hqk,qhd->khd", probs_low, out_grad, preferred_element_type=jnp.float32)
    score_grad = (probs * (prob_grad - jnp.sum(probs * prob_grad, axis=-1, keepdims=True))).astype(
        jnp.bfloat16
    )
    query_grad = jnp.einsum(
        "hqk,khd->qhd", score_grad, keys, preferred_element_type=jnp.float32
    ) * HEAD_DIM ** (-0.5)
    key_grad = jnp.einsum(
        "hqk,qhd->khd", score_grad, query, preferred_element_type=jnp.float32
    ) * HEAD_DIM ** (-0.5)
    query_grad = rotate_back(query_grad, cosine, sine)
    key_grad = rotate_back(key_grad, cosine, sine)
    return jnp.stack([query_grad, key_grad, value_grad], axis=1).astype(jnp.bfloat16)


def dot(left, right):
    return jnp.dot(left, right, preferred_element_type=jnp.float32)


def dot_nt(left, right):
    return lax.dot_general(
        left, right, (((1,), (1,)), ((), ())), preferred_element_type=jnp.float32
    )


def dot_tn(left, right):
    return lax.dot_general(
        left, right, (((0,), (0,)), ((), ())), preferred_element_type=jnp.float32
    )


CHEAP = pl.CostEstimate(flops=1, transcendentals=0, bytes_accessed=1)
SCALE = HEAD_DIM ** (-0.5)


def work(flops):
    return pl.CostEstimate(flops=4 * flops, transcendentals=0, bytes_accessed=flops // 256)


def call(body, grid, in_specs, out_specs, out_shape, info, args, scratch=(), cost=CHEAP):
    return pl.pallas_call(
        body,
        grid_spec=pltpu.PrefetchScalarGridSpec(
            num_scalar_prefetch=1,
            grid=grid,
            in_specs=in_specs,
            out_specs=out_specs,
            scratch_shapes=list(scratch),
        ),
        out_shape=out_shape,
        cost_estimate=cost,
        compiler_params=pltpu.CompilerParams(vmem_limit_bytes=56 << 20),
    )(info, *args)


def low_shape(*shape):
    return jax.ShapeDtypeStruct(shape, jnp.bfloat16)


def full_shape(*shape):
    return jax.ShapeDtypeStruct(shape, jnp.float32)


def fixed(shape):
    return pl.BlockSpec(
        shape, lambda *index: (0,) * len(shape), pipeline_mode=pl.Buffered(buffer_count=1)
    )


def held(width, columns, at):
    return pl.BlockSpec(
        (width, columns), lambda i, info: (0, at), pipeline_mode=pl.Buffered(buffer_count=1)
    )


def held_pieces(width, columns, start, size):
    return [held(width, size, start // size + piece) for piece in range(columns // size)]


def row_stats(rows):
    mean = jnp.mean(rows, axis=1, keepdims=True)
    center = rows - mean
    scale = lax.rsqrt(jnp.mean(center * center, axis=1, keepdims=True) + 1e-05)
    return (mean, scale)


def two_norms(rows, vec_ref, outs):
    rows = rows.astype(jnp.float32)
    mean, scale = row_stats(rows)
    normed = (rows - mean) * scale
    first = normed * vec_ref[0:1] + vec_ref[1:2]
    second = normed * vec_ref[2:3] + vec_ref[3:4]
    outs[0][...] = first.astype(jnp.bfloat16)
    outs[1][...] = second.astype(jnp.bfloat16)
    outs[2][...] = mean
    outs[3][...] = scale
    if len(outs) > 4:
        outs[4][...] = first.T.astype(jnp.bfloat16)
        outs[5][...] = second.T.astype(jnp.bfloat16)


def norms_body(info, z_ref, vec_ref, *outs):
    two_norms(z_ref[...], vec_ref, outs)


def norm_specs(tall, slots, width, row, turn):
    specs = [pl.BlockSpec((tall, width), lambda i, info: (row(i, info), 0))] * 2
    specs += [pl.BlockSpec((tall, 1), lambda i, info: (row(i, info), 0))] * 2
    shapes = [low_shape(slots, width)] * 2 + [full_shape(slots, 1)] * 2
    if turn:
        specs += [pl.BlockSpec((width, tall), lambda i, info: (0, row(i, info)))] * 2
        shapes += [low_shape(width, slots)] * 2
    return (specs, shapes)


def with_turned(out, turn):
    out = list(out)
    return out if turn else out + [out[0].T, out[1].T]


def norms_call(rows, vectors, info):
    slots, width = rows.shape
    tall = min(slots, 256)
    turn = tall % 128 == 0
    specs, shapes = norm_specs(tall, slots, width, lambda i, info: i, turn)
    out = call(
        norms_body,
        (slots // tall,),
        [pl.BlockSpec((tall, width), lambda i, info: (i, 0)), fixed(vectors.shape)],
        specs,
        shapes,
        info,
        (rows, vectors),
    )
    return with_turned(out, turn)


def target_body(info, x_ref, out_ref, *turned_ref):
    tall = x_ref.shape[0]
    place = pl.program_id(0) * tall + lax.broadcasted_iota(jnp.int32, x_ref.shape, 0)
    value = jnp.where(place < info[0], x_ref[...].astype(jnp.float32), 0.0)
    out_ref[...] = value.astype(jnp.bfloat16)
    if turned_ref:
        turned_ref[0][...] = value.T.astype(jnp.bfloat16)


def target_call(cotangent, slots, info):
    width = cotangent.shape[1]
    tall = min(slots, 256)
    steps = slots // tall
    turn = tall % 128 == 0
    out = call(
        target_body,
        (steps,),
        [pl.BlockSpec((tall, width), lambda i, info: (info[1] * steps + i, 0))],
        [pl.BlockSpec((tall, width), lambda i, info: (i, 0))]
        + [pl.BlockSpec((width, tall), lambda i, info: (0, i))] * turn,
        [low_shape(slots, width)] + [low_shape(width, slots)] * turn,
        info,
        (cotangent,),
    )
    return (out[0], out[1]) if turn else (out[0], out[0].T)


def assemble_body(count, normed, info, *refs):
    step = pl.program_id(0)
    rest = refs[count:]
    for which in range(count):

        @pl.when(step == which)
        def _():
            block = refs[which][...]
            if normed:
                rest[1][...] = block
                two_norms(block, rest[0], rest[2:])
            else:
                rest[0][...] = block
                if len(rest) > 1:
                    rest[1][...] = block.astype(jnp.float32).T.astype(jnp.bfloat16)


def assemble(pieces, peers, bits, vectors=None):
    count = len(pieces)
    tall, width = pieces[0].shape
    slots = count * tall
    turn = tall % 128 == 0
    me = lax.axis_index("tensor")
    order = [2 * (me ^ r) + k for k in (0, 1) for r in relative_order(bits, k)]
    info = jnp.stack([jnp.asarray(item, jnp.int32) for item in order])

    def row(s, info):
        return info[s]

    in_specs, args = [fixed(item.shape) for item in pieces], list(pieces)
    specs = [pl.BlockSpec((tall, width), lambda s, info: (info[s], 0))]
    shapes = [low_shape(slots, width)]
    if vectors is not None:
        in_specs.append(fixed(vectors.shape))
        args.append(vectors)
        more, more_shapes = norm_specs(tall, slots, width, row, turn)
        specs, shapes = specs + more, shapes + more_shapes
    elif turn:
        specs.append(pl.BlockSpec((width, tall), lambda s, info: (0, info[s])))
        shapes.append(low_shape(width, slots))
    out = call(
        functools.partial(assemble_body, count, vectors is not None),
        (count,),
        in_specs,
        specs,
        shapes,
        info,
        args,
    )
    if vectors is not None:
        return (out[0], with_turned(out[1:], turn))
    return (out[0], out[1] if turn else out[0].T)


def turned(block, tables, sign):
    cosine, low, high = tables
    front = block[:, :128]
    front = front * cosine + sign * (
        pltpu.roll(front, 128 - ROT // 2, 1) * low + pltpu.roll(front, ROT // 2, 1) * high
    )
    return jnp.concatenate([front, block[:, 128:]], axis=1)


def turn_tables(slots):
    cosine, sine = (item[:, 0] for item in angle_tables(slots))
    rest = 128 - ROT
    zero = jnp.zeros_like(sine)
    pad = jnp.zeros((slots, rest), jnp.float32)
    return (
        jnp.concatenate([cosine, cosine, pad + 1.0], axis=1),
        jnp.concatenate([-sine, zero, pad], axis=1),
        jnp.concatenate([zero, sine, pad], axis=1),
    )


def allowed_block(start, rows, span, length):
    query = start + lax.broadcasted_iota(jnp.int32, (rows, span), 0)
    key = lax.broadcasted_iota(jnp.int32, (rows, span), 1)
    return (key <= query) & (key < length)


def heads_body(
    steps, info, x_ref, wq_ref, wk_ref, wv_ref, cos_ref, low_ref, high_ref, out_ref, qkv_ref, lse_ref, k_ref, v_ref
):
    step = pl.program_id(0)
    rows = x_ref.shape[0]
    tables = (cos_ref[...], low_ref[...], high_ref[...])
    rows_here = x_ref[...]
    query = turned(dot(rows_here, wq_ref[...]), tables, 1.0).astype(jnp.bfloat16)
    keys = turned(dot(rows_here, wk_ref[...]), tables, 1.0).astype(jnp.bfloat16)
    values = dot(rows_here, wv_ref[...]).astype(jnp.bfloat16)
    qkv_ref[:, :HEAD_DIM] = query
    qkv_ref[:, HEAD_DIM : 2 * HEAD_DIM] = keys
    qkv_ref[:, 2 * HEAD_DIM :] = values
    place = pl.multiple_of(step * rows, rows)
    k_ref[pl.ds(place, rows), :] = keys
    v_ref[pl.ds(place, rows), :] = values
    for now in range(steps):

        @pl.when(step == now)
        def _():
            span = (now + 1) * rows
            scores = dot_nt(query, k_ref[:span]) * SCALE
            scores = jnp.where(allowed_block(now * rows, rows, span, info[0]), scores, -jnp.inf)
            peak = jnp.max(scores, axis=1, keepdims=True)
            expo = jnp.exp(scores - peak)
            total = jnp.sum(expo, axis=1, keepdims=True)
            probs = (expo / total).astype(jnp.bfloat16)
            out_ref[...] = dot(probs, v_ref[:span]).astype(jnp.bfloat16)
            lse_ref[...] = peak + jnp.log(total)


def heads_call(first_in, inward, tables, info):
    slots, width = first_in.shape
    rows = min(slots, 256)
    steps = slots // rows
    columns = 3 * HEAD_DIM

    def tall(size):
        return pl.BlockSpec((rows, size), lambda i, info: (i, 0))

    out, qkv, lse = call(
        functools.partial(heads_body, steps),
        (steps,),
        [tall(width)] + [held(width, HEAD_DIM, part) for part in range(3)] + [tall(128)] * 3,
        [tall(HEAD_DIM), tall(columns), tall(1)],
        [low_shape(slots, HEAD_DIM), low_shape(slots, columns), full_shape(slots, 1)],
        info,
        (first_in, inward, inward, inward, *tables),
        [pltpu.VMEM((slots, HEAD_DIM), jnp.bfloat16)] * 2,
    )
    return (out, (qkv, lse))


def heads_back_body(
    steps, info, qkv_ref, lse_ref, grad_ref, cos_ref, low_ref, high_ref, out_ref, dk_ref, dv_ref
):
    step = pl.program_id(0)
    slots = qkv_ref.shape[0]
    rows = slots // steps

    def tables(start, size):
        return tuple(ref[start : start + size] for ref in (cos_ref, low_ref, high_ref))

    @pl.when(step == 0)
    def _():
        dk_ref[...] = jnp.zeros_like(dk_ref)
        dv_ref[...] = jnp.zeros_like(dv_ref)

    for now in range(steps):

        @pl.when(step == now)
        def _():
            span, start = (now + 1) * rows, now * rows
            query = qkv_ref[start:span, :HEAD_DIM]
            keys = qkv_ref[:span, HEAD_DIM : 2 * HEAD_DIM]
            values = qkv_ref[:span, 2 * HEAD_DIM :]
            grad = grad_ref[...]
            scores = dot_nt(query, keys) * SCALE
            allowed = allowed_block(start, rows, span, info[0])
            probs = jnp.where(allowed, jnp.exp(scores - lse_ref[...]), 0.0)
            prob_grad = dot_nt(grad, values)
            spread = jnp.sum(probs * prob_grad, axis=1, keepdims=True)
            score_grad = (probs * (prob_grad - spread)).astype(jnp.bfloat16)
            query_grad = dot(score_grad, keys) * SCALE
            out_ref[start:span, :HEAD_DIM] = turned(
                query_grad, tables(start, rows), -1.0
            ).astype(jnp.bfloat16)
            dv_ref[:span] += dot_tn(probs.astype(jnp.bfloat16), grad)
            dk_ref[:span] += dot_tn(score_grad, query)

    @pl.when(step == steps - 1)
    def _():
        out_ref[:, HEAD_DIM : 2 * HEAD_DIM] = turned(
            dk_ref[...] * SCALE, tables(0, slots), -1.0
        ).astype(jnp.bfloat16)
        out_ref[:, 2 * HEAD_DIM :] = dv_ref[...].astype(jnp.bfloat16)


def heads_back_call(saved, out_grad, tables, info, cost=CHEAP):
    qkv, lse = saved
    slots, columns = qkv.shape
    rows = min(slots, 256)
    steps = slots // rows
    return call(
        functools.partial(heads_back_body, steps),
        (steps,),
        [
            fixed(qkv.shape),
            pl.BlockSpec((rows, 1), lambda i, info: (i, 0)),
            pl.BlockSpec((rows, HEAD_DIM), lambda i, info: (i, 0)),
        ]
        + [fixed((slots, 128))] * 3,
        pl.BlockSpec((slots, columns), lambda i, info: (0, 0)),
        low_shape(slots, columns),
        info,
        (qkv, lse, out_grad, *tables),
        [pltpu.VMEM((slots, HEAD_DIM), jnp.float32)] * 2,
        cost,
    )


def units_body(pieces, info, x_ref, *refs):
    weights, (offset_ref, act_ref, slope_ref) = refs[:pieces], refs[pieces:]
    size = weights[0].shape[1]
    for piece in range(pieces):
        here = slice(piece * size, (piece + 1) * size)
        hidden = dot(x_ref[...], weights[piece][...]) + offset_ref[:, here]
        cdf = 0.5 * (1.0 + lax.erf(hidden * 0.7071067811865476))
        act_ref[:, here] = (hidden * cdf).astype(jnp.bfloat16)
        bell = jnp.exp(-0.5 * hidden * hidden) * 0.3989422804014327
        slope_ref[:, here] = (cdf + hidden * bell).astype(jnp.bfloat16)


def units_call(second_in, expand, start, offsets, unit, info):
    slots, width = second_in.shape
    columns = offsets.shape[0]
    tall = min(slots, 256)
    spec = pl.BlockSpec((tall, columns), lambda i, info: (i, 0))
    weights = held_pieces(width, columns, start * unit, unit)
    return call(
        functools.partial(units_body, len(weights)),
        (slots // tall,),
        [pl.BlockSpec((tall, width), lambda i, info: (i, 0))] + weights + [fixed((1, columns))],
        [spec, spec],
        [low_shape(slots, columns)] * 2,
        info,
        (second_in, *[expand] * len(weights), offsets[None]),
    )


def halving_blocks(half, tall):
    return ([tall] * half + [half * tall]) * 2


def place_rows(info, value_ref, outs, half, tall):
    for which in range(4):
        stream, kept = which // 2, which % 2
        for place in range(half):
            start = (2 * info[which * half + place] + stream) * tall
            rows = value_ref[pl.ds(pl.multiple_of(start, tall), tall)]
            if kept:
                outs[stream * (half + 1) + half][place * tall : (place + 1) * tall] = rows
            else:
                outs[stream * (half + 1) + place][...] = rows


def partial_body(half, tall, parts, info, *refs):
    lefts, rights = [refs[k * parts : (k + 1) * parts] for k in range(4)], refs[4 * parts :][:4]
    outs, value_ref = refs[4 * parts + 4 : -1], refs[-1]
    rows = lefts[0][0].shape[0]
    for part in range(parts):
        value = None
        for left, right in zip(lefts, rights):
            term = dot_nt(left[part][...], right[...])
            value = term if value is None else value + term
        value_ref[part * rows : (part + 1) * rows] = value.astype(jnp.bfloat16)
    if half:
        place_rows(info, value_ref, outs, half, tall)
    else:
        outs[0][...] = value_ref[...]


def partial_call(heads, acts, outward, contract, outward_at, contract_at, places, cost=CHEAP):
    slots, unit = heads[0].shape
    wide = acts[0].shape[1]
    width = outward[0].shape[0]
    block = min(width, 512)
    parts = max(slots // 256, 1)
    rows = slots // parts
    half = len(places) // 4
    tall = slots // (4 * half) if half else 0
    heights = halving_blocks(half, tall) if half else [slots]
    info = jnp.stack([jnp.asarray(item, jnp.int32) for item in (places or [0])])

    def row_blocks(columns):
        return [
            pl.BlockSpec(
                (rows, columns),
                lambda j, info, part=part: (part, 0),
                pipeline_mode=pl.Buffered(buffer_count=1),
            )
            for part in range(parts)
        ]

    return call(
        functools.partial(partial_body, half, tall, parts),
        (width // block,),
        row_blocks(unit) * 2
        + row_blocks(wide) * 2
        + [pl.BlockSpec((block, unit), lambda j, info: (j, outward_at))] * 2
        + [pl.BlockSpec((block, wide), lambda j, info: (j, contract_at * unit // wide))] * 2,
        [pl.BlockSpec((height, block), lambda j, info: (0, j)) for height in heights],
        [low_shape(height, width) for height in heights],
        info,
        [item for item in (*heads, *acts) for part in range(parts)] + [*outward, *contract],
        [pltpu.VMEM((slots, block), jnp.bfloat16)],
        cost,
    )


def grads_body(plan, split, info, *refs):
    lefts = refs[: max(plan) + 1]
    rights = refs[len(lefts) : len(lefts) + len(plan)]
    rest = refs[len(lefts) + len(plan) :]
    got, outs = ((), rest) if split else (rest[:-1], rest[-1:])
    size = rights[0].shape[1]
    for place, right in enumerate(rights):
        value = dot(lefts[plan[place]][...], right[...])
        if split:
            outs[place][...] = value.astype(jnp.bfloat16)
        else:
            value = value + got[place][...].astype(jnp.float32)
            outs[0][:, place * size : (place + 1) * size] = value.astype(jnp.bfloat16)


def grads_call(lefts, rights, size, info, got=None, cost=CHEAP):
    width, slots = lefts[0].shape
    columns = sum(item.shape[1] for item in rights)
    block = min(width, 256)
    split = got is None
    spec = pl.BlockSpec((block, columns), lambda j, info: (j, 0))
    pieces = columns // size
    piece_specs = [pl.BlockSpec((block, size), lambda j, info: (j, 0))] * pieces
    plan, specs, args = [], [], []
    for which, right in enumerate(rights):
        for piece in held_pieces(slots, right.shape[1], 0, size):
            plan.append(which)
            specs.append(piece)
            args.append(right)
    return call(
        functools.partial(grads_body, plan, split),
        (width // block,),
        [pl.BlockSpec((block, slots), lambda j, info: (j, 0))] * len(lefts)
        + specs
        + ([] if split else piece_specs),
        piece_specs if split else spec,
        [low_shape(width, size)] * pieces if split else low_shape(width, columns),
        info,
        (*lefts, *args, *(got or ())),
        cost=cost,
    )


def lifted_body(pieces, info, g_ref, outward_ref, *refs):
    weights, (slope_ref, out_ref, hidden_ref, sum_ref) = refs[:pieces], refs[pieces:]
    size = weights[0].shape[1]

    @pl.when(pl.program_id(0) == 0)
    def _():
        sum_ref[...] = jnp.zeros_like(sum_ref)

    for piece in range(pieces):
        here = slice(piece * size, (piece + 1) * size)
        value = dot(g_ref[...], weights[piece][...]) * slope_ref[:, here].astype(jnp.float32)
        value = value.astype(jnp.bfloat16)
        hidden_ref[:, here] = value
        sum_ref[:, here] += jnp.sum(value.astype(jnp.float32), axis=0, keepdims=True)
    out_ref[...] = dot(g_ref[...], outward_ref[...]).astype(jnp.bfloat16)


def lifted_call(grad, outward, contract, outward_at, contract_at, slope, unit, info, cost=CHEAP):
    slots, width = grad.shape
    columns = slope.shape[1]
    tall = min(slots, 256)
    weights = held_pieces(width, columns, contract_at * unit, unit)

    def rows(size):
        return pl.BlockSpec((tall, size), lambda i, info: (i, 0))

    return call(
        functools.partial(lifted_body, len(weights)),
        (slots // tall,),
        [rows(width), held(width, unit, outward_at)] + weights + [rows(columns)],
        [rows(unit), rows(columns), pl.BlockSpec((1, columns), lambda i, info: (0, 0))],
        [low_shape(slots, unit), low_shape(slots, columns), full_shape(1, columns)],
        info,
        (grad, outward, *[contract] * len(weights), slope),
        cost=cost,
    )


def back_body(half, tall, info, *refs):
    z_ref, mean_ref, scale_ref, vec_ref = refs[:4]
    mixed, hidden, inward, expand = refs[4:6], refs[6:8], refs[8:10], refs[10:12]
    outs, sums_ref, hat_ref, total_ref, along_ref = refs[12:-4], *refs[-4:]
    part, block = pl.program_id(0), pl.program_id(1)
    size = inward[0].shape[0]
    width = z_ref.shape[1]
    columns = pl.ds(pl.multiple_of(block * size, size), size)
    mean, scale = mean_ref[...], scale_ref[...]
    first = dot_nt(mixed[0][...], inward[0][...]) + dot_nt(mixed[1][...], inward[1][...])
    second = dot_nt(hidden[0][...], expand[0][...]) + dot_nt(hidden[1][...], expand[1][...])
    normed = (z_ref[:, columns].astype(jnp.float32) - mean) * scale
    sums = [
        jnp.sum(value, axis=0, keepdims=True)
        for value in (first * normed, first, second * normed, second)
    ]

    @pl.when(part == 0)
    def _():
        for row in range(4):
            sums_ref[row : row + 1, columns] = sums[row]

    @pl.when(part > 0)
    def _():
        for row in range(4):
            sums_ref[row : row + 1, columns] += sums[row]

    hat = first * vec_ref[0:1] + second * vec_ref[2:3]
    hat_ref[:, columns] = hat
    total = jnp.sum(hat, axis=1, keepdims=True)
    along = jnp.sum(hat * normed, axis=1, keepdims=True)

    @pl.when(block == 0)
    def _():
        total_ref[...] = total
        along_ref[...] = along

    @pl.when(block > 0)
    def _():
        total_ref[...] += total
        along_ref[...] += along

    @pl.when(block == pl.num_programs(1) - 1)
    def _():
        rows = hat_ref.shape[0]
        step = tall if half else min(rows, 256)
        for start in range(0, rows, step):
            here = slice(start, start + step)
            normed_here = (z_ref[here].astype(jnp.float32) - mean_ref[here]) * scale_ref[here]
            result = scale_ref[here] * (
                hat_ref[here]
                - total_ref[here] / width
                - normed_here * (along_ref[here] / width)
            )
            result = result.astype(jnp.bfloat16)
            if not half:
                outs[0][pl.ds(part * rows + start, step)] = result
                continue
            stream = start // tall % 2
            peer = part * (rows // (2 * tall)) + start // (2 * tall)
            at = 2 * (2 * peer + stream)
            own_outs = outs[stream * (half + 1) : (stream + 1) * (half + 1)]

            @pl.when(info[at] == 0)
            def _():
                own_outs[half][pl.ds(pl.multiple_of(info[at + 1] * tall, tall), tall)] = result

            for place in range(half):

                @pl.when((info[at] == 1) & (info[at + 1] == place))
                def _():
                    own_outs[place][...] = result


def back_call(rows, stats, vectors, mixed_grads, hidden_grads, inward, expand, expand_at, me, peers, bits):
    slots, width = rows.shape
    parts = 2 if bits else 1
    rows_each = slots // parts
    block = min(width, 512)
    half = peers // 2 if bits else 0
    tall = slots // (2 * peers) if bits else 0
    heads_columns, wide = mixed_grads[0].shape[1], hidden_grads[0].shape[1]
    table = []
    for peer in range(peers if bits else 0):
        for stream in (0, 1):
            bit = step_bits(bits, stream)[0]
            own = (me >> bit) & 1
            place = (peer & ((1 << bit) - 1)) | ((peer >> (bit + 1)) << bit)
            table.append(jnp.asarray(((peer >> bit) & 1) != own, jnp.int32))
            table.append(jnp.asarray(place, jnp.int32))
    info = jnp.stack(table or [jnp.asarray(0, jnp.int32)])
    heights = halving_blocks(half, tall) if half else [slots]

    def spec(columns):
        return pl.BlockSpec((rows_each, columns), lambda i, j, info: (i, 0))

    def weights(columns, at):
        return pl.BlockSpec((block, columns), lambda i, j, info: (j, at))

    def whole(*shape):
        return pl.BlockSpec(shape, lambda i, j, info: (0, 0))

    out = call(
        functools.partial(back_body, half, tall),
        (parts, width // block),
        [spec(width), spec(1), spec(1)]
        + [pl.BlockSpec((vectors.shape[0], block), lambda i, j, info: (0, j))]
        + [spec(item.shape[1]) for item in (*mixed_grads, *hidden_grads)]
        + [weights(heads_columns, 0)] * 2
        + [weights(wide, expand_at * heads_columns // (3 * wide))] * 2,
        [whole(height, width) for height in heights] + [whole(4, width)],
        [low_shape(height, width) for height in heights] + [full_shape(4, width)],
        info,
        (rows, *stats, vectors, *mixed_grads, *hidden_grads, *inward, *expand),
        [pltpu.VMEM((rows_each, width), jnp.float32)]
        + [pltpu.VMEM((rows_each, 1), jnp.float32)] * 2,
    )
    return out[:-1], out[-1]


def share_of(total):
    return lax.psum_scatter(total, "dp", scatter_dimension=0, tiled=True)


def adam_kernel(rate, decay, arrange, info, *refs):
    grads, (master, first, second), outs = refs[:4], refs[4:7], refs[7:]

    def run(half, region, turn):
        grad = jnp.where(info[0] == 0, grads[half][...], grads[2 + half][...]).astype(jnp.float32)
        grad = grad.T if turn else grad
        new = adam_update(master[region], grad, first[region], second[region], rate, decay)
        for out, value in zip(outs, new):
            out[region] = value

    arrange(run)


def adam_columns(index, grads, arrays, depth, starts, core):
    parts, _, columns = arrays[0].shape
    half = columns // 2
    tall = depth // 2

    def arrange(run):
        for which in (0, 1):
            run(which, (0, slice(None), pl.ds(which * half, half)), False)

    def grad_spec(start):
        return pl.BlockSpec((tall, half), lambda i, j, info: (j, start + i))

    block_spec = pl.BlockSpec((1, tall, columns), lambda i, j, info: (i, j, 0))
    return call(
        functools.partial(adam_kernel, RATES[index], DECAYS[index], arrange),
        (parts, depth // tall),
        [grad_spec(starts[which // 2]) for which in range(4)] + [block_spec] * 3,
        [block_spec] * 3,
        [jax.ShapeDtypeStruct(arrays[0].shape, jnp.float32)] * 3,
        core,
        (*grads, *arrays),
    )


def adam_rows(index, grads, arrays, starts, block, core, cost=CHEAP):
    units, depth = arrays[0].shape
    each = units // 2 // block

    def arrange(run):
        for half in (0, 1):

            @pl.when(pl.program_id(0) == half)
            def _():
                run(half, Ellipsis, True)

    def grad_spec(half, start):
        def place(h, j, info):
            return (0, start + jnp.where(h == half, j, (each - 1) * (1 - half)))

        return pl.BlockSpec((depth, block), place)

    block_spec = pl.BlockSpec((block, depth), lambda h, j, info: (h * each + j, 0))
    return call(
        functools.partial(adam_kernel, RATES[index], DECAYS[index], arrange),
        (2, each),
        [grad_spec(which % 2, starts[which // 2]) for which in range(4)] + [block_spec] * 3,
        [block_spec] * 3,
        [jax.ShapeDtypeStruct(arrays[0].shape, jnp.float32)] * 3,
        core,
        (*grads, *arrays),
        cost=cost,
    )


def adam_update(master, grad, first, second, rate, decay):
    new_first = 0.9 * first + 0.1 * grad
    new_second = 0.95 * second + 0.05 * grad * grad
    corrected = new_first / (1.0 - 0.9**STEP)
    spread = jnp.sqrt(new_second / (1.0 - 0.95**STEP))
    return (master - rate * (corrected / (spread + 1e-08) + decay * master), new_first, new_second)


def local(
    tokens,
    cotangent,
    lengths,
    inward,
    outward,
    expand,
    contract,
    vectors,
    offsets,
    inward_first,
    inward_second,
    outward_first,
    outward_second,
    expand_first,
    expand_second,
    contract_first,
    contract_second,
    vectors_first,
    vectors_second,
    offsets_first,
    offsets_second,
):
    core = lax.axis_index("pipe")
    peers = lax.axis_size("tensor")
    groups = lax.axis_size("dp")
    place = lax.axis_index("tensor")
    depth = inward.shape[1]
    heads_local = inward.shape[3] // HEAD_DIM
    lone = heads_local == 2
    head_share = inward.shape[3] // 2
    unit_share = expand.shape[2] // 2
    batches = lengths.shape[0]
    width = tokens.shape[1]
    slots = tokens.shape[0] // batches
    row_share = slots // peers

    bits = halving(peers, slots)

    def packed(shard):
        mine, theirs = (item.astype(jnp.bfloat16).reshape(depth, -1) for item in halves(shard, core))
        got = swap(theirs)
        return (jnp.where(core == 0, mine, got), jnp.where(core == 0, got, mine))

    packs = [packed(item) for item in (inward[0], expand[0], outward[0].T, contract[0].T)]
    count = unit_share // head_share

    small = jnp.concatenate([vectors.reshape(-1), offsets.reshape(-1)]).astype(jnp.bfloat16)
    small = lax.all_gather(small, ("pipe", "dp"), axis=0, tiled=False).reshape(2, groups, -1)
    small = small.astype(jnp.float32)
    vector_values = [
        small[layer, :, : 5 * depth].reshape(groups, 5, depth).transpose(1, 0, 2).reshape(5, width)
        for layer in (0, 1)
    ]
    offset_pairs = [halves(small[layer, :, 5 * depth :].reshape(-1), core) for layer in (0, 1)]

    tables = angle_tables(slots)
    turns = turn_tables(slots)
    length = lax.dynamic_index_in_dim(lengths, core, 0, keepdims=False)
    info = length[None]
    own = lax.dynamic_slice_in_dim(tokens, core * slots, slots, 0)
    target, target_turned = target_call(cotangent, slots, jnp.stack([length, core]))
    places = scatter_places(place, peers, bits) if bits else []

    def whole_of(shard):
        return lax.all_gather(shard, "dp", axis=0, tiled=True)

    def pair_of(whole, *earlier):
        whole = after(whole, *earlier)
        return (whole, swap(whole))

    def block_of(array):
        block = lax.dynamic_slice_in_dim(array, place * row_share, row_share, 0)
        return block.astype(jnp.float32)

    def summed(pieces, beside=()):
        if bits:
            return jnp.concatenate(sum_scatter(pieces, peers, bits, beside), axis=0)
        return lax.psum_scatter(pieces[0], "tensor", scatter_dimension=0, tiled=True).astype(
            jnp.float32
        )

    def spread(block):
        tall = row_share // 2
        return rows_pieces((block[:tall], block[tall:]), peers, bits)

    def heads_of(first_in, inward_pair):
        if lone:
            done = [heads_call(first_in, item, turns, info) for item in inward_pair]
            return ([item[0] for item in done], [item[1] for item in done])
        mixed = [dot(first_in, w[:, : 3 * head_share]).reshape(slots, 3, -1) for w in inward_pair]
        mixed = ordered(mixed[0], mixed[1], core).reshape(slots, 3, -1, HEAD_DIM)
        out, saved = attend(mixed, length, tables)
        return (list(halves(out, core)), saved)

    def heads_back(which, out_grads, saved, cost=CHEAP):
        if lone:
            return heads_back_call(saved[which], out_grads[which], turns, info, cost)
        grad = ordered(out_grads[0], out_grads[1], core)
        mixed_grad = attend_back(grad, saved, length, tables).reshape(slots, 3, -1)
        return halves(mixed_grad, core)[which].reshape(slots, -1)

    def units_of(second_in, expand_pair, start, layer):
        done = [
            units_call(
                second_in, expand_pair[which], start, offset_pairs[layer][which], head_share, info
            )
            for which in (0, 1)
        ]
        return ([item[0] for item in done], [item[1] for item in done])

    def layer_output(layer, outward_pair, contract_pair, heads, acts, cost=CHEAP):
        pieces = partial_call(
            heads,
            acts,
            outward_pair,
            contract_pair,
            outward_at[layer],
            contract_at[layer],
            places,
            cost,
        )
        block = summed(pieces) + block_of(inputs[layer]) + vector_values[layer][4]
        return block.astype(jnp.bfloat16)

    outward_at, contract_at, expand_at = (2 * count, 3), (0, 0), (count, 4)
    shards = [packs[0][0], jnp.concatenate([packs[3][0], packs[1][0], packs[2][0]], axis=1)]
    shards.append(jnp.concatenate([after(packs[0][1], shards[1]), packs[2][1], packs[1][1]], axis=1))
    shards.append(after(packs[3][1], shards[2]))
    shards[1] = after(shards[1], shards[0])
    wholes = [whole_of(item) for item in shards]
    inputs = [own]
    normed = norms_call(own, vector_values[0], info)
    first_in, second_in = normed[:2]
    inward_pairs = [pair_of(wholes[0], first_in, second_in, target_turned)]
    heads, saved = heads_of(first_in, inward_pairs[0])
    rest_pair = pair_of(wholes[1], *heads)
    acts, slopes = units_of(second_in, rest_pair, expand_at[0], 0)
    kept = [(normed, heads, saved, acts, slopes)]
    outward_pairs, contract_pairs, expand_pairs = [rest_pair], [rest_pair], [rest_pair]
    results = [layer_output(0, rest_pair, rest_pair, heads, acts)]
    if bits:
        rows, normed = assemble(
            spread(results[0]), peers, bits, vector_values[1]
        )
        inputs.append(rows)
    else:
        inputs.append(lax.all_gather(results[0], "tensor", axis=0, tiled=True))
        normed = norms_call(inputs[1], vector_values[1], info)
    first_in, second_in = normed[:2]
    rest_pair = pair_of(wholes[2], first_in, second_in)
    for store in (inward_pairs, outward_pairs, expand_pairs):
        store.append(rest_pair)
    acts, slopes = units_of(second_in, rest_pair, expand_at[1], 1)

    grad_low, grad_turned = target, target_turned
    shares, row_grads, vector_grads, offset_grads = [None] * 2, [None] * 2, [None] * 2, [None] * 2
    for layer in (1, 0):
        if layer == 0:
            normed, heads, saved, acts, slopes = kept[0]
        dense = 2 * slots * width * unit_share
        theirs = grads_call([grad_turned], [acts[1]], head_share, info)
        if layer == 1:
            mine = grads_call([grad_turned], [acts[0]], head_share, info)
            heads, saved = heads_of(after(first_in, *theirs, *mine), rest_pair)
            theirs = [after(after(item, *mine, *heads), wholes[3]) for item in theirs]
            contract_pairs.append(pair_of(wholes[3], *theirs))
        got = [swap(item) for item in theirs]

        def lift(which, grad, cost=CHEAP):
            return lifted_call(
                grad,
                outward_pairs[layer][which],
                contract_pairs[layer][which],
                outward_at[layer],
                contract_at[layer],
                slopes[which],
                head_share,
                info,
                cost,
            )

        def total_of(lefts, theirs, mine, cost=CHEAP, between=None):
            got = [swap(item) for item in grads_call(lefts, theirs, head_share, info, cost=cost)]
            if between is not None:
                mine = [after(mine[0], between), *mine[1:]]
            return grads_call(lefts, mine, head_share, info, got, cost)

        if layer == 1:
            lifted = [lift(0, after(grad_low, *theirs), work(dense))]
            mine = [after(item, lifted[0][1]) for item in mine]
            contract_total = jnp.concatenate(
                [
                    (own.astype(jnp.float32) + item.astype(jnp.float32)).astype(jnp.bfloat16)
                    for own, item in zip(mine, got)
                ],
                axis=1,
            )
        else:
            contract_total = grads_call([grad_turned], [acts[0]], head_share, info, got)
            lifted = [lift(0, after(grad_low, contract_total))]
        contract_share = share_of(contract_total)
        lifted.append(lift(1, after(grad_low, contract_total)))
        out_grads = [item[0] for item in lifted]
        hidden_grads = [item[1] for item in lifted]
        offset_grads[layer] = [item[2][0] for item in lifted]
        first_turned, second_turned = normed[4:]
        lefts = [first_turned, grad_turned]
        small_work = work(dense // 2)
        if layer == 1:
            mixed_first = heads_back(0, out_grads, saved, small_work)
            expand_total = total_of(
                [second_turned], [hidden_grads[1]], [hidden_grads[0]], between=mixed_first
            )
            expand_share = share_of(expand_total)
            out_grads = [after(item, expand_total) for item in out_grads]
            mixed_grads = [mixed_first, heads_back(1, out_grads, saved)]
            ahead = mixed_grads
        else:
            mixed_last = heads_back(1, out_grads, saved)
            mixed_first = heads_back(0, out_grads, saved, small_work)
            mixed_grads = [mixed_first, mixed_last]
            hidden_here = [after(item, *shares[1]) for item in hidden_grads]
            other_total = total_of(
                [second_turned, first_turned, grad_turned],
                [hidden_here[1], mixed_last, heads[1]],
                [hidden_here[0], mixed_first, heads[0]],
                between=mixed_first,
            )
            ahead = [other_total]
        pieces, norm_part = back_call(
            after(inputs[layer], *ahead),
            normed[2:4],
            vector_values[layer],
            mixed_grads,
            hidden_grads,
            inward_pairs[layer],
            expand_pairs[layer],
            expand_at[layer],
            place,
            peers,
            bits,
        )
        rights = [[mixed_grads[which], heads[which]] for which in (1, 0)]
        if layer == 1:
            lefts[0] = after(lefts[0], *pieces)
            heads_total = total_of(lefts, *rights, work(dense))
            shares[1] = (share_of(heads_total), expand_share, contract_share)
            pieces = [after(item, contract_share) for item in pieces]
        else:
            shares[0] = share_of(other_total)
            contract_here = after(contract_share, *pieces)
            contract_out = adam_rows(
                3,
                (contract_here, swap(contract_here), swap(shares[1][2]), shares[1][2]),
                [item[0] for item in (contract, contract_first, contract_second)],
                (0, 0),
                head_share,
                core[None],
            )
            pairs = [
                [after(item, *pieces) for item in pair]
                for pair in (outward_pairs[1], contract_pairs[1])
            ]
            results.append(layer_output(1, *pairs, *last))
        upstream = block_of(grad_low)
        vector_grads[layer] = jnp.concatenate(
            [norm_part, jnp.sum(upstream, axis=0)[None]], axis=0
        )
        row_grads[layer] = upstream + summed(pieces, contract_out[:1] if layer == 0 else ())
        if layer == 1:
            block = row_grads[layer].astype(jnp.bfloat16)
            if bits:
                grad_low, grad_turned = assemble(
                    [after(item, expand_share) for item in spread(block)], peers, bits
                )
            else:
                grad_low = lax.all_gather(block, "tensor", axis=0, tiled=True)
                grad_turned = grad_low.T
            last = (heads, acts)

    activations = jnp.where(core == 0, results[0], results[1])
    got = swap(jnp.where(core == 0, results[1], results[0]))
    activations = jnp.where(
        core == 0, jnp.stack([activations, got]), jnp.stack([got, activations])
    )[None]
    gradients = jnp.where(core == 0, row_grads[0], row_grads[1])
    got = swap(jnp.where(core == 0, row_grads[1], row_grads[0]))
    gradients = jnp.where(core == 0, jnp.stack([gradients, got]), jnp.stack([got, gradients]))[None]

    vector_sum = added(jnp.stack(vector_grads), "tensor")
    offset_sum = jnp.stack([ordered(item[0], item[1], core) for item in offset_grads])
    small_sum = jnp.concatenate([vector_sum.reshape(2, -1), offset_sum], axis=1)
    small_sum = added(added(small_sum, "pipe"), "dp")
    small_sum = lax.dynamic_index_in_dim(small_sum, core, 0, keepdims=False)
    where = lax.axis_index("dp")
    vector_grad = lax.dynamic_slice_in_dim(
        small_sum[: 5 * width].reshape(5, width), where * depth, depth, 1
    )
    offset_size = offsets.shape[1]
    offset_grad = lax.dynamic_slice_in_dim(
        small_sum, 5 * width + where * offset_size, offset_size, 0
    )

    def viewed(*arrays):
        return [item[0] for item in arrays]

    def parts_first(*arrays):
        return [item[0].transpose(1, 0, 2) for item in arrays]

    which = core[None]
    expand_1, heads_1 = swap(shares[1][1]), swap(shares[1][0])
    vectors_out = adam_update(
        vectors, vector_grad[None], vectors_first, vectors_second, RATES[4], DECAYS[4]
    )
    offsets_out = adam_update(
        offsets, offset_grad[None], offsets_first, offsets_second, RATES[5], DECAYS[5]
    )
    other_share = after(shares[0], contract_out[0], expand_1, heads_1)
    other_0 = swap(other_share)
    expand_out = adam_columns(
        2,
        (other_share, other_0, expand_1, shares[1][1]),
        [expand, expand_first, expand_second],
        depth,
        (0, 0),
        which,
    )
    inward_out = adam_columns(
        0,
        (other_share, other_0, heads_1, shares[1][0]),
        parts_first(inward, inward_first, inward_second),
        depth,
        (count, 0),
        which,
    )
    outward_out = adam_rows(
        1,
        (other_share, other_0, heads_1, shares[1][0]),
        viewed(outward, outward_first, outward_second),
        (count + 3, 3),
        head_share,
        which,
    )
    outputs = [activations, gradients]
    outputs.extend([item.transpose(1, 0, 2)[None] for item in inward_out])
    outputs.extend([item[None] for item in outward_out])
    outputs.extend(expand_out)
    outputs.extend([item[None] for item in contract_out])
    outputs.extend(vectors_out)
    outputs.extend(offsets_out)
    return tuple(outputs)


def solution(mesh):
    return jax.shard_map(
        local,
        mesh=mesh,
        in_specs=(
            P("dp", None),
            P("dp", None),
            P("dp"),
            P("pipe", "dp", None, "tensor"),
            P("pipe", "tensor", "dp"),
            P("pipe", "dp", "tensor"),
            P("pipe", "tensor", "dp"),
            P("pipe", None, "dp"),
            P("pipe", ("tensor", "dp")),
            P("pipe", "dp", None, "tensor"),
            P("pipe", "dp", None, "tensor"),
            P("pipe", "tensor", "dp"),
            P("pipe", "tensor", "dp"),
            P("pipe", "dp", "tensor"),
            P("pipe", "dp", "tensor"),
            P("pipe", "tensor", "dp"),
            P("pipe", "tensor", "dp"),
            P("pipe", None, "dp"),
            P("pipe", None, "dp"),
            P("pipe", ("tensor", "dp")),
            P("pipe", ("tensor", "dp")),
        ),
        out_specs=(
            P("pipe", "dp", "tensor", None),
            P("pipe", "dp", "tensor", None),
            P("pipe", "dp", None, "tensor"),
            P("pipe", "dp", None, "tensor"),
            P("pipe", "dp", None, "tensor"),
            P("pipe", "tensor", "dp"),
            P("pipe", "tensor", "dp"),
            P("pipe", "tensor", "dp"),
            P("pipe", "dp", "tensor"),
            P("pipe", "dp", "tensor"),
            P("pipe", "dp", "tensor"),
            P("pipe", "tensor", "dp"),
            P("pipe", "tensor", "dp"),
            P("pipe", "tensor", "dp"),
            P("pipe", None, "dp"),
            P("pipe", None, "dp"),
            P("pipe", None, "dp"),
            P("pipe", ("tensor", "dp")),
            P("pipe", ("tensor", "dp")),
            P("pipe", ("tensor", "dp")),
        ),
        check_vma=False,
    )
```
